128 devices in a mesh: dp: 16 (over y, z), mp: 8 (over x, core).
Axes of the slice: x: 4, y: 4, z: 4, core: 2. Of those that a mesh axis runs over, the one named last changes fastest.
Arguments:
- activations: bfloat16 [16384, 4096], P('dp'), may hold values from -6 to 6
- gate_weight: bfloat16 [4096, 8192], P(None, 'mp'), may hold values from -0.09375 to 0.09375
- inner_weight: bfloat16 [4096, 8192], P(None, 'mp'), may hold values from -0.09375 to 0.09375
- state_proj: bfloat16 [4096, 256], replicated, may hold values from -0.09375 to 0.09375
- step_weight: bfloat16 [4096, 128], P(None, 'mp'), may hold values from -0.09375 to 0.09375
- inner_kernel: bfloat16 [4, 8192], P(None, 'mp'), may hold values from -3 to 3
- state_kernel: bfloat16 [4, 256], replicated, may hold values from -3 to 3
- step_bias: float32 [128], P('mp'), may hold values from -1.5 to 0.5
- decay_rate: float32 [128], P('mp'), may hold values from 0.002 to 0.1
- skip_scale: float32 [128], P('mp'), may hold values from 0.5 to 1.5
- norm_gain: bfloat16 [8192], P('mp'), may hold values from 0.099609375 to 1.8984375
- scan_cache: float32 [48, 128, 64, 128], P('dp', 'mp'), may hold values from -6 to 6
- window_cache: bfloat16 [48, 128, 192], P('dp', 'mp'), may hold values from -6 to 6
- state_history: bfloat16 [64, 3, 256], P('dp'), may hold values from -6 to 6
- hit_owner: int32 [64, 128], P('dp', 'mp'), may hold values from 0 to 15, as said below
- hit_slot: int32 [64, 128], P('dp', 'mp'), may hold values from 0 to 2
Outputs:
- normed: bfloat16 [16384, 8192], P('dp', 'mp')
- final_state: float32 [64, 128, 64, 128], P('dp', 'mp')
The draws below stay inside these ranges and needn't reach their ends.
Inputs may be any that keep to these rules, and one draw needn't show every extreme that they name: Among the entries of hit_owner held by one device (its requests, its heads), no owner appears more than 8 times, and some owner appears exactly 8 times.
All inputs are finite; a program needn't handle non-finite values.
Results may differ from the reference program's by a relative error of at most 0.013.
Values sent between devices are 32-bit elements; how exact they have to be, the bound alone decides.
No kernel may reach another device: no remote copies, remote signals or barrier semaphores. Data moves between devices by JAX's collectives and lax.ppermute only.
A program may use at most 128 MiB of HBM per device.

```python
import math
import jax
import jax.numpy as jnp
from jax import lax

D = 4096
HEADS = 128
P_SIZE = 64
N = 128
KC = 4
L = 256
REQ_DEV = 4
SLOTS = 3
REQUESTS = 64
TOKENS = 16384
HEADS_DEV = 16
ENTRIES = 64
CAP = 8
CACHE_SLOTS = 48
N_DP = 16
N_MP = 8


def draw_hit_owner(key, part):
    key = jax.random.fold_in(key, 7)
    device_count = N_DP * N_MP
    key_list = jax.random.split(key, device_count)

    def per_device(device_key):
        key_order, key_rest, key_final = jax.random.split(device_key, 3)
        owner_order = jax.random.permutation(key_order, N_DP).astype(jnp.int32)
        owner_pool = jnp.repeat(owner_order, CAP, total_repeat_length=N_DP * CAP)
        remainder = owner_pool[CAP:][jax.random.permutation(key_rest, N_DP * CAP - CAP)]
        selected = jnp.concatenate([owner_pool[:CAP], remainder])[:ENTRIES]
        return selected[jax.random.permutation(key_final, ENTRIES)]
    owner_table = jax.vmap(per_device)(key_list)
    owner_table = owner_table.reshape(N_DP, N_MP, REQ_DEV, HEADS_DEV).transpose(0, 2, 1, 3).reshape(REQUESTS, HEADS)
    return owner_table.astype(jnp.int32)


def set_ends(array, stream_key, low, high):
    longest = array.shape.index(max(array.shape))
    spots = []
    for shift in (0, 1):
        where = [jax.random.randint(jax.random.fold_in(stream_key, axis), (), 0, length) for axis, length in enumerate(array.shape)]
        where[longest] = (where[longest] + shift) % array.shape[longest]
        spots.append(tuple(where))
    return array.at[spots[0]].set(low).at[spots[1]].set(high)


def shard_levels(key, shape, cuts, smallest, largest):
    factor_of = 1.0
    for axis_at, shards_of in cuts:
        steps = jax.random.uniform(jax.random.fold_in(jax.random.fold_in(key, 6), axis_at), (shards_of,), jnp.float32, smallest / len(cuts), largest / len(cuts))
        factor_of = factor_of * jnp.repeat(jnp.exp(steps), shape[axis_at] // shards_of).reshape((-1,) + (1,) * (len(shape) - 1 - axis_at))
    return factor_of


def scatter_about(own_key, extent, scale, reach, cuts=(), kind=jnp.bfloat16):
    gain = shard_levels(own_key, extent, cuts, -0.22, 0.18) if cuts else 1.0
    values = jax.random.normal(own_key, extent, jnp.float32) * scale * gain
    return jnp.minimum(jnp.maximum(values, -reach), reach).astype(kind)


def setup_inputs(seed: int = 0) -> dict:
    seeds = jax.random.split(jax.random.key(seed), 17)
    return {
        "activations": scatter_about(seeds[0], (TOKENS, D), 1.0, 6.0, ((0, 16),)),
        "gate_weight": scatter_about(seeds[1], (D, HEADS * P_SIZE), D ** -0.5, 0.09375, ((1, 8),)),
        "inner_weight": scatter_about(seeds[2], (D, HEADS * P_SIZE), D ** -0.5, 0.09375, ((1, 8),)),
        "state_proj": scatter_about(seeds[3], (D, 2 * N), D ** -0.5, 0.09375),
        "step_weight": scatter_about(seeds[4], (D, HEADS), D ** -0.5, 0.09375, ((1, 8),)),
        "inner_kernel": scatter_about(seeds[5], (KC, HEADS * P_SIZE), KC ** -0.5, 3.0, ((1, 8),)),
        "state_kernel": scatter_about(seeds[6], (KC, 2 * N), KC ** -0.5, 3.0),
        "step_bias": jnp.clip(-1.5 + 2.0 * jax.random.uniform(seeds[7], (HEADS,), jnp.float32) ** shard_levels(seeds[7], (HEADS,), ((0, 8),), -0.2, 0.2), -1.5, 0.5),
        "decay_rate": jnp.clip(jnp.exp(math.log(0.1) - 3.912023 * jax.random.uniform(seeds[8], (HEADS,), jnp.float32) ** shard_levels(seeds[8], (HEADS,), ((0, 8),), -0.2, 0.2)), 0.002, 0.1),
        "skip_scale": jnp.clip(0.5 + 1.0 * jax.random.uniform(seeds[9], (HEADS,), jnp.float32) ** shard_levels(seeds[9], (HEADS,), ((0, 8),), -0.2, 0.2), 0.5, 1.5),
        "norm_gain": jnp.clip(1.0 + 0.18 * jax.random.normal(seeds[10], (HEADS * P_SIZE,), jnp.float32), 0.099609375, 1.8984375).astype(jnp.bfloat16),
        "scan_cache": scatter_about(seeds[11], (CACHE_SLOTS, HEADS, P_SIZE, N), 1.0, 6.0, ((0, 16), (1, 8)), jnp.float32),
        "window_cache": scatter_about(seeds[12], (CACHE_SLOTS, HEADS, (KC - 1) * P_SIZE), 1.0, 6.0, ((0, 16), (1, 8))),
        "state_history": scatter_about(seeds[13], (REQUESTS, KC - 1, 2 * N), 1.0, 6.0, ((0, 16),)),
        "hit_owner": draw_hit_owner(jax.random.fold_in(seeds[16], 71), 0),
        "hit_slot": set_ends(jax.random.randint(seeds[15], (REQUESTS, HEADS), 0, SLOTS), jax.random.fold_in(seeds[15], 1), 0, SLOTS - 1).astype(jnp.int32),
    }


EPSILON = 1e-05
HIGHEST = lax.Precision.HIGHEST

def causal_conv(history, current, kernel):
    joined = jnp.concatenate([history, current], axis=1)
    kernel_width = kernel.shape[0]
    seq_length = current.shape[1]
    running = jnp.zeros(current.shape, jnp.float32)
    for tap_index in range(kernel_width):
        running = running + kernel[tap_index].astype(jnp.float32) * joined[:, tap_index:tap_index + seq_length].astype(jnp.float32)
    return jax.nn.silu(running).astype(jnp.bfloat16)

def reference(activations, gate_weight, inner_weight, state_proj, step_weight, inner_kernel, state_kernel, step_bias, decay_rate, skip_scale, norm_gain, scan_cache, window_cache, state_history, hit_owner, hit_slot):
    gate_all = jnp.dot(activations, gate_weight, preferred_element_type=jnp.float32).astype(jnp.bfloat16)
    inner_all = jnp.dot(activations, inner_weight, preferred_element_type=jnp.float32).astype(jnp.bfloat16)
    mixed_all = jnp.dot(activations, state_proj, preferred_element_type=jnp.float32).astype(jnp.bfloat16)
    step_all = jnp.dot(activations, step_weight, preferred_element_type=jnp.float32)
    blocks = (hit_owner * SLOTS + hit_slot).astype(jnp.int32)
    head_index = jnp.arange(HEADS, dtype=jnp.int32)

    def per_request(inputs):
        gate_rows, inner_rows, mixed_rows, step_rows, history, block_ids = inputs
        start_state = scan_cache[block_ids, head_index]
        window = window_cache[block_ids, head_index].reshape(HEADS, KC - 1, P_SIZE).transpose(1, 0, 2).reshape(KC - 1, HEADS * P_SIZE)
        inner_conv = causal_conv(window[None], inner_rows[None], inner_kernel)[0]
        state_conv = causal_conv(history[None], mixed_rows[None], state_kernel)[0]
        b_part = state_conv[:, :N].astype(jnp.float32)
        c_part = state_conv[:, N:].astype(jnp.float32)
        step_size = jax.nn.softplus(step_rows + step_bias)
        cumulative = jnp.cumsum(-decay_rate * step_size, axis=0)
        cum_heads = cumulative.T
        scores = jnp.dot(state_conv[:, N:], state_conv[:, :N].T, preferred_element_type=jnp.float32)
        causal = jnp.tril(jnp.ones((L, L), dtype=bool))
        log_gap = cum_heads[:, :, None] - cum_heads[:, None, :]
        decay_factor = jnp.where(causal[None], jnp.exp(jnp.where(causal[None], log_gap, 0.0)), 0.0)
        weights = (decay_factor * scores[None] * step_size.T[:, None, :]).astype(jnp.bfloat16)
        inner_heads = inner_conv.reshape(L, HEADS, P_SIZE).astype(jnp.float32)
        intra_block = jnp.einsum('hts,shp->thp', weights.astype(jnp.float32), inner_heads, precision=HIGHEST)
        carried = jnp.exp(cumulative)[:, :, None] * jnp.einsum('hpn,tn->thp', start_state, c_part, precision=HIGHEST)
        output_heads = intra_block + carried + skip_scale[None, :, None] * inner_heads
        tail_weight = jnp.exp(cumulative[-1][None, :] - cumulative) * step_size
        final_state = jnp.exp(cumulative[-1])[:, None, None] * start_state + jnp.einsum('shp,sn->hpn', inner_heads * tail_weight[:, :, None], b_part, precision=HIGHEST)
        gated_rows = output_heads.reshape(L, HEADS * P_SIZE) * jax.nn.silu(gate_rows.astype(jnp.float32))
        mean_square = lax.optimization_barrier(jnp.mean(gated_rows * gated_rows, axis=1))
        normed = (gated_rows * lax.rsqrt(mean_square + EPSILON)[:, None] * norm_gain.astype(jnp.float32)).astype(jnp.bfloat16)
        return (normed, final_state)
    outputs, finals = lax.map(per_request, (gate_all.reshape(REQUESTS, L, HEADS * P_SIZE), inner_all.reshape(REQUESTS, L, HEADS * P_SIZE), mixed_all.reshape(REQUESTS, L, 2 * N), step_all.reshape(REQUESTS, L, HEADS), state_history, blocks))
    return (outputs.reshape(TOKENS, HEADS * P_SIZE), finals)
```

```python
import functools

import jax
import jax.numpy as jnp
from jax import lax
from jax.experimental import pallas as pl
from jax.experimental.pallas import tpu as pltpu
from jax.sharding import PartitionSpec as P

EPSILON = 1e-05
CAP = 8
F32 = jnp.float32
BF16 = jnp.bfloat16
MIB = 1024 * 1024


def silu(v):
    half = 0.5 * v
    return half + half * jnp.tanh(half)


def full(shape, **kw):
    return pl.BlockSpec(shape, lambda *_: (0,) * len(shape), **kw)


def prep_kernel(owner_ref, slot_ref, wanted_ref, pos_ref, count_ref):
    owners = wanted_ref.shape[0]
    requests, heads = owner_ref.shape
    for o in range(owners):
        count_ref[o] = 0
        for k in range(CAP):
            wanted_ref[o, 0, k] = 0
    for r in range(requests):
        for h in range(heads):
            o = owner_ref[r, h]
            k = count_ref[o]
            count_ref[o] = k + 1
            wanted_ref[o, 0, k] = slot_ref[r, h] * heads + h
            pos_ref[r * heads + h] = o * CAP + k


def prep(hit_owner, hit_slot, owners):
    entries = hit_owner.size
    smem = pl.BlockSpec(memory_space=pltpu.SMEM)
    return pl.pallas_call(
        prep_kernel,
        out_shape=(
            jax.ShapeDtypeStruct((owners, 1, 128), jnp.int32),
            jax.ShapeDtypeStruct((entries,), jnp.int32),
        ),
        in_specs=[smem, smem],
        out_specs=(smem, smem),
        scratch_shapes=[pltpu.SMEM((owners,), jnp.int32)],
        name="prep",
    )(hit_owner, hit_slot)


def pick_kernel(codes_ref, cache_ref, out_ref):
    d = pl.program_id(0)
    for k in range(CAP):
        out_ref[0, k] = cache_ref[codes_ref[d, 0, k]]


def pick(codes, cache):
    owners = codes.shape[0]
    blocks, p, n = cache.shape
    return pl.pallas_call(
        pick_kernel,
        out_shape=jax.ShapeDtypeStruct((owners, CAP, p, n), F32),
        grid_spec=pltpu.PrefetchScalarGridSpec(
            num_scalar_prefetch=1,
            grid=(owners,),
            in_specs=[full((blocks, p, n), pipeline_mode=pl.Buffered(1))],
            out_specs=pl.BlockSpec((1, CAP, p, n), lambda d, c: (d, 0, 0, 0)),
        ),
        compiler_params=pltpu.CompilerParams(vmem_limit_bytes=8 * MIB),
        cost_estimate=pl.CostEstimate(flops=0, bytes_accessed=6 * MIB, transcendentals=0),
        name="pick",
    )(codes, cache)


TILE = 256


def project_kernel(steps, act_ref, wi_ref, wg_ref, ws_ref, wd_ref, inner_ref, gate_ref, state_ref, step_ref):
    j = pl.program_id(0)
    rows = act_ref.shape[0]
    chunk = 256

    def run(w_ref, out_ref):
        @pl.loop(0, rows // chunk)
        def _(m):
            at = pl.ds(pl.multiple_of(m * chunk, chunk), chunk)
            out_ref[at, :] = jnp.dot(act_ref[at, :], w_ref[...], preferred_element_type=F32).astype(out_ref.dtype)

    @pl.when(j == 0)
    def _():
        run(ws_ref, state_ref)
        run(wd_ref, step_ref)

    @pl.when((j > 0) & (j <= steps))
    def _():
        run(wi_ref, inner_ref)

    @pl.when(j > steps)
    def _():
        run(wg_ref, gate_ref)


def project(act, wi, wg, ws, wd):
    rows, depth = act.shape
    width = wi.shape[1]
    steps = width // TILE

    def at_inner(j):
        return (0, jnp.clip(j - 1, 0, steps - 1))

    def at_gate(j):
        return (0, jnp.clip(j - 1 - steps, 0, steps - 1))

    flops = 2 * rows * depth * (2 * width + ws.shape[1] + wd.shape[1])
    return pl.pallas_call(
        functools.partial(project_kernel, steps),
        out_shape=(
            jax.ShapeDtypeStruct((rows, width), BF16),
            jax.ShapeDtypeStruct((rows, width), BF16),
            jax.ShapeDtypeStruct((rows, ws.shape[1]), BF16),
            jax.ShapeDtypeStruct((rows, wd.shape[1]), F32),
        ),
        grid=(1 + 2 * steps,),
        in_specs=[
            full((rows, depth), pipeline_mode=pl.Buffered(1)),
            pl.BlockSpec((depth, TILE), at_inner),
            pl.BlockSpec((depth, TILE), at_gate),
            full(ws.shape, pipeline_mode=pl.Buffered(1)),
            full(wd.shape, pipeline_mode=pl.Buffered(1)),
        ],
        out_specs=(
            pl.BlockSpec((rows, TILE), at_inner),
            pl.BlockSpec((rows, TILE), at_gate),
            full((rows, ws.shape[1])),
            full((rows, wd.shape[1])),
        ),
        compiler_params=pltpu.CompilerParams(vmem_limit_bytes=36 * MIB),
        cost_estimate=pl.CostEstimate(flops=flops, bytes_accessed=32 * MIB, transcendentals=0),
        name="project",
    )(act, wi, wg, ws, wd)


def ssd_kernel(
    inner_ref,
    gate_ref,
    state_ref,
    step_ref,
    win_ref,
    hist_ref,
    ik_ref,
    sk_ref,
    bias_ref,
    decay_ref,
    skip_ref,
    az_ref,
    ez_ref,
    c_ref,
    f1_ref,
    el_ref,
    u_ref,
    v_ref,
):
    seq, width = inner_ref.shape
    heads = step_ref.shape[1]
    p = width // heads
    taps = ik_ref.shape[0]
    n = state_ref.shape[1] // 2
    lead = 8 - (taps - 1)
    half = seq // 2

    v_ref[lead:8, :] = hist_ref[0].astype(F32)
    v_ref[8:, :] = state_ref[...].astype(F32)
    sk = sk_ref[...].astype(F32)
    run = jnp.zeros((seq, 2 * n), F32)
    for k in range(taps):
        run = run + sk[k : k + 1] * v_ref[lead + k : lead + k + seq, :]
    conv = silu(run).astype(BF16)
    b = conv[:, :n]
    c = conv[:, n:]
    c_ref[...] = c

    raw = step_ref[...] + bias_ref[...]
    dt = jnp.maximum(raw, 0.0) + jnp.log1p(jnp.exp(-jnp.abs(raw)))
    dt = jnp.concatenate([dt, jnp.zeros((seq, 128 - heads), F32)], axis=1)
    decay = jnp.concatenate([decay_ref[...], jnp.zeros((1, 128 - heads), F32)], axis=1)
    t_at = lax.broadcasted_iota(jnp.int32, (seq, seq), 0)
    s_at = lax.broadcasted_iota(jnp.int32, (seq, seq), 1)
    causal = s_at <= t_at
    cum = jnp.dot(
        causal.astype(F32), -decay * dt, preferred_element_type=F32, precision=lax.Precision.HIGHEST
    )
    cum_t = cum.T
    dt_t = dt.T
    last = cum[seq - 1 : seq]
    spread = (
        lax.broadcasted_iota(jnp.int32, (128, width), 1) // p
        == lax.broadcasted_iota(jnp.int32, (128, width), 0)
    )
    spread = spread.astype(F32).astype(BF16)
    grown = jnp.exp(cum)
    tail = jnp.exp(last - cum) * dt
    el_ref[0] = jnp.broadcast_to(jnp.exp(cum_t[:heads, seq - 1 : seq]), (heads, n))

    scores = lax.dot_general(c, b, (((1,), (1,)), ((), ())), preferred_element_type=F32)
    scores = jnp.where(causal, scores, 0.0)
    top = scores[:half, :half]
    bottom = scores[half:]

    u_ref[lead:8, :] = win_ref[0]
    u_ref[8:, :] = inner_ref[...].astype(F32)
    lane = lax.broadcasted_iota(jnp.int32, (1, 128), 1)
    for q in range(width // 128):
        cols = slice(q * 128, q * 128 + 128)
        ik = ik_ref[:, cols].astype(F32)
        run = jnp.zeros((seq, 128), F32)
        for k in range(taps):
            run = run + ik[k : k + 1] * u_ref[lead + k : lead + k + seq, cols]
        x = silu(run).astype(BF16)
        xf = x.astype(F32)
        y_top = jnp.zeros((half, 128), F32)
        y_bottom = jnp.zeros((seq - half, 128), F32)
        for s in range(128 // p):
            h = q * (128 // p) + s
            own = (lane >= s * p) & (lane < (s + 1) * p)
            xs = jnp.where(own, xf, 0.0).astype(BF16)
            col = cum[:, h : h + 1]
            row = cum_t[h : h + 1]
            dr = dt_t[h : h + 1]
            w_top = jnp.exp(jnp.minimum(col[:half] - row[:, :half], 0.0)) * (top * dr[:, :half])
            w_bottom = jnp.exp(jnp.minimum(col[half:] - row, 0.0)) * (bottom * dr)
            y_top = y_top + jnp.dot(w_top.astype(BF16), xs[:half], preferred_element_type=F32)
            y_bottom = y_bottom + jnp.dot(w_bottom.astype(BF16), xs, preferred_element_type=F32)
        y = jnp.concatenate([y_top, y_bottom], axis=0) + skip_ref[:, cols] * xf
        z = silu(gate_ref[:, cols].astype(F32))
        az_ref[:, cols] = (y * z).astype(BF16)
        ez = jnp.dot(grown.astype(BF16), spread[:, cols], preferred_element_type=F32) * z
        ez_ref[:, cols] = ez.astype(BF16)
        tw = jnp.dot(tail.astype(BF16), spread[:, cols], preferred_element_type=F32)
        xt = (xf * tw).astype(BF16)
        f1_ref[0, cols, :] = lax.dot_general(
            xt, b, (((0,), (0,)), ((), ())), preferred_element_type=F32
        )


def ssd(inner, gate, state, step, window, history, ik, sk, bias, decay, skip):
    tokens, width = inner.shape
    requests = history.shape[0]
    seq = tokens // requests
    heads = step.shape[1]
    n2 = state.shape[1]
    n = n2 // 2
    rows = lambda w: pl.BlockSpec((seq, w), lambda r: (r, 0))
    per = lambda *s: pl.BlockSpec((1,) + s, lambda r: (r,) + (0,) * len(s))
    return pl.pallas_call(
        ssd_kernel,
        out_shape=(
            jax.ShapeDtypeStruct((tokens, width), BF16),
            jax.ShapeDtypeStruct((tokens, width), BF16),
            jax.ShapeDtypeStruct((tokens, n), BF16),
            jax.ShapeDtypeStruct((requests, width, n), F32),
            jax.ShapeDtypeStruct((requests, heads, n), F32),
        ),
        grid=(requests,),
        in_specs=[
            rows(width),
            rows(width),
            rows(n2),
            rows(heads),
            per(*window.shape[1:]),
            per(*history.shape[1:]),
            full(ik.shape),
            full(sk.shape),
            full(bias.shape),
            full(decay.shape),
            full(skip.shape),
        ],
        out_specs=(rows(width), rows(width), rows(n), per(width, n), per(heads, n)),
        scratch_shapes=[pltpu.VMEM((seq + 8, width), F32), pltpu.VMEM((seq + 8, n2), F32)],
        compiler_params=pltpu.CompilerParams(vmem_limit_bytes=32 * MIB),
        cost_estimate=pl.CostEstimate(
            flops=2 * tokens * width * seq * 2, bytes_accessed=14 * MIB, transcendentals=tokens * seq * heads
        ),
        name="ssd",
    )(inner, gate, state, step, window, history, ik, sk, bias, decay, skip)


def tail_kernel(pos_ref, back_ref, az_ref, ez_ref, c_ref, f1_ref, el_ref, g_ref, sq_ref, final_ref, s_ref):
    r = pl.program_id(0)
    heads, n = el_ref.shape[1:]
    p = back_ref.shape[1]
    seq, width = az_ref.shape
    for h in range(heads):
        block = back_ref[pos_ref[r * heads + h]]
        at = slice(h * p, h * p + p)
        final_ref[0, h] = el_ref[0, h : h + 1] * block + f1_ref[0, at]
        s_ref[at] = block.astype(BF16)
    c = c_ref[...]
    total = jnp.zeros((seq, 128), F32)
    for q in range(width // 256):
        cols = slice(q * 256, q * 256 + 256)
        seen = lax.dot_general(c, s_ref[cols], (((1,), (1,)), ((), ())), preferred_element_type=F32)
        g = az_ref[:, cols].astype(F32) + ez_ref[:, cols].astype(F32) * seen
        g_ref[:, cols] = g.astype(BF16)
        g2 = g * g
        total = total + g2[:, :128] + g2[:, 128:]

    @pl.when(r == 0)
    def _():
        sq_ref[...] = jnp.zeros_like(sq_ref)

    sq_ref[pl.ds(r, 1), :] = jnp.sum(total.T, axis=0, keepdims=True)


def tail(pos, back, az, ez, c, f1, el):
    requests, heads, n = el.shape
    tokens, width = az.shape
    p = back.shape[1]
    seq = tokens // requests
    rows = lambda w: pl.BlockSpec((seq, w), lambda r, _: (r, 0))
    per = lambda *s: pl.BlockSpec((1,) + s, lambda r, _: (r,) + (0,) * len(s))
    return pl.pallas_call(
        tail_kernel,
        out_shape=(
            jax.ShapeDtypeStruct((tokens, width), BF16),
            jax.ShapeDtypeStruct((8, seq), F32),
            jax.ShapeDtypeStruct((requests, heads, p, n), F32),
        ),
        grid_spec=pltpu.PrefetchScalarGridSpec(
            num_scalar_prefetch=1,
            grid=(requests,),
            in_specs=[
                full(back.shape, pipeline_mode=pl.Buffered(1)),
                rows(width),
                rows(width),
                rows(n),
                per(width, n),
                per(heads, n),
            ],
            out_specs=(rows(width), full((8, seq)), per(heads, p, n)),
            scratch_shapes=[pltpu.VMEM((width, n), BF16)],
        ),
        compiler_params=pltpu.CompilerParams(vmem_limit_bytes=24 * MIB),
        cost_estimate=pl.CostEstimate(
            flops=2 * tokens * width * n, bytes_accessed=14 * MIB, transcendentals=0
        ),
        name="tail",
    )(pos, back, az, ez, c, f1, el)


def norm_kernel(channels, g_ref, s0_ref, s1_ref, s2_ref, s3_ref, gain_ref, out_ref):
    r = pl.program_id(0)
    at = pl.ds(r, 1)
    seq, width = g_ref.shape
    square = s0_ref[at] + s1_ref[at] + s2_ref[at] + s3_ref[at]
    scale = lax.rsqrt(square / channels + EPSILON)
    scale = jnp.broadcast_to(scale, (128, seq)).T
    gain = gain_ref[...].astype(F32)
    for q in range(width // 128):
        cols = slice(q * 128, q * 128 + 128)
        out_ref[:, cols] = (g_ref[:, cols].astype(F32) * scale * gain[:, cols]).astype(BF16)


def normalise(g, parts, gain, channels):
    tokens, width = g.shape
    seq = parts[0].shape[1]
    rows = pl.BlockSpec((seq, width), lambda r: (r, 0))
    return pl.pallas_call(
        functools.partial(norm_kernel, channels),
        out_shape=jax.ShapeDtypeStruct((tokens, width), BF16),
        grid=(tokens // seq,),
        in_specs=[rows] + [full(parts[0].shape)] * 4 + [full(gain.shape)],
        out_specs=rows,
        compiler_params=pltpu.CompilerParams(vmem_limit_bytes=8 * MIB),
        cost_estimate=pl.CostEstimate(flops=2 * tokens * width, bytes_accessed=4 * MIB, transcendentals=0),
        name="normalise",
    )(g, *parts, gain)


def local(
    activations,
    gate_weight,
    inner_weight,
    state_proj,
    step_weight,
    inner_kernel,
    state_kernel,
    step_bias,
    decay_rate,
    skip_scale,
    norm_gain,
    scan_cache,
    window_cache,
    state_history,
    hit_owner,
    hit_slot,
):
    owners = lax.axis_size("dp")
    groups = lax.axis_size("mp")
    requests, heads = hit_owner.shape
    slots, _, p, n = scan_cache.shape
    width = inner_weight.shape[1]
    lead = inner_kernel.shape[0] - 1

    wanted, pos = prep(hit_owner, hit_slot, owners)
    codes = lax.all_to_all(wanted, "dp", split_axis=0, concat_axis=0, tiled=True)
    windows = lax.all_gather(window_cache.astype(F32), "dp", tiled=True)
    sent = pick(codes, scan_cache.reshape(slots * heads, p, n))
    back = lax.all_to_all(sent, "dp", split_axis=0, concat_axis=0, tiled=True)

    window = windows[hit_owner * slots + hit_slot, jnp.arange(heads)[None]]
    window = window.reshape(requests, heads, lead, p).transpose(0, 2, 1, 3).reshape(requests, lead, width)
    inner, gate, state, step = project(activations, inner_weight, gate_weight, state_proj, step_weight)
    az, ez, c, f1, el = ssd(
        inner,
        gate,
        state,
        step,
        window,
        state_history,
        inner_kernel,
        state_kernel,
        step_bias[None],
        decay_rate[None],
        jnp.repeat(skip_scale, p)[None],
    )
    g, square, final = tail(pos, back.reshape(owners * CAP, p, n), az, ez, c, f1, el)
    pair = [(i, i ^ 1) for i in range(groups)]
    square = square + lax.ppermute(square, "mp", pair)
    parts = [square] + [
        lax.ppermute(square, "mp", [(i, (i + 2 * s) % groups) for i in range(groups)])
        for s in range(1, groups // 2)
    ]
    normed = normalise(g, parts, norm_gain[None], width * groups)
    return normed, final


def solution(mesh):
    placed = (
        P("dp", None),
        P(None, "mp"),
        P(None, "mp"),
        P(),
        P(None, "mp"),
        P(None, "mp"),
        P(),
        P("mp"),
        P("mp"),
        P("mp"),
        P("mp"),
        P("dp", "mp", None, None),
        P("dp", "mp", None),
        P("dp", None, None),
        P("dp", "mp"),
        P("dp", "mp"),
    )
    return jax.shard_map(
        local,
        mesh=mesh,
        in_specs=placed,
        out_specs=(P("dp", "mp"), P("dp", "mp", None, None)),
        check_vma=False,
    )
```

```python
import functools

import jax
import jax.numpy as jnp
from jax import lax
from jax.experimental import pallas as pl
from jax.experimental.pallas import tpu as pltpu
from jax.sharding import PartitionSpec as P

EPSILON = 1e-05
CAP = 8
F32 = jnp.float32
BF16 = jnp.bfloat16
MIB = 1024 * 1024


def silu(v):
    half = 0.5 * v
    return half + half * jnp.tanh(half)


def full(shape, **kw):
    return pl.BlockSpec(shape, lambda *_: (0,) * len(shape), **kw)


def prep_kernel(owner_ref, slot_ref, wanted_ref, pos_ref, count_ref):
    owners = wanted_ref.shape[0]
    requests, heads = owner_ref.shape
    for o in range(owners):
        count_ref[o] = 0
        for k in range(CAP):
            wanted_ref[o, 0, k] = 0
    for r in range(requests):
        for h in range(heads):
            o = owner_ref[r, h]
            k = count_ref[o]
            count_ref[o] = k + 1
            wanted_ref[o, 0, k] = slot_ref[r, h] * heads + h
            pos_ref[r * heads + h] = o * CAP + k


def prep(hit_owner, hit_slot, owners):
    entries = hit_owner.size
    smem = pl.BlockSpec(memory_space=pltpu.SMEM)
    return pl.pallas_call(
        prep_kernel,
        out_shape=(
            jax.ShapeDtypeStruct((owners, 1, 128), jnp.int32),
            jax.ShapeDtypeStruct((entries,), jnp.int32),
        ),
        in_specs=[smem, smem],
        out_specs=(smem, smem),
        scratch_shapes=[pltpu.SMEM((owners,), jnp.int32)],
        name="prep",
    )(hit_owner, hit_slot)


def pick_kernel(codes_ref, cache_ref, window_ref, out_ref, wa_ref, wb_ref, rows_ref, sem):
    owners = out_ref.shape[0]
    p = cache_ref.shape[1]
    half = window_ref.shape[1] // 3
    cached = CAP * p

    @pl.loop(0, owners)
    def _(d):
        for k in range(CAP):
            pltpu.make_async_copy(
                cache_ref.at[codes_ref[d, 0, k]], out_ref.at[d, k * p : k * p + p], sem
            ).start()

    w = window_ref[...].astype(F32)
    first = w[:, : 2 * half]
    second = jnp.concatenate([w[:, 2 * half :], jnp.zeros((w.shape[0], half), F32)], axis=1)
    odd = lax.broadcasted_iota(jnp.int32, first.shape, 0) % 2 == 1
    wa_ref[...] = jnp.where(odd, pltpu.roll(first, half, 1), first)
    wb_ref[...] = jnp.where(odd, pltpu.roll(second, half, 1), second)

    @pl.loop(0, owners)
    def _(d):
        for k in range(CAP):
            at = pl.ds(codes_ref[d, 0, k], 1)
            rows_ref[d, 2 * k : 2 * k + 1] = wa_ref[at]
            rows_ref[d, 2 * k + 1 : 2 * k + 2] = wb_ref[at]

    pltpu.make_async_copy(rows_ref, out_ref.at[:, cached:], sem).start()
    pltpu.make_async_copy(out_ref, out_ref, sem).wait()


def pick(codes, cache, window):
    owners = codes.shape[0]
    blocks, p, n = cache.shape
    return pl.pallas_call(
        pick_kernel,
        out_shape=jax.ShapeDtypeStruct((owners, CAP * p + 2 * CAP, n), F32),
        in_specs=[
            pl.BlockSpec(memory_space=pltpu.SMEM),
            pl.BlockSpec(memory_space=pl.ANY),
            pl.BlockSpec(memory_space=pltpu.VMEM),
        ],
        out_specs=pl.BlockSpec(memory_space=pl.ANY),
        scratch_shapes=[
            pltpu.VMEM((blocks, n), F32),
            pltpu.VMEM((blocks, n), F32),
            pltpu.VMEM((owners, 2 * CAP, n), F32),
            pltpu.SemaphoreType.DMA,
        ],
        compiler_params=pltpu.CompilerParams(vmem_limit_bytes=60 * MIB),
        cost_estimate=pl.CostEstimate(flops=0, bytes_accessed=8 * MIB, transcendentals=0),
        name="pick",
    )(codes, cache, window)


TILE = 256


def project_kernel(steps, act_ref, wi_ref, wg_ref, ws_ref, wd_ref, inner_ref, gate_ref, state_ref, step_ref):
    j = pl.program_id(0)
    rows = act_ref.shape[0]
    chunk = 1024

    def run(w_ref, out_ref):
        @pl.loop(0, rows // chunk)
        def _(m):
            at = pl.ds(pl.multiple_of(m * chunk, chunk), chunk)
            out_ref[at, :] = jnp.dot(act_ref[at, :], w_ref[...], preferred_element_type=F32).astype(out_ref.dtype)

    @pl.when(j == 0)
    def _():
        run(ws_ref, state_ref)
        run(wd_ref, step_ref)

    @pl.when((j > 0) & (j <= steps))
    def _():
        run(wi_ref, inner_ref)

    @pl.when(j > steps)
    def _():
        run(wg_ref, gate_ref)


def project(act, wi, wg, ws, wd):
    rows, depth = act.shape
    width = wi.shape[1]
    steps = width // TILE

    def at_inner(j):
        return (0, jnp.clip(j - 1, 0, steps - 1))

    def at_gate(j):
        return (0, jnp.clip(j - 1 - steps, 0, steps - 1))

    flops = 2 * rows * depth * (2 * width + ws.shape[1] + wd.shape[1])
    return pl.pallas_call(
        functools.partial(project_kernel, steps),
        out_shape=(
            jax.ShapeDtypeStruct((rows, width), BF16),
            jax.ShapeDtypeStruct((rows, width), BF16),
            jax.ShapeDtypeStruct((rows, ws.shape[1]), BF16),
            jax.ShapeDtypeStruct((rows, wd.shape[1]), F32),
        ),
        grid=(1 + 2 * steps,),
        in_specs=[
            full((rows, depth), pipeline_mode=pl.Buffered(1)),
            pl.BlockSpec((depth, TILE), at_inner),
            pl.BlockSpec((depth, TILE), at_gate),
            full(ws.shape, pipeline_mode=pl.Buffered(1)),
            full(wd.shape, pipeline_mode=pl.Buffered(1)),
        ],
        out_specs=(
            pl.BlockSpec((rows, TILE), at_inner),
            pl.BlockSpec((rows, TILE), at_gate),
            full((rows, ws.shape[1])),
            full((rows, wd.shape[1])),
        ),
        compiler_params=pltpu.CompilerParams(vmem_limit_bytes=36 * MIB),
        cost_estimate=pl.CostEstimate(flops=flops, bytes_accessed=32 * MIB, transcendentals=0),
        name="project",
    )(act, wi, wg, ws, wd)


def ssd_kernel(
    inner_ref,
    gate_ref,
    state_ref,
    step_ref,
    hist_ref,
    ik_ref,
    sk_ref,
    bias_ref,
    decay_ref,
    skip_ref,
    az_ref,
    ez_ref,
    c_ref,
    b_ref,
    f1_ref,
    el_ref,
    first_ref,
    u_ref,
    v_ref,
):
    seq, width = inner_ref.shape
    heads = step_ref.shape[1]
    p = width // heads
    taps = ik_ref.shape[0]
    lag = taps - 1
    n = state_ref.shape[1] // 2
    lead = 8 - lag
    half = seq // 2

    v_ref[lead:8, :] = hist_ref[0].astype(F32)
    v_ref[8:, :] = state_ref[...].astype(F32)
    sk = sk_ref[...].astype(F32)
    run = jnp.zeros((seq, 2 * n), F32)
    for k in range(taps):
        run = run + sk[k : k + 1] * v_ref[lead + k : lead + k + seq, :]
    conv = silu(run).astype(BF16)
    b = conv[:, :n]
    c = conv[:, n:]
    c_ref[...] = c
    b_ref[0] = b[:16].astype(F32)[:8]

    raw = step_ref[...] + bias_ref[...]
    dt = jnp.maximum(raw, 0.0) + jnp.log1p(jnp.exp(-jnp.abs(raw)))
    dt = jnp.concatenate([dt, jnp.zeros((seq, 128 - heads), F32)], axis=1)
    decay = jnp.concatenate([decay_ref[...], jnp.zeros((1, 128 - heads), F32)], axis=1)
    t_at = lax.broadcasted_iota(jnp.int32, (seq, seq), 0)
    s_at = lax.broadcasted_iota(jnp.int32, (seq, seq), 1)
    causal = s_at <= t_at
    cum = jnp.dot(
        causal.astype(F32), -decay * dt, preferred_element_type=F32, precision=lax.Precision.HIGHEST
    )
    cum_t = cum.T
    dt_t = dt.T
    begin = cum[lag - 1 : lag]
    last = cum[seq - 1 : seq]
    spread = (
        lax.broadcasted_iota(jnp.int32, (128, width), 1) // p
        == lax.broadcasted_iota(jnp.int32, (128, width), 0)
    )
    spread = spread.astype(F32).astype(BF16)
    early = lax.broadcasted_iota(jnp.int32, (seq, 128), 0) < lag
    grown = jnp.exp(jnp.where(early, cum, jnp.minimum(cum - begin, 0.0))).astype(BF16)
    tail = jnp.exp(jnp.minimum(last - cum, 0.0)) * dt
    begin_t = cum_t[:heads, lag - 1 : lag]
    last_t = cum_t[:heads, seq - 1 : seq]
    el_ref[0, :heads] = jnp.broadcast_to(jnp.exp(jnp.minimum(last_t - begin_t, 0.0)), (heads, n))
    el_ref[0, heads:] = jnp.broadcast_to(jnp.exp(begin_t), (heads, n))

    scores = lax.dot_general(c, b, (((1,), (1,)), ((), ())), preferred_element_type=F32)
    scores = jnp.where(causal, scores, 0.0)
    top = scores[:half, :half]
    bottom = scores[half:]

    row8 = lax.broadcasted_iota(jnp.int32, (8, 128), 0)
    cum8 = cum[:8]
    dt8 = dt[:8]
    small = [jnp.where(row8 < lag, jnp.exp(jnp.minimum(begin - cum8, 0.0)) * dt8, 0.0).astype(BF16)]
    for j in range(lag):
        rows = []
        for t in range(8):
            if j <= t < lag:
                s = t - j
                gap = jnp.exp(jnp.minimum(cum[t : t + 1] - cum[s : s + 1], 0.0))
                rows.append(gap * scores[t : t + 1, s : s + 1] * dt[s : s + 1])
            else:
                rows.append(jnp.zeros((1, 128), F32))
        small.append(jnp.concatenate(rows, axis=0).astype(BF16))
    small = jnp.concatenate([m.astype(F32) for m in small], axis=0).astype(BF16)

    u_ref[:8, :] = jnp.zeros((8, width), F32)
    u_ref[8:, :] = inner_ref[...].astype(F32)
    lane = lax.broadcasted_iota(jnp.int32, (1, 128), 1)
    for q in range(width // 128):
        cols = slice(q * 128, q * 128 + 128)
        ik = ik_ref[:, cols].astype(F32)
        run = jnp.zeros((seq, 128), F32)
        for k in range(taps):
            run = run + ik[k : k + 1] * u_ref[lead + k : lead + k + seq, cols]
        x = jnp.where(early, 0.0, silu(run)).astype(BF16)
        xf = x.astype(F32)
        y_top = jnp.zeros((half, 128), F32)
        y_bottom = jnp.zeros((seq - half, 128), F32)
        for s in range(128 // p):
            h = q * (128 // p) + s
            own = (lane >= s * p) & (lane < (s + 1) * p)
            xs = jnp.where(own, xf, 0.0).astype(BF16)
            col = cum[:, h : h + 1]
            row = cum_t[h : h + 1]
            dr = dt_t[h : h + 1]
            w_top = jnp.exp(jnp.minimum(col[:half] - row[:, :half], 0.0)) * (top * dr[:, :half])
            w_bottom = jnp.exp(jnp.minimum(col[half:] - row, 0.0)) * (bottom * dr)
            y_top = y_top + jnp.dot(w_top.astype(BF16), xs[:half], preferred_element_type=F32)
            y_bottom = y_bottom + jnp.dot(w_bottom.astype(BF16), xs, preferred_element_type=F32)
        skip = skip_ref[:, cols]
        y = jnp.concatenate([y_top, y_bottom], axis=0) + skip * xf
        z = silu(gate_ref[:, cols].astype(F32))
        az_ref[:, cols] = (y * z).astype(BF16)
        ez = jnp.dot(grown, spread[:, cols], preferred_element_type=F32) * z
        ez_ref[:, cols] = ez.astype(BF16)
        tw = jnp.dot(tail.astype(BF16), spread[:, cols], preferred_element_type=F32)
        xt = (xf * tw).astype(BF16)
        f1_ref[0, cols, :] = lax.dot_general(
            xt, b, (((0,), (0,)), ((), ())), preferred_element_type=F32
        )
        wide = jnp.dot(small, spread[:, cols], preferred_element_type=F32)
        first_ref[0, 0:8, cols] = run[:8]
        first_ref[0, 8:16, cols] = wide[:8]
        z8 = z[:8]
        first_ref[0, 16:24, cols] = jnp.where(row8 < lag, (wide[8:16] + skip) * z8, 0.0)
        for j in range(1, lag):
            first_ref[0, 16 + 8 * j : 24 + 8 * j, cols] = wide[8 + 8 * j : 16 + 8 * j] * z8


def ssd(inner, gate, state, step, history, ik, sk, bias, decay, skip):
    tokens, width = inner.shape
    requests = history.shape[0]
    seq = tokens // requests
    heads = step.shape[1]
    n2 = state.shape[1]
    n = n2 // 2
    lag = ik.shape[0] - 1
    rows = lambda w: pl.BlockSpec((seq, w), lambda r: (r, 0))
    per = lambda *s: pl.BlockSpec((1,) + s, lambda r: (r,) + (0,) * len(s))
    return pl.pallas_call(
        ssd_kernel,
        out_shape=(
            jax.ShapeDtypeStruct((tokens, width), BF16),
            jax.ShapeDtypeStruct((tokens, width), BF16),
            jax.ShapeDtypeStruct((tokens, n), BF16),
            jax.ShapeDtypeStruct((requests, 8, n), F32),
            jax.ShapeDtypeStruct((requests, width, n), F32),
            jax.ShapeDtypeStruct((requests, 2 * heads, n), F32),
            jax.ShapeDtypeStruct((requests, 16 + 8 * lag, width), F32),
        ),
        grid=(requests,),
        in_specs=[
            rows(width),
            rows(width),
            rows(n2),
            rows(heads),
            per(*history.shape[1:]),
            full(ik.shape),
            full(sk.shape),
            full(bias.shape),
            full(decay.shape),
            full(skip.shape),
        ],
        out_specs=(
            rows(width),
            rows(width),
            rows(n),
            per(8, n),
            per(width, n),
            per(2 * heads, n),
            per(16 + 8 * lag, width),
        ),
        scratch_shapes=[pltpu.VMEM((seq + 8, width), F32), pltpu.VMEM((seq + 8, n2), F32)],
        compiler_params=pltpu.CompilerParams(vmem_limit_bytes=24 * MIB),
        cost_estimate=pl.CostEstimate(
            flops=2 * tokens * width * seq * 2, bytes_accessed=14 * MIB, transcendentals=tokens * seq * heads
        ),
        name="ssd",
    )(inner, gate, state, step, history, ik, sk, bias, decay, skip)


def tail_kernel(
    pos_ref,
    back_ref,
    az_ref,
    ez_ref,
    c_ref,
    b_ref,
    f1_ref,
    el_ref,
    first_ref,
    ik_ref,
    g_ref,
    sq_ref,
    final_ref,
    held_ref,
    rows_ref,
    s_ref,
    raw_ref,
    win_ref,
    mix_ref,
    x_ref,
    sem,
    row_sem,
):
    r = pl.program_id(0)
    requests = pl.num_programs(0)
    heads = el_ref.shape[1] // 2
    p = held_ref.shape[1]
    seq, width = az_ref.shape
    lag = ik_ref.shape[0] - 1
    cached = CAP * p

    def fetch(q):
        for h in range(heads):
            e = q * heads + h
            at = pos_ref[e]
            pltpu.make_async_copy(
                back_ref.at[at // CAP, pl.ds(pl.multiple_of((at % CAP) * p, p), p)],
                held_ref.at[e],
                sem.at[q],
            ).start()

    row_copy = pltpu.make_async_copy(back_ref.at[:, cached:], rows_ref, row_sem)

    @pl.when(r == 0)
    def _():
        row_copy.start()
        fetch(0)
        sq_ref[...] = jnp.zeros_like(sq_ref)
        win_ref[...] = jnp.zeros_like(win_ref)
        x_ref[...] = jnp.zeros_like(x_ref)
        row_copy.wait()

    @pl.when(r + 1 < requests)
    def _():
        fetch(r + 1)

    low = lax.broadcasted_iota(jnp.int32, (1, 128), 1) < p
    flat = rows_ref.reshape(rows_ref.shape[0] * rows_ref.shape[1], 128)
    for q in range(heads // 2):
        cols = slice(q * 128, q * 128 + 128)
        even = 2 * pos_ref[r * heads + 2 * q]
        odd = 2 * pos_ref[r * heads + 2 * q + 1]
        a0, a1 = flat[pl.ds(even, 1)], flat[pl.ds(odd, 1)]
        b0, b1 = flat[pl.ds(even + 1, 1)], flat[pl.ds(odd + 1, 1)]
        win_ref[0:1, cols] = jnp.where(low, a0, a1)
        win_ref[2:3, cols] = jnp.where(low, b0, b1)
        mix_ref[q : q + 1] = jnp.where(low, a1, a0)
    mix = pltpu.roll(mix_ref[...], p, 1)
    for q in range(heads // 2):
        win_ref[1:2, q * 128 : q * 128 + 128] = mix[q : q + 1]

    ik = ik_ref[...].astype(F32)
    run = first_ref[0, 0:8]
    for k in range(lag):
        run = run + ik[k : k + 1] * win_ref[k : k + 8]
    row8 = lax.broadcasted_iota(jnp.int32, (8, width), 0)
    x = jnp.where(row8 < lag, silu(run), 0.0).astype(BF16).astype(F32)
    x_ref[8:16] = x
    extra = first_ref[0, 16:24] * x
    for j in range(1, lag):
        extra = extra + first_ref[0, 16 + 8 * j : 24 + 8 * j] * x_ref[8 - j : 16 - j]
    grow = (x * first_ref[0, 8:16]).T.astype(BF16)
    add = jnp.dot(grow, b_ref[0].astype(BF16), preferred_element_type=F32)

    pltpu.make_async_copy(
        held_ref.at[pl.ds(r * heads, heads)], held_ref.at[pl.ds(r * heads, heads)], sem.at[r]
    ).wait()
    for h in range(heads):
        at = slice(h * p, h * p + p)
        block = held_ref[r * heads + h]
        raw_ref[at] = block.astype(BF16)
        block = el_ref[0, heads + h : heads + h + 1] * block + add[at]
        s_ref[at] = block.astype(BF16)
        final_ref[0, h] = el_ref[0, h : h + 1] * block + f1_ref[0, at]

    c = c_ref[...]
    total = jnp.zeros((seq - 16, 128), F32)
    total16 = jnp.zeros((16, 128), F32)
    row16 = lax.broadcasted_iota(jnp.int32, (16, 256), 0)
    nt = (((1,), (1,)), ((), ()))
    for q in range(width // 256):
        cols = slice(q * 256, q * 256 + 256)
        seen = lax.dot_general(c, s_ref[cols], nt, preferred_element_type=F32)
        seen16 = lax.dot_general(c[:16], raw_ref[cols], nt, preferred_element_type=F32)
        seen16 = jnp.where(row16 < lag, seen16, seen[:16])
        az = az_ref[:, cols].astype(F32)
        ez = ez_ref[:, cols].astype(F32)
        g = az[16:] + ez[16:] * seen[16:]
        g16 = az[:16] + ez[:16] * seen16
        g16 = g16 + jnp.concatenate([extra[:, cols], jnp.zeros((8, 256), F32)], axis=0)
        g_ref[:16, cols] = g16.astype(BF16)
        g_ref[16:, cols] = g.astype(BF16)
        g = g * g
        g16 = g16 * g16
        total = total + g[:, :128] + g[:, 128:]
        total16 = total16 + g16[:, :128] + g16[:, 128:]
    total = jnp.concatenate([total16, total], axis=0)
    sq_ref[pl.ds(r, 1), :] = jnp.sum(total.T, axis=0, keepdims=True)


def tail(pos, back, az, ez, c, b, f1, el, first, ik):
    requests, heads2, n = el.shape
    heads = heads2 // 2
    tokens, width = az.shape
    p = width // heads
    seq = tokens // requests
    owners = back.shape[0]
    rows = lambda w: pl.BlockSpec((seq, w), lambda r, _: (r, 0))
    per = lambda *s: pl.BlockSpec((1,) + s, lambda r, _: (r,) + (0,) * len(s))
    return pl.pallas_call(
        tail_kernel,
        out_shape=(
            jax.ShapeDtypeStruct((tokens, width), BF16),
            jax.ShapeDtypeStruct((8, seq), F32),
            jax.ShapeDtypeStruct((requests, heads, p, n), F32),
        ),
        grid_spec=pltpu.PrefetchScalarGridSpec(
            num_scalar_prefetch=1,
            grid=(requests,),
            in_specs=[
                pl.BlockSpec(memory_space=pl.ANY),
                rows(width),
                rows(width),
                rows(n),
                per(*b.shape[1:]),
                per(width, n),
                per(heads2, n),
                per(*first.shape[1:]),
                full(ik.shape),
            ],
            out_specs=(rows(width), full((8, seq)), per(heads, p, n)),
            scratch_shapes=[
                pltpu.VMEM((requests * heads, p, n), F32),
                pltpu.VMEM((owners, 2 * CAP, n), F32),
                pltpu.VMEM((width, n), BF16),
                pltpu.VMEM((width, n), BF16),
                pltpu.VMEM((16, width), F32),
                pltpu.VMEM((8, 128), F32),
                pltpu.VMEM((16, width), F32),
                pltpu.SemaphoreType.DMA((requests,)),
                pltpu.SemaphoreType.DMA,
            ],
        ),
        compiler_params=pltpu.CompilerParams(vmem_limit_bytes=24 * MIB),
        cost_estimate=pl.CostEstimate(
            flops=2 * tokens * width * n, bytes_accessed=14 * MIB, transcendentals=0
        ),
        name="tail",
    )(pos, back, az, ez, c, b, f1, el, first, ik)


def norm_kernel(channels, g_ref, s0_ref, s1_ref, s2_ref, s3_ref, gain_ref, out_ref):
    r = pl.program_id(0)
    at = pl.ds(r, 1)
    seq, width = g_ref.shape
    square = s0_ref[at] + s1_ref[at] + s2_ref[at] + s3_ref[at]
    scale = lax.rsqrt(square / channels + EPSILON)
    scale = jnp.broadcast_to(scale, (128, seq)).T
    gain = gain_ref[...].astype(F32)
    for q in range(width // 128):
        cols = slice(q * 128, q * 128 + 128)
        out_ref[:, cols] = (g_ref[:, cols].astype(F32) * scale * gain[:, cols]).astype(BF16)


def normalise(g, parts, gain, channels):
    tokens, width = g.shape
    seq = parts[0].shape[1]
    rows = pl.BlockSpec((seq, width), lambda r: (r, 0))
    return pl.pallas_call(
        functools.partial(norm_kernel, channels),
        out_shape=jax.ShapeDtypeStruct((tokens, width), BF16),
        grid=(tokens // seq,),
        in_specs=[rows] + [full(parts[0].shape)] * 4 + [full(gain.shape)],
        out_specs=rows,
        compiler_params=pltpu.CompilerParams(vmem_limit_bytes=8 * MIB),
        cost_estimate=pl.CostEstimate(flops=2 * tokens * width, bytes_accessed=4 * MIB, transcendentals=0),
        name="normalise",
    )(g, *parts, gain)


def local(
    activations,
    gate_weight,
    inner_weight,
    state_proj,
    step_weight,
    inner_kernel,
    state_kernel,
    step_bias,
    decay_rate,
    skip_scale,
    norm_gain,
    scan_cache,
    window_cache,
    state_history,
    hit_owner,
    hit_slot,
):
    owners = lax.axis_size("dp")
    groups = lax.axis_size("mp")
    requests, heads = hit_owner.shape
    slots, _, p, n = scan_cache.shape
    width = inner_weight.shape[1]
    blocks = slots * heads

    wanted, pos = prep(hit_owner, hit_slot, owners)
    codes = lax.all_to_all(wanted, "dp", split_axis=0, concat_axis=0, tiled=True)
    sent = pick(codes, scan_cache.reshape(blocks, p, n), window_cache.reshape(blocks, -1))
    back = lax.all_to_all(sent, "dp", split_axis=0, concat_axis=0, tiled=True)

    inner, gate, state, step = project(activations, inner_weight, gate_weight, state_proj, step_weight)
    az, ez, c, b, f1, el, first = ssd(
        inner,
        gate,
        state,
        step,
        state_history,
        inner_kernel,
        state_kernel,
        step_bias[None],
        decay_rate[None],
        jnp.repeat(skip_scale, p)[None],
    )
    g, square, final = tail(pos, back, az, ez, c, b, f1, el, first, inner_kernel)
    pair = [(i, i ^ 1) for i in range(groups)]
    square = square + lax.ppermute(square, "mp", pair)
    parts = [square] + [
        lax.ppermute(square, "mp", [(i, (i + 2 * s) % groups) for i in range(groups)])
        for s in range(1, groups // 2)
    ]
    normed = normalise(g, parts, norm_gain[None], width * groups)
    return normed, final


def solution(mesh):
    placed = (
        P("dp", None),
        P(None, "mp"),
        P(None, "mp"),
        P(),
        P(None, "mp"),
        P(None, "mp"),
        P(),
        P("mp"),
        P("mp"),
        P("mp"),
        P("mp"),
        P("dp", "mp", None, None),
        P("dp", "mp", None),
        P("dp", None, None),
        P("dp", "mp"),
        P("dp", "mp"),
    )
    return jax.shard_map(
        local,
        mesh=mesh,
        in_specs=placed,
        out_specs=(P("dp", "mp"), P("dp", "mp", None, None)),
        check_vma=False,
    )
```

```python
import functools

import jax
import jax.numpy as jnp
from jax import lax
from jax.experimental import pallas as pl
from jax.experimental.pallas import tpu as pltpu
from jax.sharding import PartitionSpec as P

EPSILON = 1e-05
CAP = 8
F32 = jnp.float32
BF16 = jnp.bfloat16
MIB = 1024 * 1024


def silu(v):
    half = 0.5 * v
    return half + half * jnp.tanh(half)


def full(shape, **kw):
    return pl.BlockSpec(shape, lambda *_: (0,) * len(shape), **kw)


def prep_kernel(owner_ref, slot_ref, wanted_ref, pos_ref, count_ref):
    owners = wanted_ref.shape[0]
    requests, heads = owner_ref.shape
    for o in range(owners):
        count_ref[o] = 0
        for k in range(CAP):
            wanted_ref[o, 0, k] = 0
    for r in range(requests):
        for h in range(heads):
            o = owner_ref[r, h]
            k = count_ref[o]
            count_ref[o] = k + 1
            wanted_ref[o, 0, k] = slot_ref[r, h] * heads + h
            pos_ref[r * heads + h] = o * CAP + k


def prep(hit_owner, hit_slot, owners):
    entries = hit_owner.size
    smem = pl.BlockSpec(memory_space=pltpu.SMEM)
    return pl.pallas_call(
        prep_kernel,
        out_shape=(
            jax.ShapeDtypeStruct((owners, 1, 128), jnp.int32),
            jax.ShapeDtypeStruct((entries,), jnp.int32),
        ),
        in_specs=[smem, smem],
        out_specs=(smem, smem),
        scratch_shapes=[pltpu.SMEM((owners,), jnp.int32)],
        name="prep",
    )(hit_owner, hit_slot)


def pick_kernel(codes_ref, cache_ref, window_ref, out_ref, wa_ref, wb_ref, rows_ref, sem):
    owners = out_ref.shape[0]
    p = cache_ref.shape[1]
    half = window_ref.shape[1] // 3
    cached = CAP * p

    @pl.loop(0, owners)
    def _(d):
        for k in range(CAP):
            pltpu.make_async_copy(
                cache_ref.at[codes_ref[d, 0, k]], out_ref.at[d, k * p : k * p + p], sem
            ).start()

    w = window_ref[...].astype(F32)
    first = w[:, : 2 * half]
    second = jnp.concatenate([w[:, 2 * half :], jnp.zeros((w.shape[0], half), F32)], axis=1)
    odd = lax.broadcasted_iota(jnp.int32, first.shape, 0) % 2 == 1
    wa_ref[...] = jnp.where(odd, pltpu.roll(first, half, 1), first)
    wb_ref[...] = jnp.where(odd, pltpu.roll(second, half, 1), second)

    @pl.loop(0, owners)
    def _(d):
        for k in range(CAP):
            at = pl.ds(codes_ref[d, 0, k], 1)
            rows_ref[d, 2 * k : 2 * k + 1] = wa_ref[at]
            rows_ref[d, 2 * k + 1 : 2 * k + 2] = wb_ref[at]

    pltpu.make_async_copy(rows_ref, out_ref.at[:, cached:], sem).start()
    pltpu.make_async_copy(out_ref, out_ref, sem).wait()


def pick(codes, cache, window):
    owners = codes.shape[0]
    blocks, p, n = cache.shape
    return pl.pallas_call(
        pick_kernel,
        out_shape=jax.ShapeDtypeStruct((owners, CAP * p + 2 * CAP, n), F32),
        in_specs=[
            pl.BlockSpec(memory_space=pltpu.SMEM),
            pl.BlockSpec(memory_space=pltpu.VMEM),
            pl.BlockSpec(memory_space=pltpu.VMEM),
        ],
        out_specs=pl.BlockSpec(memory_space=pl.ANY),
        scratch_shapes=[
            pltpu.VMEM((blocks, n), F32),
            pltpu.VMEM((blocks, n), F32),
            pltpu.VMEM((owners, 2 * CAP, n), F32),
            pltpu.SemaphoreType.DMA,
        ],
        compiler_params=pltpu.CompilerParams(vmem_limit_bytes=60 * MIB),
        cost_estimate=pl.CostEstimate(flops=0, bytes_accessed=8 * MIB, transcendentals=0),
        name="pick",
    )(codes, cache, window)


TILE = 256


def project_kernel(steps, act_ref, wi_ref, wg_ref, ws_ref, wd_ref, inner_ref, gate_ref, state_ref, step_ref):
    j = pl.program_id(0)
    rows = act_ref.shape[0]
    chunk = 1024

    def run(w_ref, out_ref):
        @pl.loop(0, rows // chunk)
        def _(m):
            at = pl.ds(pl.multiple_of(m * chunk, chunk), chunk)
            out_ref[at, :] = jnp.dot(act_ref[at, :], w_ref[...], preferred_element_type=F32).astype(out_ref.dtype)

    @pl.when(j == 0)
    def _():
        run(ws_ref, state_ref)
        run(wd_ref, step_ref)

    @pl.when((j > 0) & (j <= steps))
    def _():
        run(wi_ref, inner_ref)

    @pl.when(j > steps)
    def _():
        run(wg_ref, gate_ref)


def project(act, wi, wg, ws, wd):
    rows, depth = act.shape
    width = wi.shape[1]
    steps = width // TILE

    def at_inner(j):
        return (0, jnp.clip(j - 1, 0, steps - 1))

    def at_gate(j):
        return (0, jnp.clip(j - 1 - steps, 0, steps - 1))

    flops = 2 * rows * depth * (2 * width + ws.shape[1] + wd.shape[1])
    return pl.pallas_call(
        functools.partial(project_kernel, steps),
        out_shape=(
            jax.ShapeDtypeStruct((rows, width), BF16),
            jax.ShapeDtypeStruct((rows, width), BF16),
            jax.ShapeDtypeStruct((rows, ws.shape[1]), BF16),
            jax.ShapeDtypeStruct((rows, wd.shape[1]), F32),
        ),
        grid=(1 + 2 * steps,),
        in_specs=[
            full((rows, depth), pipeline_mode=pl.Buffered(1)),
            pl.BlockSpec((depth, TILE), at_inner),
            pl.BlockSpec((depth, TILE), at_gate),
            full(ws.shape, pipeline_mode=pl.Buffered(1)),
            full(wd.shape, pipeline_mode=pl.Buffered(1)),
        ],
        out_specs=(
            pl.BlockSpec((rows, TILE), at_inner),
            pl.BlockSpec((rows, TILE), at_gate),
            full((rows, ws.shape[1])),
            full((rows, wd.shape[1])),
        ),
        compiler_params=pltpu.CompilerParams(vmem_limit_bytes=36 * MIB),
        cost_estimate=pl.CostEstimate(flops=flops, bytes_accessed=32 * MIB, transcendentals=0),
        name="project",
    )(act, wi, wg, ws, wd)


def ssd_kernel(
    inner_ref,
    gate_ref,
    state_ref,
    step_ref,
    hist_ref,
    ik_ref,
    sk_ref,
    bias_ref,
    decay_ref,
    skip_ref,
    az_ref,
    ez_ref,
    c_ref,
    b_ref,
    f1_ref,
    el_ref,
    first_ref,
    u_ref,
    v_ref,
):
    seq, width = inner_ref.shape
    heads = step_ref.shape[1]
    p = width // heads
    taps = ik_ref.shape[0]
    lag = taps - 1
    n = state_ref.shape[1] // 2
    lead = 8 - lag
    half = seq // 2

    v_ref[lead:8, :] = hist_ref[0].astype(F32)
    v_ref[8:, :] = state_ref[...].astype(F32)
    sk = sk_ref[...].astype(F32)
    run = jnp.zeros((seq, 2 * n), F32)
    for k in range(taps):
        run = run + sk[k : k + 1] * v_ref[lead + k : lead + k + seq, :]
    conv = silu(run).astype(BF16)
    b = conv[:, :n]
    c = conv[:, n:]
    c_ref[...] = c
    b_ref[0] = b[:16].astype(F32)[:8]

    raw = step_ref[...] + bias_ref[...]
    dt = jnp.maximum(raw, 0.0) + jnp.log1p(jnp.exp(-jnp.abs(raw)))
    dt = jnp.concatenate([dt, jnp.zeros((seq, 128 - heads), F32)], axis=1)
    decay = jnp.concatenate([decay_ref[...], jnp.zeros((1, 128 - heads), F32)], axis=1)
    t_at = lax.broadcasted_iota(jnp.int32, (seq, seq), 0)
    s_at = lax.broadcasted_iota(jnp.int32, (seq, seq), 1)
    causal = s_at <= t_at
    cum = jnp.dot(
        causal.astype(F32), -decay * dt, preferred_element_type=F32, precision=lax.Precision.HIGHEST
    )
    cum_t = cum.T
    dt_t = dt.T
    begin = cum[lag - 1 : lag]
    last = cum[seq - 1 : seq]
    spread = (
        lax.broadcasted_iota(jnp.int32, (128, width), 1) // p
        == lax.broadcasted_iota(jnp.int32, (128, width), 0)
    )
    spread = spread.astype(F32).astype(BF16)
    early = lax.broadcasted_iota(jnp.int32, (seq, 128), 0) < lag
    grown = jnp.exp(jnp.where(early, cum, jnp.minimum(cum - begin, 0.0))).astype(BF16)
    tail = jnp.exp(jnp.minimum(last - cum, 0.0)) * dt
    begin_t = cum_t[:heads, lag - 1 : lag]
    last_t = cum_t[:heads, seq - 1 : seq]
    el_ref[0, :heads] = jnp.broadcast_to(jnp.exp(jnp.minimum(last_t - begin_t, 0.0)), (heads, n))
    el_ref[0, heads:] = jnp.broadcast_to(jnp.exp(begin_t), (heads, n))

    scores = lax.dot_general(c, b, (((1,), (1,)), ((), ())), preferred_element_type=F32)
    scores = jnp.where(causal, scores, 0.0)
    top = scores[:half, :half]
    bottom = scores[half:]

    row8 = lax.broadcasted_iota(jnp.int32, (8, 128), 0)
    cum8 = cum[:8]
    dt8 = dt[:8]
    small = [jnp.where(row8 < lag, jnp.exp(jnp.minimum(begin - cum8, 0.0)) * dt8, 0.0).astype(BF16)]
    for j in range(lag):
        rows = []
        for t in range(8):
            if j <= t < lag:
                s = t - j
                gap = jnp.exp(jnp.minimum(cum[t : t + 1] - cum[s : s + 1], 0.0))
                rows.append(gap * scores[t : t + 1, s : s + 1] * dt[s : s + 1])
            else:
                rows.append(jnp.zeros((1, 128), F32))
        small.append(jnp.concatenate(rows, axis=0).astype(BF16))
    small = jnp.concatenate([m.astype(F32) for m in small], axis=0).astype(BF16)

    u_ref[:8, :] = jnp.zeros((8, width), F32)
    u_ref[8:, :] = inner_ref[...].astype(F32)
    lane = lax.broadcasted_iota(jnp.int32, (1, 128), 1)
    for q in range(width // 128):
        cols = slice(q * 128, q * 128 + 128)
        ik = ik_ref[:, cols].astype(F32)
        run = jnp.zeros((seq, 128), F32)
        for k in range(taps):
            run = run + ik[k : k + 1] * u_ref[lead + k : lead + k + seq, cols]
        x = jnp.where(early, 0.0, silu(run)).astype(BF16)
        xf = x.astype(F32)
        y_top = jnp.zeros((half, 128), F32)
        y_bottom = jnp.zeros((seq - half, 128), F32)
        for s in range(128 // p):
            h = q * (128 // p) + s
            own = (lane >= s * p) & (lane < (s + 1) * p)
            xs = jnp.where(own, xf, 0.0).astype(BF16)
            col = cum[:, h : h + 1]
            row = cum_t[h : h + 1]
            dr = dt_t[h : h + 1]
            w_top = jnp.exp(jnp.minimum(col[:half] - row[:, :half], 0.0)) * (top * dr[:, :half])
            w_bottom = jnp.exp(jnp.minimum(col[half:] - row, 0.0)) * (bottom * dr)
            y_top = y_top + jnp.dot(w_top.astype(BF16), xs[:half], preferred_element_type=F32)
            y_bottom = y_bottom + jnp.dot(w_bottom.astype(BF16), xs, preferred_element_type=F32)
        skip = skip_ref[:, cols]
        y = jnp.concatenate([y_top, y_bottom], axis=0) + skip * xf
        z = silu(gate_ref[:, cols].astype(F32))
        az_ref[:, cols] = (y * z).astype(BF16)
        ez = jnp.dot(grown, spread[:, cols], preferred_element_type=F32) * z
        ez_ref[:, cols] = ez.astype(BF16)
        tw = jnp.dot(tail.astype(BF16), spread[:, cols], preferred_element_type=F32)
        xt = (xf * tw).astype(BF16)
        f1_ref[0, cols, :] = lax.dot_general(
            xt, b, (((0,), (0,)), ((), ())), preferred_element_type=F32
        )
        wide = jnp.dot(small, spread[:, cols], preferred_element_type=F32)
        first_ref[0, 0:8, cols] = run[:8]
        first_ref[0, 8:16, cols] = wide[:8]
        z8 = z[:8]
        first_ref[0, 16:24, cols] = jnp.where(row8 < lag, (wide[8:16] + skip) * z8, 0.0)
        for j in range(1, lag):
            first_ref[0, 16 + 8 * j : 24 + 8 * j, cols] = wide[8 + 8 * j : 16 + 8 * j] * z8


def ssd(inner, gate, state, step, history, ik, sk, bias, decay, skip):
    tokens, width = inner.shape
    requests = history.shape[0]
    seq = tokens // requests
    heads = step.shape[1]
    n2 = state.shape[1]
    n = n2 // 2
    lag = ik.shape[0] - 1
    rows = lambda w: pl.BlockSpec((seq, w), lambda r: (r, 0))
    per = lambda *s: pl.BlockSpec((1,) + s, lambda r: (r,) + (0,) * len(s))
    return pl.pallas_call(
        ssd_kernel,
        out_shape=(
            jax.ShapeDtypeStruct((tokens, width), BF16),
            jax.ShapeDtypeStruct((tokens, width), BF16),
            jax.ShapeDtypeStruct((tokens, n), BF16),
            jax.ShapeDtypeStruct((requests, 8, n), F32),
            jax.ShapeDtypeStruct((requests, width, n), F32),
            jax.ShapeDtypeStruct((requests, 2 * heads, n), F32),
            jax.ShapeDtypeStruct((requests, 16 + 8 * lag, width), F32),
        ),
        grid=(requests,),
        in_specs=[
            rows(width),
            rows(width),
            rows(n2),
            rows(heads),
            per(*history.shape[1:]),
            full(ik.shape),
            full(sk.shape),
            full(bias.shape),
            full(decay.shape),
            full(skip.shape),
        ],
        out_specs=(
            rows(width),
            rows(width),
            rows(n),
            per(8, n),
            per(width, n),
            per(2 * heads, n),
            per(16 + 8 * lag, width),
        ),
        scratch_shapes=[pltpu.VMEM((seq + 8, width), F32), pltpu.VMEM((seq + 8, n2), F32)],
        compiler_params=pltpu.CompilerParams(vmem_limit_bytes=60 * MIB),
        cost_estimate=pl.CostEstimate(
            flops=2 * tokens * width * seq * 2, bytes_accessed=14 * MIB, transcendentals=tokens * seq * heads
        ),
        name="ssd",
    )(inner, gate, state, step, history, ik, sk, bias, decay, skip)


def fetch_blocks(pos_ref, back_ref, held_ref, sem, r, heads):
    p = held_ref.shape[1]
    for h in range(heads):
        e = r * heads + h
        at = pos_ref[e]
        pltpu.make_async_copy(
            back_ref.at[at // CAP, pl.ds(pl.multiple_of((at % CAP) * p, p), p)],
            held_ref.at[e],
            sem.at[r],
        ).start()


def await_blocks(held_ref, sem, r, heads):
    part = held_ref.at[pl.ds(r * heads, heads)]
    pltpu.make_async_copy(part, part, sem.at[r]).wait()


def first_sources(grow_ref, b_ref, r):
    own = lax.broadcasted_iota(jnp.int32, b_ref.shape, 0) // 8 == r
    b = jnp.where(own, b_ref[...], 0.0).astype(BF16)
    return jnp.dot(grow_ref[...], b, preferred_element_type=F32)


def tail_kernel(
    pos_ref,
    back_ref,
    az_ref,
    ez_ref,
    c_ref,
    b_ref,
    el_ref,
    first_ref,
    ik_ref,
    g_ref,
    sq_ref,
    grow_ref,
    held_ref,
    rows_ref,
    s_ref,
    raw_ref,
    win_ref,
    mix_ref,
    x_ref,
    extra_ref,
    sem,
    row_sem,
):
    r = pl.program_id(0)
    requests = first_ref.shape[0]
    heads = el_ref.shape[1] // 2
    p = held_ref.shape[1]
    seq, width = az_ref.shape
    lag = ik_ref.shape[0] - 1
    cached = CAP * p
    row_copy = pltpu.make_async_copy(back_ref.at[:, cached:], rows_ref, row_sem)

    @pl.when(r == 0)
    def _():
        row_copy.start()
        fetch_blocks(pos_ref, back_ref, held_ref, sem, 0, heads)
        sq_ref[...] = jnp.zeros_like(sq_ref)
        win_ref[...] = jnp.zeros_like(win_ref)
        x_ref[...] = jnp.zeros_like(x_ref)
        row_copy.wait()
        low = lax.broadcasted_iota(jnp.int32, (1, 128), 1) < p
        flat = rows_ref.reshape(rows_ref.shape[0] * rows_ref.shape[1], 128)
        pairs = heads // 2
        for i in range(requests):
            for q in range(pairs):
                cols = slice(q * 128, q * 128 + 128)
                even = 2 * pos_ref[i * heads + 2 * q]
                odd = 2 * pos_ref[i * heads + 2 * q + 1]
                a0, a1 = flat[pl.ds(even, 1)], flat[pl.ds(odd, 1)]
                b0, b1 = flat[pl.ds(even + 1, 1)], flat[pl.ds(odd + 1, 1)]
                win_ref[i, 0:1, cols] = jnp.where(low, a0, a1)
                win_ref[i, 2:3, cols] = jnp.where(low, b0, b1)
                mix_ref[i * pairs + q : i * pairs + q + 1] = jnp.where(low, a1, a0)
        mix = pltpu.roll(mix_ref[...], p, 1)
        for i in range(requests):
            for q in range(pairs):
                win_ref[i, 1:2, q * 128 : q * 128 + 128] = mix[i * pairs + q : i * pairs + q + 1]
        ik = ik_ref[...].astype(F32)
        run = first_ref[:, 0:8]
        for k in range(lag):
            run = run + ik[k : k + 1][None] * win_ref[:, k : k + 8]
        row8 = lax.broadcasted_iota(jnp.int32, run.shape, 1)
        x = jnp.where(row8 < lag, silu(run), 0.0).astype(BF16).astype(F32)
        x_ref[:, 8:16] = x
        extra = first_ref[:, 16:24] * x
        for j in range(1, lag):
            extra = extra + first_ref[:, 16 + 8 * j : 24 + 8 * j] * x_ref[:, 8 - j : 16 - j]
        extra_ref[...] = extra
        grow_ref[...] = (x * first_ref[:, 8:16]).reshape(requests * 8, width).T.astype(BF16)

    @pl.when(r + 1 < requests)
    def _():
        fetch_blocks(pos_ref, back_ref, held_ref, sem, r + 1, heads)

    add = first_sources(grow_ref, b_ref, r)
    await_blocks(held_ref, sem, r, heads)
    for h in range(heads):
        at = slice(h * p, h * p + p)
        block = held_ref[r * heads + h]
        raw_ref[at] = block.astype(BF16)
        s_ref[at] = (el_ref[0, heads + h : heads + h + 1] * block + add[at]).astype(BF16)

    c = c_ref[...]
    total = jnp.zeros((seq - 16, 128), F32)
    total16 = jnp.zeros((16, 128), F32)
    row16 = lax.broadcasted_iota(jnp.int32, (16, 256), 0)
    nt = (((1,), (1,)), ((), ()))
    for q in range(width // 256):
        cols = slice(q * 256, q * 256 + 256)
        seen = lax.dot_general(c, s_ref[cols], nt, preferred_element_type=F32)
        seen16 = lax.dot_general(c[:16], raw_ref[cols], nt, preferred_element_type=F32)
        seen16 = jnp.where(row16 < lag, seen16, seen[:16])
        az = az_ref[:, cols].astype(F32)
        ez = ez_ref[:, cols].astype(F32)
        g = az[16:] + ez[16:] * seen[16:]
        g16 = az[:16] + ez[:16] * seen16
        g16 = g16 + jnp.concatenate([extra_ref[r, :, cols], jnp.zeros((8, 256), F32)], axis=0)
        g_ref[:16, cols] = g16.astype(BF16)
        g_ref[16:, cols] = g.astype(BF16)
        g = g * g
        g16 = g16 * g16
        total = total + g[:, :128] + g[:, 128:]
        total16 = total16 + g16[:, :128] + g16[:, 128:]
    total = jnp.concatenate([total16, total], axis=0)
    sq_ref[pl.ds(r, 1), :] = jnp.sum(total.T, axis=0, keepdims=True)


def tail(pos, back, az, ez, c, b, el, first, ik):
    requests, heads2, n = el.shape
    heads = heads2 // 2
    tokens, width = az.shape
    p = width // heads
    seq = tokens // requests
    owners = back.shape[0]
    rows = lambda w: pl.BlockSpec((seq, w), lambda r, _: (r, 0))
    per = lambda *s: pl.BlockSpec((1,) + s, lambda r, _: (r,) + (0,) * len(s))
    once = lambda s: full(s, pipeline_mode=pl.Buffered(1))
    return pl.pallas_call(
        tail_kernel,
        out_shape=(
            jax.ShapeDtypeStruct((tokens, width), BF16),
            jax.ShapeDtypeStruct((8, seq), F32),
            jax.ShapeDtypeStruct((width, requests * 8), BF16),
        ),
        grid_spec=pltpu.PrefetchScalarGridSpec(
            num_scalar_prefetch=1,
            grid=(requests,),
            in_specs=[
                pl.BlockSpec(memory_space=pl.ANY),
                rows(width),
                rows(width),
                rows(n),
                once(b.shape),
                per(heads2, n),
                once(first.shape),
                once(ik.shape),
            ],
            out_specs=(rows(width), full((8, seq)), full((width, requests * 8))),
            scratch_shapes=[
                pltpu.VMEM((requests * heads, p, n), F32),
                pltpu.VMEM((owners, 2 * CAP, n), F32),
                pltpu.VMEM((width, n), BF16),
                pltpu.VMEM((width, n), BF16),
                pltpu.VMEM((requests, 16, width), F32),
                pltpu.VMEM((requests * heads // 2, 128), F32),
                pltpu.VMEM((requests, 16, width), F32),
                pltpu.VMEM((requests, 8, width), F32),
                pltpu.SemaphoreType.DMA((requests,)),
                pltpu.SemaphoreType.DMA,
            ],
        ),
        compiler_params=pltpu.CompilerParams(vmem_limit_bytes=60 * MIB),
        cost_estimate=pl.CostEstimate(
            flops=2 * tokens * width * n, bytes_accessed=10 * MIB, transcendentals=0
        ),
        name="tail",
    )(pos, back, az, ez, c, b, el, first, ik)


def final_kernel(pos_ref, back_ref, grow_ref, b_ref, el_ref, f1_ref, final_ref, held_ref, sem):
    r = pl.program_id(0)
    requests = pl.num_programs(0)
    heads = el_ref.shape[1] // 2
    p = held_ref.shape[1]

    @pl.when(r == 0)
    def _():
        fetch_blocks(pos_ref, back_ref, held_ref, sem, 0, heads)

    @pl.when(r + 1 < requests)
    def _():
        fetch_blocks(pos_ref, back_ref, held_ref, sem, r + 1, heads)

    add = first_sources(grow_ref, b_ref, r)
    await_blocks(held_ref, sem, r, heads)
    for h in range(heads):
        at = slice(h * p, h * p + p)
        block = el_ref[0, heads + h : heads + h + 1] * held_ref[r * heads + h] + add[at]
        final_ref[0, h] = el_ref[0, h : h + 1] * block + f1_ref[0, at]


def finals(pos, back, grow, b, el, f1):
    requests, heads2, n = el.shape
    heads = heads2 // 2
    width = f1.shape[1]
    p = width // heads
    per = lambda *s: pl.BlockSpec((1,) + s, lambda r, _: (r,) + (0,) * len(s))
    once = lambda s: full(s, pipeline_mode=pl.Buffered(1))
    return pl.pallas_call(
        final_kernel,
        out_shape=jax.ShapeDtypeStruct((requests, heads, p, n), F32),
        grid_spec=pltpu.PrefetchScalarGridSpec(
            num_scalar_prefetch=1,
            grid=(requests,),
            in_specs=[
                pl.BlockSpec(memory_space=pl.ANY),
                once(grow.shape),
                once(b.shape),
                per(heads2, n),
                per(width, n),
            ],
            out_specs=per(heads, p, n),
            scratch_shapes=[
                pltpu.VMEM((requests * heads, p, n), F32),
                pltpu.SemaphoreType.DMA((requests,)),
            ],
        ),
        compiler_params=pltpu.CompilerParams(vmem_limit_bytes=60 * MIB),
        cost_estimate=pl.CostEstimate(
            flops=2 * requests * width * n * 32, bytes_accessed=6 * MIB, transcendentals=0
        ),
        name="finals",
    )(pos, back, grow, b, el, f1)


def norm_kernel(channels, g_ref, s0_ref, s1_ref, s2_ref, s3_ref, gain_ref, out_ref):
    r = pl.program_id(0)
    at = pl.ds(r, 1)
    seq, width = g_ref.shape
    square = s0_ref[at] + s1_ref[at] + s2_ref[at] + s3_ref[at]
    scale = lax.rsqrt(square / channels + EPSILON)
    scale = jnp.broadcast_to(scale, (128, seq)).T
    gain = gain_ref[...].astype(F32)
    for q in range(width // 128):
        cols = slice(q * 128, q * 128 + 128)
        out_ref[:, cols] = (g_ref[:, cols].astype(F32) * scale * gain[:, cols]).astype(BF16)


def normalise(g, parts, gain, channels):
    tokens, width = g.shape
    seq = parts[0].shape[1]
    rows = pl.BlockSpec((seq, width), lambda r: (r, 0))
    return pl.pallas_call(
        functools.partial(norm_kernel, channels),
        out_shape=jax.ShapeDtypeStruct((tokens, width), BF16),
        grid=(tokens // seq,),
        in_specs=[rows] + [full(parts[0].shape)] * 4 + [full(gain.shape)],
        out_specs=rows,
        compiler_params=pltpu.CompilerParams(vmem_limit_bytes=60 * MIB),
        cost_estimate=pl.CostEstimate(flops=2 * tokens * width, bytes_accessed=4 * MIB, transcendentals=0),
        name="normalise",
    )(g, *parts, gain)


def local(
    activations,
    gate_weight,
    inner_weight,
    state_proj,
    step_weight,
    inner_kernel,
    state_kernel,
    step_bias,
    decay_rate,
    skip_scale,
    norm_gain,
    scan_cache,
    window_cache,
    state_history,
    hit_owner,
    hit_slot,
):
    owners = lax.axis_size("dp")
    groups = lax.axis_size("mp")
    requests, heads = hit_owner.shape
    slots, _, p, n = scan_cache.shape
    width = inner_weight.shape[1]
    blocks = slots * heads

    wanted, pos = prep(hit_owner, hit_slot, owners)
    codes = lax.all_to_all(wanted, "dp", split_axis=0, concat_axis=0, tiled=True)
    sent = pick(codes, scan_cache.reshape(blocks, p, n), window_cache.reshape(blocks, -1))
    back = lax.all_to_all(sent, "dp", split_axis=0, concat_axis=0, tiled=True)

    inner, gate, state, step = project(activations, inner_weight, gate_weight, state_proj, step_weight)
    az, ez, c, b, f1, el, first = ssd(
        inner,
        gate,
        state,
        step,
        state_history,
        inner_kernel,
        state_kernel,
        step_bias[None],
        decay_rate[None],
        jnp.repeat(skip_scale, p)[None],
    )
    b = b.reshape(-1, n)
    g, square, grow = tail(pos, back, az, ez, c, b, el, first, inner_kernel)
    final = finals(pos, back, grow, b, el, f1)
    pair = [(i, i ^ 1) for i in range(groups)]
    square = square + lax.ppermute(square, "mp", pair)
    parts = [square] + [
        lax.ppermute(square, "mp", [(i, (i + 2 * s) % groups) for i in range(groups)])
        for s in range(1, groups // 2)
    ]
    normed = normalise(g, parts, norm_gain[None], width * groups)
    return normed, final


def solution(mesh):
    placed = (
        P("dp", None),
        P(None, "mp"),
        P(None, "mp"),
        P(),
        P(None, "mp"),
        P(None, "mp"),
        P(),
        P("mp"),
        P("mp"),
        P("mp"),
        P("mp"),
        P("dp", "mp", None, None),
        P("dp", "mp", None),
        P("dp", None, None),
        P("dp", "mp"),
        P("dp", "mp"),
    )
    return jax.shard_map(
        local,
        mesh=mesh,
        in_specs=placed,
        out_specs=(P("dp", "mp"), P("dp", "mp", None, None)),
        check_vma=False,
    )
```

```python
import functools

import jax
import jax.numpy as jnp
from jax import lax
from jax.experimental import pallas as pl
from jax.experimental.pallas import tpu as pltpu
from jax.sharding import PartitionSpec as P

EPSILON = 1e-05
CAP = 8
F32 = jnp.float32
BF16 = jnp.bfloat16
MIB = 1024 * 1024


def silu(v):
    half = 0.5 * v
    return half + half * jnp.tanh(half)


def full(shape, **kw):
    return pl.BlockSpec(shape, lambda *_: (0,) * len(shape), **kw)


def prep_kernel(owner_ref, slot_ref, wanted_ref, pos_ref, count_ref):
    owners = wanted_ref.shape[0]
    requests, heads = owner_ref.shape
    for o in range(owners):
        count_ref[o] = 0
        for k in range(CAP):
            wanted_ref[o, 0, k] = 0
    for r in range(requests):
        for h in range(heads):
            o = owner_ref[r, h]
            k = count_ref[o]
            count_ref[o] = k + 1
            wanted_ref[o, 0, k] = slot_ref[r, h] * heads + h
            pos_ref[r * heads + h] = o * CAP + k


def prep(hit_owner, hit_slot, owners):
    entries = hit_owner.size
    smem = pl.BlockSpec(memory_space=pltpu.SMEM)
    return pl.pallas_call(
        prep_kernel,
        out_shape=(
            jax.ShapeDtypeStruct((owners, 1, 128), jnp.int32),
            jax.ShapeDtypeStruct((entries,), jnp.int32),
        ),
        in_specs=[smem, smem],
        out_specs=(smem, smem),
        scratch_shapes=[pltpu.SMEM((owners,), jnp.int32)],
        name="prep",
    )(hit_owner, hit_slot)


def pick_kernel(codes_ref, cache_ref, window_ref, out_ref, wa_ref, wb_ref, rows_ref, sem):
    owners = out_ref.shape[0]
    p = cache_ref.shape[1]
    half = window_ref.shape[1] // 3
    cached = CAP * p

    @pl.loop(0, owners)
    def _(d):
        for k in range(CAP):
            pltpu.make_async_copy(
                cache_ref.at[codes_ref[d, 0, k]], out_ref.at[d, k * p : k * p + p], sem
            ).start()

    w = window_ref[...].astype(F32)
    first = w[:, : 2 * half]
    second = jnp.concatenate([w[:, 2 * half :], jnp.zeros((w.shape[0], half), F32)], axis=1)
    odd = lax.broadcasted_iota(jnp.int32, first.shape, 0) % 2 == 1
    wa_ref[...] = jnp.where(odd, pltpu.roll(first, half, 1), first)
    wb_ref[...] = jnp.where(odd, pltpu.roll(second, half, 1), second)

    @pl.loop(0, owners)
    def _(d):
        for k in range(CAP):
            at = pl.ds(codes_ref[d, 0, k], 1)
            rows_ref[d, 2 * k : 2 * k + 1] = wa_ref[at]
            rows_ref[d, 2 * k + 1 : 2 * k + 2] = wb_ref[at]

    pltpu.make_async_copy(rows_ref, out_ref.at[:, cached:], sem).start()
    pltpu.make_async_copy(out_ref, out_ref, sem).wait()


def pick(codes, cache, window):
    owners = codes.shape[0]
    blocks, p, n = cache.shape
    return pl.pallas_call(
        pick_kernel,
        out_shape=jax.ShapeDtypeStruct((owners, CAP * p + 2 * CAP, n), F32),
        in_specs=[
            pl.BlockSpec(memory_space=pltpu.SMEM),
            pl.BlockSpec(memory_space=pltpu.VMEM),
            pl.BlockSpec(memory_space=pltpu.VMEM),
        ],
        out_specs=pl.BlockSpec(memory_space=pl.ANY),
        scratch_shapes=[
            pltpu.VMEM((blocks, n), F32),
            pltpu.VMEM((blocks, n), F32),
            pltpu.VMEM((owners, 2 * CAP, n), F32),
            pltpu.SemaphoreType.DMA,
        ],
        compiler_params=pltpu.CompilerParams(vmem_limit_bytes=60 * MIB),
        cost_estimate=pl.CostEstimate(flops=0, bytes_accessed=8 * MIB, transcendentals=0),
        name="pick",
    )(codes, cache, window)


TILE = 256


def project_kernel(steps, act_ref, wi_ref, wg_ref, ws_ref, wd_ref, inner_ref, gate_ref, state_ref, step_ref):
    j = pl.program_id(0)
    rows = act_ref.shape[0]
    chunk = 1024

    def run(w_ref, out_ref):
        @pl.loop(0, rows // chunk)
        def _(m):
            at = pl.ds(pl.multiple_of(m * chunk, chunk), chunk)
            out_ref[at, :] = jnp.dot(act_ref[at, :], w_ref[...], preferred_element_type=F32).astype(out_ref.dtype)

    @pl.when(j == 0)
    def _():
        run(ws_ref, state_ref)
        run(wd_ref, step_ref)

    @pl.when((j > 0) & (j <= steps))
    def _():
        run(wi_ref, inner_ref)

    @pl.when(j > steps)
    def _():
        run(wg_ref, gate_ref)


def project(act, wi, wg, ws, wd):
    rows, depth = act.shape
    width = wi.shape[1]
    steps = width // TILE

    def at_inner(j):
        return (0, jnp.clip(j - 1, 0, steps - 1))

    def at_gate(j):
        return (0, jnp.clip(j - 1 - steps, 0, steps - 1))

    flops = 2 * rows * depth * (2 * width + ws.shape[1] + wd.shape[1])
    return pl.pallas_call(
        functools.partial(project_kernel, steps),
        out_shape=(
            jax.ShapeDtypeStruct((rows, width), BF16),
            jax.ShapeDtypeStruct((rows, width), BF16),
            jax.ShapeDtypeStruct((rows, ws.shape[1]), BF16),
            jax.ShapeDtypeStruct((rows, wd.shape[1]), F32),
        ),
        grid=(1 + 2 * steps,),
        in_specs=[
            full((rows, depth), pipeline_mode=pl.Buffered(1)),
            pl.BlockSpec((depth, TILE), at_inner),
            pl.BlockSpec((depth, TILE), at_gate),
            full(ws.shape, pipeline_mode=pl.Buffered(1)),
            full(wd.shape, pipeline_mode=pl.Buffered(1)),
        ],
        out_specs=(
            pl.BlockSpec((rows, TILE), at_inner),
            pl.BlockSpec((rows, TILE), at_gate),
            full((rows, ws.shape[1])),
            full((rows, wd.shape[1])),
        ),
        compiler_params=pltpu.CompilerParams(vmem_limit_bytes=60 * MIB),
        cost_estimate=pl.CostEstimate(flops=flops, bytes_accessed=32 * MIB, transcendentals=0),
        name="project",
    )(act, wi, wg, ws, wd)


def ssd_kernel(
    inner_ref,
    gate_ref,
    state_ref,
    step_ref,
    hist_ref,
    ik_ref,
    sk_ref,
    bias_ref,
    decay_ref,
    skip_ref,
    az_ref,
    ez_ref,
    c_ref,
    f1_ref,
    small_ref,
    first_ref,
    u_ref,
    v_ref,
):
    seq, width = inner_ref.shape
    heads = step_ref.shape[1]
    p = width // heads
    taps = ik_ref.shape[0]
    lag = taps - 1
    n = state_ref.shape[1] // 2
    lead = 8 - lag
    half = seq // 2

    v_ref[lead:8, :] = hist_ref[0].astype(F32)
    v_ref[8:, :] = state_ref[...].astype(F32)
    sk = sk_ref[...].astype(F32)
    run = jnp.zeros((seq, 2 * n), F32)
    for k in range(taps):
        run = run + sk[k : k + 1] * v_ref[lead + k : lead + k + seq, :]
    conv = silu(run).astype(BF16)
    b = conv[:, :n]
    c = conv[:, n:]
    c_ref[...] = c
    small_ref[0, 2 * heads :] = b[:16].astype(F32)[:8]

    raw = step_ref[...] + bias_ref[...]
    dt = jnp.maximum(raw, 0.0) + jnp.log1p(jnp.exp(-jnp.abs(raw)))
    dt = jnp.concatenate([dt, jnp.zeros((seq, 128 - heads), F32)], axis=1)
    decay = jnp.concatenate([decay_ref[...], jnp.zeros((1, 128 - heads), F32)], axis=1)
    t_at = lax.broadcasted_iota(jnp.int32, (seq, seq), 0)
    s_at = lax.broadcasted_iota(jnp.int32, (seq, seq), 1)
    causal = s_at <= t_at
    cum = jnp.dot(
        causal.astype(F32), -decay * dt, preferred_element_type=F32, precision=lax.Precision.HIGHEST
    )
    cum_t = cum.T
    dt_t = dt.T
    begin = cum[lag - 1 : lag]
    last = cum[seq - 1 : seq]
    spread = (
        lax.broadcasted_iota(jnp.int32, (128, width), 1) // p
        == lax.broadcasted_iota(jnp.int32, (128, width), 0)
    )
    spread = spread.astype(F32).astype(BF16)
    early = lax.broadcasted_iota(jnp.int32, (seq, 128), 0) < lag
    grown = jnp.exp(jnp.where(early, cum, jnp.minimum(cum - begin, 0.0))).astype(BF16)
    tail = jnp.exp(jnp.minimum(last - cum, 0.0)) * dt
    begin_t = cum_t[:heads, lag - 1 : lag]
    last_t = cum_t[:heads, seq - 1 : seq]
    small_ref[0, :heads] = jnp.broadcast_to(jnp.exp(jnp.minimum(last_t - begin_t, 0.0)), (heads, n))
    small_ref[0, heads : 2 * heads] = jnp.broadcast_to(jnp.exp(begin_t), (heads, n))

    scores = lax.dot_general(c, b, (((1,), (1,)), ((), ())), preferred_element_type=F32)
    scores = jnp.where(causal, scores, 0.0)
    top = scores[:half, :half]
    bottom = scores[half:]

    row8 = lax.broadcasted_iota(jnp.int32, (8, 128), 0)
    cum8 = cum[:8]
    dt8 = dt[:8]
    small = [jnp.where(row8 < lag, jnp.exp(jnp.minimum(begin - cum8, 0.0)) * dt8, 0.0).astype(BF16)]
    for j in range(lag):
        rows = []
        for t in range(8):
            if j <= t < lag:
                s = t - j
                gap = jnp.exp(jnp.minimum(cum[t : t + 1] - cum[s : s + 1], 0.0))
                rows.append(gap * scores[t : t + 1, s : s + 1] * dt[s : s + 1])
            else:
                rows.append(jnp.zeros((1, 128), F32))
        small.append(jnp.concatenate(rows, axis=0).astype(BF16))
    small = jnp.concatenate([m.astype(F32) for m in small], axis=0).astype(BF16)

    u_ref[:8, :] = jnp.zeros((8, width), F32)
    u_ref[8:, :] = inner_ref[...].astype(F32)
    lane = lax.broadcasted_iota(jnp.int32, (1, 128), 1)
    for q in range(width // 128):
        cols = slice(q * 128, q * 128 + 128)
        ik = ik_ref[:, cols].astype(F32)
        run = jnp.zeros((seq, 128), F32)
        for k in range(taps):
            run = run + ik[k : k + 1] * u_ref[lead + k : lead + k + seq, cols]
        x = jnp.where(early, 0.0, silu(run)).astype(BF16)
        xf = x.astype(F32)
        y_top = jnp.zeros((half, 128), F32)
        y_bottom = jnp.zeros((seq - half, 128), F32)
        for s in range(128 // p):
            h = q * (128 // p) + s
            own = (lane >= s * p) & (lane < (s + 1) * p)
            xs = jnp.where(own, xf, 0.0).astype(BF16)
            col = cum[:, h : h + 1]
            row = cum_t[h : h + 1]
            dr = dt_t[h : h + 1]
            w_top = jnp.exp(jnp.minimum(col[:half] - row[:, :half], 0.0)) * (top * dr[:, :half])
            w_bottom = jnp.exp(jnp.minimum(col[half:] - row, 0.0)) * (bottom * dr)
            y_top = y_top + jnp.dot(w_top.astype(BF16), xs[:half], preferred_element_type=F32)
            y_bottom = y_bottom + jnp.dot(w_bottom.astype(BF16), xs, preferred_element_type=F32)
        skip = skip_ref[:, cols]
        y = jnp.concatenate([y_top, y_bottom], axis=0) + skip * xf
        z = silu(gate_ref[:, cols].astype(F32))
        az_ref[:, cols] = (y * z).astype(BF16)
        ez = jnp.dot(grown, spread[:, cols], preferred_element_type=F32) * z
        ez_ref[:, cols] = ez.astype(BF16)
        tw = jnp.dot(tail.astype(BF16), spread[:, cols], preferred_element_type=F32)
        xt = (xf * tw).astype(BF16)
        f1_ref[0, cols, :] = lax.dot_general(
            xt, b, (((0,), (0,)), ((), ())), preferred_element_type=F32
        )
        wide = jnp.dot(small, spread[:, cols], preferred_element_type=F32)
        first_ref[0, 0:8, cols] = run[:8]
        first_ref[0, 16 + 8 * lag : 16 + 8 * lag + taps, cols] = ik
        first_ref[0, 8:16, cols] = wide[:8]
        z8 = z[:8]
        first_ref[0, 16:24, cols] = jnp.where(row8 < lag, (wide[8:16] + skip) * z8, 0.0)
        for j in range(1, lag):
            first_ref[0, 16 + 8 * j : 24 + 8 * j, cols] = wide[8 + 8 * j : 16 + 8 * j] * z8


def ssd(inner, gate, state, step, history, ik, sk, bias, decay, skip):
    tokens, width = inner.shape
    requests = history.shape[0]
    seq = tokens // requests
    heads = step.shape[1]
    n2 = state.shape[1]
    n = n2 // 2
    lag = ik.shape[0] - 1
    rows = lambda w: pl.BlockSpec((seq, w), lambda r: (r, 0))
    per = lambda *s: pl.BlockSpec((1,) + s, lambda r: (r,) + (0,) * len(s))
    return pl.pallas_call(
        ssd_kernel,
        out_shape=(
            jax.ShapeDtypeStruct((tokens, width), BF16),
            jax.ShapeDtypeStruct((tokens, width), BF16),
            jax.ShapeDtypeStruct((tokens, n), BF16),
            jax.ShapeDtypeStruct((requests, width, n), F32),
            jax.ShapeDtypeStruct((requests, 2 * heads + 8, n), F32),
            jax.ShapeDtypeStruct((requests, 24 + 8 * lag, width), F32),
        ),
        grid=(requests,),
        in_specs=[
            rows(width),
            rows(width),
            rows(n2),
            rows(heads),
            per(*history.shape[1:]),
            full(ik.shape),
            full(sk.shape),
            full(bias.shape),
            full(decay.shape),
            full(skip.shape),
        ],
        out_specs=(
            rows(width),
            rows(width),
            rows(n),
            per(width, n),
            per(2 * heads + 8, n),
            per(24 + 8 * lag, width),
        ),
        scratch_shapes=[pltpu.VMEM((seq + 8, width), F32), pltpu.VMEM((seq + 8, n2), F32)],
        compiler_params=pltpu.CompilerParams(vmem_limit_bytes=60 * MIB),
        cost_estimate=pl.CostEstimate(
            flops=2 * tokens * width * seq * 2, bytes_accessed=14 * MIB, transcendentals=tokens * seq * heads
        ),
        name="ssd",
    )(inner, gate, state, step, history, ik, sk, bias, decay, skip)


def first_sources(grow_ref, small_ref, r):
    requests = small_ref.shape[0]
    b = small_ref[r, small_ref.shape[1] - 8 :]
    zero = jnp.zeros_like(b)
    b = jnp.concatenate([b if i == r else zero for i in range(requests)], axis=0).astype(BF16)
    return jnp.dot(grow_ref[...], b, preferred_element_type=F32)


def tail_kernel(
    pos_ref,
    back_ref,
    az_hbm,
    ez_hbm,
    c_hbm,
    small_hbm,
    first_hbm,
    g_ref,
    sq_ref,
    grow_ref,
    held_ref,
    az_ref,
    ez_ref,
    c_ref,
    small_ref,
    first_ref,
    rows_ref,
    s_ref,
    raw_ref,
    win_ref,
    mix_ref,
    x_ref,
    extra_ref,
    sem,
    az_sem,
    ez_sem,
    c_sem,
    once_sem,
):
    requests = first_ref.shape[0]
    heads = (small_ref.shape[1] - 8) // 2
    p = held_ref.shape[1]
    tokens, width = g_ref.shape
    seq = tokens // requests
    lag = (first_ref.shape[1] - 24) // 8
    pairs = heads // 2

    def rows_of(r):
        return slice(r * seq, r * seq + seq)

    def copies(r):
        return (
            pltpu.make_async_copy(az_hbm.at[rows_of(r)], az_ref.at[rows_of(r)], az_sem.at[r]),
            pltpu.make_async_copy(ez_hbm.at[rows_of(r)], ez_ref.at[rows_of(r)], ez_sem.at[r]),
            pltpu.make_async_copy(c_hbm.at[rows_of(r)], c_ref.at[rows_of(r)], c_sem.at[r]),
        )

    def fetch(r):
        for h in range(heads):
            e = r * heads + h
            at = pos_ref[e]
            pltpu.make_async_copy(
                back_ref.at[at // CAP, pl.ds(pl.multiple_of((at % CAP) * p, p), p)],
                held_ref.at[e],
                sem.at[r],
            ).start()
        for copy in copies(r):
            copy.start()

    once = (
        pltpu.make_async_copy(back_ref.at[:, CAP * p :], rows_ref, once_sem.at[0]),
        pltpu.make_async_copy(first_hbm, first_ref, once_sem.at[1]),
        pltpu.make_async_copy(small_hbm, small_ref, once_sem.at[2]),
    )
    for copy in once:
        copy.start()
    fetch(0)
    fetch(1)
    win_ref[...] = jnp.zeros_like(win_ref)
    x_ref[...] = jnp.zeros_like(x_ref)
    once[0].wait()

    low = lax.broadcasted_iota(jnp.int32, (1, 128), 1) < p
    flat = rows_ref.reshape(rows_ref.shape[0] * rows_ref.shape[1], 128)
    for i in range(requests):
        for q in range(pairs):
            cols = slice(q * 128, q * 128 + 128)
            even = 2 * pos_ref[i * heads + 2 * q]
            odd = 2 * pos_ref[i * heads + 2 * q + 1]
            a0, a1 = flat[pl.ds(even, 1)], flat[pl.ds(odd, 1)]
            b0, b1 = flat[pl.ds(even + 1, 1)], flat[pl.ds(odd + 1, 1)]
            win_ref[i, 0:1, cols] = jnp.where(low, a0, a1)
            win_ref[i, 2:3, cols] = jnp.where(low, b0, b1)
            mix_ref[i * pairs + q : i * pairs + q + 1] = jnp.where(low, a1, a0)
    mix = pltpu.roll(mix_ref[...], p, 1)
    for i in range(requests):
        for q in range(pairs):
            win_ref[i, 1:2, q * 128 : q * 128 + 128] = mix[i * pairs + q : i * pairs + q + 1]

    once[1].wait()
    run = first_ref[:, 0:8]
    for k in range(lag):
        at = 16 + 8 * lag + k
        run = run + first_ref[:, at : at + 1] * win_ref[:, k : k + 8]
    row8 = lax.broadcasted_iota(jnp.int32, run.shape, 1)
    x = jnp.where(row8 < lag, silu(run), 0.0).astype(BF16).astype(F32)
    x_ref[:, 8:16] = x
    extra = first_ref[:, 16:24] * x
    for j in range(1, lag):
        extra = extra + first_ref[:, 16 + 8 * j : 24 + 8 * j] * x_ref[:, 8 - j : 16 - j]
    extra_ref[...] = extra
    grow_ref[...] = (x * first_ref[:, 8:16]).reshape(requests * 8, width).T.astype(BF16)

    for r in range(2, requests):
        fetch(r)

    once[2].wait()
    row16 = lax.broadcasted_iota(jnp.int32, (16, 256), 0)
    nt = (((1,), (1,)), ((), ()))
    squares = []
    for r in range(requests):
        rows = rows_of(r)
        add = first_sources(grow_ref, small_ref, r)
        part = held_ref.at[r * heads : r * heads + heads]
        pltpu.make_async_copy(part, part, sem.at[r]).wait()
        for h in range(heads):
            at = slice(h * p, h * p + p)
            block = held_ref[r * heads + h]
            raw_ref[r % 2, at] = block.astype(BF16)
            s_ref[r % 2, at] = (small_ref[r, heads + h : heads + h + 1] * block + add[at]).astype(BF16)
        for copy in copies(r):
            copy.wait()
        c = c_ref[rows]
        total = jnp.zeros((seq - 16, 128), F32)
        total16 = jnp.zeros((16, 128), F32)
        for q in range(width // 256):
            cols = slice(q * 256, q * 256 + 256)
            seen = lax.dot_general(c, s_ref[r % 2, cols], nt, preferred_element_type=F32)
            seen16 = lax.dot_general(c[:16], raw_ref[r % 2, cols], nt, preferred_element_type=F32)
            seen16 = jnp.where(row16 < lag, seen16, seen[:16])
            az = az_ref[rows, cols].astype(F32)
            ez = ez_ref[rows, cols].astype(F32)
            g = az[16:] + ez[16:] * seen[16:]
            g16 = az[:16] + ez[:16] * seen16
            g16 = g16 + jnp.concatenate([extra_ref[r, :, cols], jnp.zeros((8, 256), F32)], axis=0)
            g_ref[r * seq : r * seq + 16, cols] = g16.astype(BF16)
            g_ref[r * seq + 16 : r * seq + seq, cols] = g.astype(BF16)
            g = g * g
            g16 = g16 * g16
            total = total + g[:, :128] + g[:, 128:]
            total16 = total16 + g16[:, :128] + g16[:, 128:]
        total = jnp.concatenate([total16, total], axis=0)
        squares.append(jnp.sum(total.T, axis=0, keepdims=True))
    squares.append(jnp.zeros((8 - requests, seq), F32))
    sq_ref[...] = jnp.concatenate(squares, axis=0)


def in_hbm(*arrays):
    return [pltpu.with_memory_space_constraint(v, pltpu.HBM) for v in arrays]


def tail(pos, back, az, ez, c, small, first):
    requests, packed, n = small.shape
    heads = (packed - 8) // 2
    tokens, width = az.shape
    p = width // heads
    seq = tokens // requests
    owners = back.shape[0]
    vmem = pl.BlockSpec(memory_space=pltpu.VMEM)
    hbm = pl.BlockSpec(memory_space=pltpu.HBM)
    return pl.pallas_call(
        tail_kernel,
        out_shape=(
            pltpu.VMEM((tokens, width), BF16),
            pltpu.VMEM((8, seq), F32),
            pltpu.VMEM((width, requests * 8), BF16),
            pltpu.VMEM((requests * heads, p, n), F32),
        ),
        in_specs=[pl.BlockSpec(memory_space=pltpu.SMEM)] + [hbm] * 6,
        out_specs=(vmem,) * 4,
        scratch_shapes=[
            pltpu.VMEM((tokens, width), BF16),
            pltpu.VMEM((tokens, width), BF16),
            pltpu.VMEM((tokens, n), BF16),
            pltpu.VMEM(small.shape, F32),
            pltpu.VMEM(first.shape, F32),
            pltpu.VMEM((owners, 2 * CAP, n), F32),
            pltpu.VMEM((2, width, n), BF16),
            pltpu.VMEM((2, width, n), BF16),
            pltpu.VMEM((requests, 16, width), F32),
            pltpu.VMEM((requests * heads // 2, 128), F32),
            pltpu.VMEM((requests, 16, width), F32),
            pltpu.VMEM((requests, 8, width), F32),
            pltpu.SemaphoreType.DMA((requests,)),
            pltpu.SemaphoreType.DMA((requests,)),
            pltpu.SemaphoreType.DMA((requests,)),
            pltpu.SemaphoreType.DMA((requests,)),
            pltpu.SemaphoreType.DMA((3,)),
        ],
        compiler_params=pltpu.CompilerParams(vmem_limit_bytes=24 * MIB),
        cost_estimate=pl.CostEstimate(
            flops=2 * tokens * width * n, bytes_accessed=10 * MIB, transcendentals=0
        ),
        name="tail",
    )(pos, *in_hbm(back, az, ez, c, small, first))


def final_kernel(held_ref, grow_ref, small_ref, f1_hbm, out_ref, f1_ref, made_ref, f1_sem, sem):
    requests, heads, p = out_ref.shape[:3]

    def part(r):
        return pltpu.make_async_copy(f1_hbm.at[r], f1_ref.at[r], f1_sem.at[r])

    for r in range(requests):
        part(r).start()

    def copy(r):
        return pltpu.make_async_copy(made_ref.at[r], out_ref.at[r], sem.at[r])

    for r in range(requests):
        add = first_sources(grow_ref, small_ref, r)
        part(r).wait()
        for h in range(heads):
            at = slice(h * p, h * p + p)
            block = small_ref[r, heads + h : heads + h + 1] * held_ref[r * heads + h] + add[at]
            made_ref[r, h] = small_ref[r, h : h + 1] * block + f1_ref[r, at]
        copy(r).start()
    for r in range(requests):
        copy(r).wait()


def finals(held, grow, small, f1):
    requests, width, n = f1.shape
    heads = (small.shape[1] - 8) // 2
    p = width // heads
    vmem = pl.BlockSpec(memory_space=pltpu.VMEM)
    return pl.pallas_call(
        final_kernel,
        out_shape=jax.ShapeDtypeStruct((requests, heads, p, n), F32),
        in_specs=[vmem] * 3 + [pl.BlockSpec(memory_space=pltpu.HBM)],
        out_specs=pl.BlockSpec(memory_space=pltpu.HBM),
        scratch_shapes=[
            pltpu.VMEM((requests, width, n), F32),
            pltpu.VMEM((requests, heads, p, n), F32),
            pltpu.SemaphoreType.DMA((requests,)),
            pltpu.SemaphoreType.DMA((requests,)),
        ],
        compiler_params=pltpu.CompilerParams(vmem_limit_bytes=16 * MIB),
        cost_estimate=pl.CostEstimate(
            flops=2 * requests * width * n * 32, bytes_accessed=6 * MIB, transcendentals=0
        ),
        name="finals",
    )(held, grow, small, *in_hbm(f1))


def norm_kernel(channels, g_ref, s0_ref, s1_ref, s2_ref, s3_ref, gain_ref, out_ref, made_ref, sem):
    tokens, width = g_ref.shape
    seq = s0_ref.shape[1]
    step = 128
    gain = gain_ref[...].astype(F32)
    square = s0_ref[...] + s1_ref[...] + s2_ref[...] + s3_ref[...]
    scale = lax.rsqrt(square / channels + EPSILON)

    def copy(i):
        rows = slice(i * step, i * step + step)
        return pltpu.make_async_copy(made_ref.at[rows], out_ref.at[rows], sem.at[i])

    for i in range(tokens // step):
        rows = slice(i * step, i * step + step)
        r, at = i * step // seq, i * step % seq
        wide = jnp.broadcast_to(scale[r : r + 1, at : at + step], (128, step)).T
        for q in range(width // 128):
            cols = slice(q * 128, q * 128 + 128)
            made_ref[rows, cols] = (g_ref[rows, cols].astype(F32) * wide * gain[:, cols]).astype(BF16)
        copy(i).start()
    for i in range(tokens // step):
        copy(i).wait()


def normalise(g, parts, gain, channels):
    tokens, width = g.shape
    vmem = pl.BlockSpec(memory_space=pltpu.VMEM)
    return pl.pallas_call(
        functools.partial(norm_kernel, channels),
        out_shape=jax.ShapeDtypeStruct((tokens, width), BF16),
        in_specs=[vmem] * 6,
        out_specs=pl.BlockSpec(memory_space=pltpu.HBM),
        scratch_shapes=[pltpu.VMEM((tokens, width), BF16), pltpu.SemaphoreType.DMA((tokens // 128,))],
        compiler_params=pltpu.CompilerParams(vmem_limit_bytes=8 * MIB),
        cost_estimate=pl.CostEstimate(flops=2 * tokens * width, bytes_accessed=4 * MIB, transcendentals=0),
        name="normalise",
    )(g, *parts, gain)


def local(
    activations,
    gate_weight,
    inner_weight,
    state_proj,
    step_weight,
    inner_kernel,
    state_kernel,
    step_bias,
    decay_rate,
    skip_scale,
    norm_gain,
    scan_cache,
    window_cache,
    state_history,
    hit_owner,
    hit_slot,
):
    owners = lax.axis_size("dp")
    groups = lax.axis_size("mp")
    requests, heads = hit_owner.shape
    slots, _, p, n = scan_cache.shape
    width = inner_weight.shape[1]
    blocks = slots * heads

    wanted, pos = prep(hit_owner, hit_slot, owners)
    codes = lax.all_to_all(wanted, "dp", split_axis=0, concat_axis=0, tiled=True)
    sent = pick(codes, scan_cache.reshape(blocks, p, n), window_cache.reshape(blocks, -1))
    back = lax.all_to_all(sent, "dp", split_axis=0, concat_axis=0, tiled=True)

    inner, gate, state, step = project(activations, inner_weight, gate_weight, state_proj, step_weight)
    az, ez, c, f1, small, first = ssd(
        inner,
        gate,
        state,
        step,
        state_history,
        inner_kernel,
        state_kernel,
        step_bias[None],
        decay_rate[None],
        jnp.repeat(skip_scale, p)[None],
    )
    g, square, grow, held = tail(pos, back, az, ez, c, small, first)
    final = finals(held, grow, small, f1)
    pair = [(i, i ^ 1) for i in range(groups)]
    square = square + lax.ppermute(square, "mp", pair)
    parts = [square] + [
        lax.ppermute(square, "mp", [(i, (i + 2 * s) % groups) for i in range(groups)])
        for s in range(1, groups // 2)
    ]
    normed = normalise(g, parts, norm_gain[None], width * groups)
    return normed, final


def solution(mesh):
    placed = (
        P("dp", None),
        P(None, "mp"),
        P(None, "mp"),
        P(),
        P(None, "mp"),
        P(None, "mp"),
        P(),
        P("mp"),
        P("mp"),
        P("mp"),
        P("mp"),
        P("dp", "mp", None, None),
        P("dp", "mp", None),
        P("dp", None, None),
        P("dp", "mp"),
        P("dp", "mp"),
    )
    return jax.shard_map(
        local,
        mesh=mesh,
        in_specs=placed,
        out_specs=(P("dp", "mp"), P("dp", "mp", None, None)),
        check_vma=False,
    )
```

```python
import functools

import jax
import jax.numpy as jnp
from jax import lax
from jax.experimental import pallas as pl
from jax.experimental.pallas import tpu as pltpu
from jax.sharding import PartitionSpec as P

EPSILON = 1e-05
CAP = 8
F32 = jnp.float32
BF16 = jnp.bfloat16
MIB = 1024 * 1024


def silu(v):
    half = 0.5 * v
    return half + half * jnp.tanh(half)


def full(shape, **kw):
    return pl.BlockSpec(shape, lambda *_: (0,) * len(shape), **kw)


def in_hbm(*arrays):
    return [pltpu.with_memory_space_constraint(v, pltpu.HBM) for v in arrays]


def in_vmem(*arrays):
    return [pltpu.with_memory_space_constraint(v, pltpu.VMEM) for v in arrays]


def prep_kernel(
    owner_ref, slot_ref, cache_hbm, window_ref, wanted_ref, pos_ref, cache_ref, wa_ref, wb_ref, count_ref, sem
):
    owners = wanted_ref.shape[0]
    requests, heads = owner_ref.shape
    copy = pltpu.make_async_copy(cache_hbm, cache_ref, sem)
    copy.start()
    half = window_ref.shape[1] // 3
    w = window_ref[...].astype(F32)
    first = w[:, : 2 * half]
    second = jnp.concatenate([w[:, 2 * half :], jnp.zeros((w.shape[0], half), F32)], axis=1)
    odd = lax.broadcasted_iota(jnp.int32, first.shape, 0) % 2 == 1
    wa_ref[...] = jnp.where(odd, pltpu.roll(first, half, 1), first)
    wb_ref[...] = jnp.where(odd, pltpu.roll(second, half, 1), second)
    for o in range(owners):
        count_ref[o] = 0
        for k in range(CAP):
            wanted_ref[o, 0, k] = 0
    for r in range(requests):
        for h in range(heads):
            o = owner_ref[r, h]
            k = count_ref[o]
            count_ref[o] = k + 1
            wanted_ref[o, 0, k] = slot_ref[r, h] * heads + h
            pos_ref[r * heads + h] = o * CAP + k
    copy.wait()


def prep(hit_owner, hit_slot, cache, window, owners):
    entries = hit_owner.size
    smem = pl.BlockSpec(memory_space=pltpu.SMEM)
    vmem = pl.BlockSpec(memory_space=pltpu.VMEM)
    blocks, p, n = cache.shape
    return pl.pallas_call(
        prep_kernel,
        out_shape=(
            jax.ShapeDtypeStruct((owners, 1, 128), jnp.int32),
            jax.ShapeDtypeStruct((entries,), jnp.int32),
            pltpu.VMEM((blocks, p, n), F32),
            pltpu.VMEM((blocks, n), F32),
            pltpu.VMEM((blocks, n), F32),
        ),
        in_specs=[smem, smem, pl.BlockSpec(memory_space=pltpu.HBM), vmem],
        out_specs=(smem, smem, vmem, vmem, vmem),
        scratch_shapes=[pltpu.SMEM((owners,), jnp.int32), pltpu.SemaphoreType.DMA],
        compiler_params=pltpu.CompilerParams(vmem_limit_bytes=8 * MIB),
        name="prep",
    )(*in_hbm(hit_owner, hit_slot, cache, window))


def pick_kernel(codes_ref, cache_ref, wa_ref, wb_ref, out_ref, rows_ref, sem):
    owners = out_ref.shape[0]
    p = cache_ref.shape[1]
    cached = CAP * p

    @pl.loop(0, owners)
    def _(d):
        for k in range(CAP):
            pltpu.make_async_copy(
                cache_ref.at[codes_ref[d, 0, k]], out_ref.at[d, k * p : k * p + p], sem
            ).start()

    @pl.loop(0, owners)
    def _(d):
        for k in range(CAP):
            at = pl.ds(codes_ref[d, 0, k], 1)
            rows_ref[d, 2 * k : 2 * k + 1] = wa_ref[at]
            rows_ref[d, 2 * k + 1 : 2 * k + 2] = wb_ref[at]

    pltpu.make_async_copy(rows_ref, out_ref.at[:, cached:], sem).start()
    pltpu.make_async_copy(out_ref, out_ref, sem).wait()


def pick(codes, cache, wa, wb):
    owners = codes.shape[0]
    blocks, p, n = cache.shape
    vmem = pl.BlockSpec(memory_space=pltpu.VMEM)
    hbm = pl.BlockSpec(memory_space=pltpu.HBM)
    return pl.pallas_call(
        pick_kernel,
        out_shape=pltpu.HBM((owners, CAP * p + 2 * CAP, n), F32),
        in_specs=[pl.BlockSpec(memory_space=pltpu.SMEM), vmem, vmem, vmem],
        out_specs=hbm,
        scratch_shapes=[pltpu.VMEM((owners, 2 * CAP, n), F32), pltpu.SemaphoreType.DMA],
        compiler_params=pltpu.CompilerParams(vmem_limit_bytes=8 * MIB),
        cost_estimate=pl.CostEstimate(flops=0, bytes_accessed=8 * MIB, transcendentals=0),
        name="pick",
    )(codes, *in_vmem(cache, wa, wb))


TILE = 256


def project_kernel(steps, act_ref, wi_ref, wg_ref, ws_ref, wd_ref, inner_ref, gate_ref, state_ref, step_ref):
    j = pl.program_id(0)
    rows = act_ref.shape[0]
    chunk = 1024

    def run(w_ref, out_ref):
        @pl.loop(0, rows // chunk)
        def _(m):
            at = pl.ds(pl.multiple_of(m * chunk, chunk), chunk)
            out_ref[at, :] = jnp.dot(act_ref[at, :], w_ref[...], preferred_element_type=F32).astype(out_ref.dtype)

    @pl.when(j == 0)
    def _():
        run(ws_ref, state_ref)
        run(wd_ref, step_ref)

    @pl.when((j > 0) & (j <= steps))
    def _():
        run(wi_ref, inner_ref)

    @pl.when(j > steps)
    def _():
        run(wg_ref, gate_ref)


def project(act, wi, wg, ws, wd):
    rows, depth = act.shape
    width = wi.shape[1]
    steps = width // TILE

    def at_inner(j):
        return (0, jnp.clip(j - 1, 0, steps - 1))

    def at_gate(j):
        return (0, jnp.clip(j - 1 - steps, 0, steps - 1))

    flops = 2 * rows * depth * (2 * width + ws.shape[1] + wd.shape[1])
    return pl.pallas_call(
        functools.partial(project_kernel, steps),
        out_shape=(
            jax.ShapeDtypeStruct((rows, width), BF16),
            jax.ShapeDtypeStruct((rows, width), BF16),
            jax.ShapeDtypeStruct((rows, ws.shape[1]), BF16),
            jax.ShapeDtypeStruct((rows, wd.shape[1]), F32),
        ),
        grid=(1 + 2 * steps,),
        in_specs=[
            full((rows, depth), pipeline_mode=pl.Buffered(1)),
            pl.BlockSpec((depth, TILE), at_inner),
            pl.BlockSpec((depth, TILE), at_gate),
            full(ws.shape, pipeline_mode=pl.Buffered(1)),
            full(wd.shape, pipeline_mode=pl.Buffered(1)),
        ],
        out_specs=(
            pl.BlockSpec((rows, TILE), at_inner),
            pl.BlockSpec((rows, TILE), at_gate),
            full((rows, ws.shape[1])),
            full((rows, wd.shape[1])),
        ),
        compiler_params=pltpu.CompilerParams(vmem_limit_bytes=60 * MIB),
        cost_estimate=pl.CostEstimate(flops=flops, bytes_accessed=32 * MIB, transcendentals=0),
        name="project",
    )(act, wi, wg, ws, wd)


def ssd_kernel(
    inner_ref,
    gate_ref,
    state_ref,
    step_ref,
    hist_ref,
    ik_ref,
    sk_ref,
    bias_ref,
    decay_ref,
    skip_ref,
    az_ref,
    ez_ref,
    c_ref,
    f1_ref,
    small_ref,
    first_ref,
    u_ref,
    v_ref,
):
    seq, width = inner_ref.shape
    heads = step_ref.shape[1]
    p = width // heads
    taps = ik_ref.shape[0]
    lag = taps - 1
    n = state_ref.shape[1] // 2
    lead = 8 - lag
    half = seq // 2

    v_ref[lead:8, :] = hist_ref[0].astype(F32)
    v_ref[8:, :] = state_ref[...].astype(F32)
    sk = sk_ref[...].astype(F32)
    run = jnp.zeros((seq, 2 * n), F32)
    for k in range(taps):
        run = run + sk[k : k + 1] * v_ref[lead + k : lead + k + seq, :]
    conv = silu(run).astype(BF16)
    b = conv[:, :n]
    c = conv[:, n:]
    c_ref[:, :n] = c
    small_ref[0, 2 * heads :] = b[:16].astype(F32)[:8]

    raw = step_ref[...] + bias_ref[...]
    dt = jnp.maximum(raw, 0.0) + jnp.log1p(jnp.exp(-jnp.abs(raw)))
    dt = jnp.concatenate([dt, jnp.zeros((seq, 128 - heads), F32)], axis=1)
    decay = jnp.concatenate([decay_ref[...], jnp.zeros((1, 128 - heads), F32)], axis=1)
    t_at = lax.broadcasted_iota(jnp.int32, (seq, seq), 0)
    s_at = lax.broadcasted_iota(jnp.int32, (seq, seq), 1)
    causal = s_at <= t_at
    cum = jnp.dot(
        causal.astype(F32), -decay * dt, preferred_element_type=F32, precision=lax.Precision.HIGHEST
    )
    cum_t = cum.T
    dt_t = dt.T
    begin = cum[lag - 1 : lag]
    last = cum[seq - 1 : seq]
    spread = (
        lax.broadcasted_iota(jnp.int32, (128, width), 1) // p
        == lax.broadcasted_iota(jnp.int32, (128, width), 0)
    )
    spread = spread.astype(F32).astype(BF16)
    early = lax.broadcasted_iota(jnp.int32, (seq, 128), 0) < lag
    grown = jnp.exp(jnp.where(early, cum, jnp.minimum(cum - begin, 0.0))).astype(BF16)
    tail = jnp.exp(jnp.minimum(last - cum, 0.0)) * dt
    begin_t = cum_t[:heads, lag - 1 : lag]
    last_t = cum_t[:heads, seq - 1 : seq]
    small_ref[0, :heads] = jnp.broadcast_to(jnp.exp(jnp.minimum(last_t - begin_t, 0.0)), (heads, n))
    small_ref[0, heads : 2 * heads] = jnp.broadcast_to(jnp.exp(begin_t), (heads, n))

    scores = lax.dot_general(c, b, (((1,), (1,)), ((), ())), preferred_element_type=F32)
    scores = jnp.where(causal, scores, 0.0)
    own = scores[:, :n]
    seen = (lax.broadcasted_iota(jnp.int32, own.shape, 1) < lag) & (
        lax.broadcasted_iota(jnp.int32, own.shape, 0) >= lag
    )
    c_ref[:, n:] = pltpu.roll(jnp.where(seen, own, 0.0), 8 * pl.program_id(0), 1).astype(BF16)
    top = scores[:half, :half]
    bottom = scores[half:]

    row8 = lax.broadcasted_iota(jnp.int32, (8, 128), 0)
    cum8 = cum[:8]
    dt8 = dt[:8]
    small = [jnp.where(row8 < lag, jnp.exp(jnp.minimum(begin - cum8, 0.0)) * dt8, 0.0).astype(BF16)]
    for j in range(lag):
        rows = []
        for t in range(8):
            if j <= t < lag:
                s = t - j
                gap = jnp.exp(jnp.minimum(cum[t : t + 1] - cum[s : s + 1], 0.0))
                rows.append(gap * scores[t : t + 1, s : s + 1] * dt[s : s + 1])
            else:
                rows.append(jnp.zeros((1, 128), F32))
        small.append(jnp.concatenate(rows, axis=0).astype(BF16))
    small = jnp.concatenate([m.astype(F32) for m in small], axis=0).astype(BF16)

    u_ref[:8, :] = jnp.zeros((8, width), F32)
    u_ref[8:, :] = inner_ref[...].astype(F32)
    lane = lax.broadcasted_iota(jnp.int32, (1, 128), 1)
    for q in range(width // 128):
        cols = slice(q * 128, q * 128 + 128)
        ik = ik_ref[:, cols].astype(F32)
        run = jnp.zeros((seq, 128), F32)
        for k in range(taps):
            run = run + ik[k : k + 1] * u_ref[lead + k : lead + k + seq, cols]
        x = jnp.where(early, 0.0, silu(run)).astype(BF16)
        xf = x.astype(F32)
        y_top = jnp.zeros((half, 128), F32)
        y_bottom = jnp.zeros((seq - half, 128), F32)
        for s in range(128 // p):
            h = q * (128 // p) + s
            own = (lane >= s * p) & (lane < (s + 1) * p)
            xs = jnp.where(own, xf, 0.0).astype(BF16)
            col = cum[:, h : h + 1]
            row = cum_t[h : h + 1]
            dr = dt_t[h : h + 1]
            w_top = jnp.exp(jnp.minimum(col[:half] - row[:, :half], 0.0)) * (top * dr[:, :half])
            w_bottom = jnp.exp(jnp.minimum(col[half:] - row, 0.0)) * (bottom * dr)
            y_top = y_top + jnp.dot(w_top.astype(BF16), xs[:half], preferred_element_type=F32)
            y_bottom = y_bottom + jnp.dot(w_bottom.astype(BF16), xs, preferred_element_type=F32)
        skip = skip_ref[:, cols]
        y = jnp.concatenate([y_top, y_bottom], axis=0) + skip * xf
        z = silu(gate_ref[:, cols].astype(F32))
        az_ref[:, cols] = (y * z).astype(BF16)
        ez = jnp.dot(grown, spread[:, cols], preferred_element_type=F32) * z
        ez_ref[:, cols] = ez.astype(BF16)
        tw = jnp.dot(tail.astype(BF16), spread[:, cols], preferred_element_type=F32)
        xt = (xf * tw).astype(BF16)
        f1_ref[0, cols, :] = lax.dot_general(
            xt, b, (((0,), (0,)), ((), ())), preferred_element_type=F32
        )
        wide = jnp.dot(small, spread[:, cols], preferred_element_type=F32)
        first_ref[0, 0:8, cols] = run[:8]
        first_ref[0, 16 + 8 * lag : 16 + 8 * lag + taps, cols] = ik
        first_ref[0, 8:16, cols] = wide[:8]
        z8 = z[:8]
        first_ref[0, 16:24, cols] = jnp.where(row8 < lag, (wide[8:16] + skip) * z8, 0.0)
        for j in range(1, lag):
            first_ref[0, 16 + 8 * j : 24 + 8 * j, cols] = wide[8 + 8 * j : 16 + 8 * j] * z8


def ssd(inner, gate, state, step, history, ik, sk, bias, decay, skip):
    tokens, width = inner.shape
    requests = history.shape[0]
    seq = tokens // requests
    heads = step.shape[1]
    n2 = state.shape[1]
    n = n2 // 2
    lag = ik.shape[0] - 1
    rows = lambda w: pl.BlockSpec((seq, w), lambda r: (r, 0))
    per = lambda *s: pl.BlockSpec((1,) + s, lambda r: (r,) + (0,) * len(s))
    return pl.pallas_call(
        ssd_kernel,
        out_shape=(
            pltpu.VMEM((tokens, width), BF16),
            pltpu.HBM((tokens, width), BF16),
            pltpu.VMEM((tokens, 2 * n), BF16),
            pltpu.HBM((requests, width, n), F32),
            pltpu.VMEM((requests, 2 * heads + 8, n), F32),
            pltpu.VMEM((requests, 24 + 8 * lag, width), F32),
        ),
        grid=(requests,),
        in_specs=[
            rows(width),
            rows(width),
            rows(n2),
            rows(heads),
            per(*history.shape[1:]),
            full(ik.shape),
            full(sk.shape),
            full(bias.shape),
            full(decay.shape),
            full(skip.shape),
        ],
        out_specs=(
            rows(width),
            rows(width),
            rows(2 * n),
            per(width, n),
            per(2 * heads + 8, n),
            per(24 + 8 * lag, width),
        ),
        scratch_shapes=[pltpu.VMEM((seq + 8, width), F32), pltpu.VMEM((seq + 8, n2), F32)],
        compiler_params=pltpu.CompilerParams(vmem_limit_bytes=40 * MIB),
        cost_estimate=pl.CostEstimate(
            flops=2 * tokens * width * seq * 2, bytes_accessed=14 * MIB, transcendentals=tokens * seq * heads
        ),
        name="ssd",
    )(*in_hbm(inner, gate, state, step), history, ik, sk, bias, decay, skip)


def first_sources(grow_ref, small_ref, r):
    requests = small_ref.shape[0]
    b = small_ref[r, small_ref.shape[1] - 8 :]
    zero = jnp.zeros_like(b)
    b = jnp.concatenate([b if i == r else zero for i in range(requests)], axis=0).astype(BF16)
    return jnp.dot(grow_ref[...], b, preferred_element_type=F32)


def tail_kernel(
    pos_ref,
    back_ref,
    ez_hbm,
    f1_hbm,
    az_ref,
    c_ref,
    small_ref,
    first_ref,
    g_ref,
    sq_ref,
    grow_ref,
    held_ref,
    f1_ref,
    ez_ref,
    rows_ref,
    s_ref,
    raw_ref,
    win_ref,
    mix_ref,
    x_ref,
    extra_ref,
    sem,
    ez_sem,
    once_sem,
):
    requests = first_ref.shape[0]
    heads = (small_ref.shape[1] - 8) // 2
    p = held_ref.shape[1]
    tokens, width = g_ref.shape
    seq = tokens // requests
    lag = (first_ref.shape[1] - 24) // 8
    pairs = heads // 2

    def rows_of(r):
        return slice(r * seq, r * seq + seq)

    def ez_copy(r):
        return pltpu.make_async_copy(ez_hbm.at[rows_of(r)], ez_ref.at[rows_of(r)], ez_sem.at[r])

    def fetch(r):
        for h in range(heads):
            e = r * heads + h
            at = pos_ref[e]
            pltpu.make_async_copy(
                back_ref.at[at // CAP, pl.ds(pl.multiple_of((at % CAP) * p, p), p)],
                held_ref.at[e],
                sem.at[r],
            ).start()
        ez_copy(r).start()

    row_copy = pltpu.make_async_copy(back_ref.at[:, CAP * p :], rows_ref, once_sem.at[0])
    f1_copy = pltpu.make_async_copy(f1_hbm, f1_ref, once_sem.at[1])
    row_copy.start()
    fetch(0)
    fetch(1)
    win_ref[...] = jnp.zeros_like(win_ref)
    x_ref[...] = jnp.zeros_like(x_ref)
    row_copy.wait()

    low = lax.broadcasted_iota(jnp.int32, (1, 128), 1) < p
    flat = rows_ref.reshape(rows_ref.shape[0] * rows_ref.shape[1], 128)
    for i in range(requests):
        for q in range(pairs):
            cols = slice(q * 128, q * 128 + 128)
            even = 2 * pos_ref[i * heads + 2 * q]
            odd = 2 * pos_ref[i * heads + 2 * q + 1]
            a0, a1 = flat[pl.ds(even, 1)], flat[pl.ds(odd, 1)]
            b0, b1 = flat[pl.ds(even + 1, 1)], flat[pl.ds(odd + 1, 1)]
            win_ref[i, 0:1, cols] = jnp.where(low, a0, a1)
            win_ref[i, 2:3, cols] = jnp.where(low, b0, b1)
            mix_ref[i * pairs + q : i * pairs + q + 1] = jnp.where(low, a1, a0)
    mix = pltpu.roll(mix_ref[...], p, 1)
    for i in range(requests):
        for q in range(pairs):
            win_ref[i, 1:2, q * 128 : q * 128 + 128] = mix[i * pairs + q : i * pairs + q + 1]

    run = first_ref[:, 0:8]
    for k in range(lag):
        at = 16 + 8 * lag + k
        run = run + first_ref[:, at : at + 1] * win_ref[:, k : k + 8]
    row8 = lax.broadcasted_iota(jnp.int32, run.shape, 1)
    x = jnp.where(row8 < lag, silu(run), 0.0).astype(BF16).astype(F32)
    x_ref[:, 8:16] = x
    extra = first_ref[:, 16:24] * x
    for j in range(1, lag):
        extra = extra + first_ref[:, 16 + 8 * j : 24 + 8 * j] * x_ref[:, 8 - j : 16 - j]
    extra_ref[...] = extra
    grow = (x * first_ref[:, 8:16]).reshape(requests * 8, width).T
    grow_ref[...] = grow.astype(BF16)
    n = c_ref.shape[1] // 2
    grow = jnp.concatenate([grow, jnp.zeros((width, n - requests * 8), F32)], axis=1).astype(BF16)
    s_ref[0, :, n:] = grow
    s_ref[1, :, n:] = grow

    for r in range(2, requests):
        fetch(r)
    f1_copy.start()

    row16 = lax.broadcasted_iota(jnp.int32, (16, 256), 0)
    nt = (((1,), (1,)), ((), ()))
    squares = []
    for r in range(requests):
        rows = rows_of(r)
        part = held_ref.at[r * heads : r * heads + heads]
        pltpu.make_async_copy(part, part, sem.at[r]).wait()
        for h in range(heads):
            at = slice(h * p, h * p + p)
            block = held_ref[r * heads + h]
            raw_ref[r % 2, at] = block.astype(BF16)
            s_ref[r % 2, at, :n] = (small_ref[r, heads + h : heads + h + 1] * block).astype(BF16)
        ez_copy(r).wait()
        c = c_ref[rows]
        total = jnp.zeros((seq - 16, 128), F32)
        total16 = jnp.zeros((16, 128), F32)
        for q in range(width // 256):
            cols = slice(q * 256, q * 256 + 256)
            seen = lax.dot_general(c, s_ref[r % 2, cols], nt, preferred_element_type=F32)
            seen16 = lax.dot_general(c[:16, :n], raw_ref[r % 2, cols], nt, preferred_element_type=F32)
            seen16 = jnp.where(row16 < lag, seen16, seen[:16])
            az = az_ref[rows, cols].astype(F32)
            ez = ez_ref[rows, cols].astype(F32)
            g = az[16:] + ez[16:] * seen[16:]
            g16 = az[:16] + ez[:16] * seen16
            g16 = g16 + jnp.concatenate([extra_ref[r, :, cols], jnp.zeros((8, 256), F32)], axis=0)
            g_ref[r * seq : r * seq + 16, cols] = g16.astype(BF16)
            g_ref[r * seq + 16 : r * seq + seq, cols] = g.astype(BF16)
            g = g * g
            g16 = g16 * g16
            total = total + g[:, :128] + g[:, 128:]
            total16 = total16 + g16[:, :128] + g16[:, 128:]
        total = jnp.concatenate([total16, total], axis=0)
        squares.append(jnp.sum(total.T, axis=0, keepdims=True))
    squares.append(jnp.zeros((8 - requests, seq), F32))
    sq_ref[...] = jnp.concatenate(squares, axis=0)
    f1_copy.wait()


def tail(pos, back, ez, f1, az, c, small, first):
    requests, packed, n = small.shape
    heads = (packed - 8) // 2
    assert requests * 8 <= n
    tokens, width = az.shape
    p = width // heads
    seq = tokens // requests
    owners = back.shape[0]
    vmem = pl.BlockSpec(memory_space=pltpu.VMEM)
    hbm = pl.BlockSpec(memory_space=pltpu.HBM)
    return pl.pallas_call(
        tail_kernel,
        out_shape=(
            pltpu.VMEM((tokens, width), BF16),
            pltpu.VMEM((8, seq), F32),
            pltpu.VMEM((width, requests * 8), BF16),
            pltpu.VMEM((requests * heads, p, n), F32),
            pltpu.VMEM(f1.shape, F32),
        ),
        in_specs=[pl.BlockSpec(memory_space=pltpu.SMEM)] + [hbm] * 3 + [vmem] * 4,
        out_specs=(vmem,) * 5,
        scratch_shapes=[
            pltpu.VMEM((tokens, width), BF16),
            pltpu.VMEM((owners, 2 * CAP, n), F32),
            pltpu.VMEM((2, width, 2 * n), BF16),
            pltpu.VMEM((2, width, n), BF16),
            pltpu.VMEM((requests, 16, width), F32),
            pltpu.VMEM((requests * heads // 2, 128), F32),
            pltpu.VMEM((requests, 16, width), F32),
            pltpu.VMEM((requests, 8, width), F32),
            pltpu.SemaphoreType.DMA((requests,)),
            pltpu.SemaphoreType.DMA((requests,)),
            pltpu.SemaphoreType.DMA((2,)),
        ],
        compiler_params=pltpu.CompilerParams(vmem_limit_bytes=24 * MIB),
        cost_estimate=pl.CostEstimate(
            flops=2 * tokens * width * n, bytes_accessed=10 * MIB, transcendentals=0
        ),
        name="tail",
    )(pos, *in_hbm(back, ez, f1), *in_vmem(az, c, small, first))


def final_kernel(held_ref, grow_ref, small_ref, f1_ref, out_ref, made_ref, sem):
    requests, heads, p = out_ref.shape[:3]

    def copy(r):
        return pltpu.make_async_copy(made_ref.at[r], out_ref.at[r], sem.at[r])

    for r in range(requests):
        add = first_sources(grow_ref, small_ref, r)
        for h in range(heads):
            at = slice(h * p, h * p + p)
            block = small_ref[r, heads + h : heads + h + 1] * held_ref[r * heads + h] + add[at]
            made_ref[r, h] = small_ref[r, h : h + 1] * block + f1_ref[r, at]
        copy(r).start()
    for r in range(requests):
        copy(r).wait()


def finals(held, grow, small, f1):
    requests, width, n = f1.shape
    heads = (small.shape[1] - 8) // 2
    p = width // heads
    vmem = pl.BlockSpec(memory_space=pltpu.VMEM)
    return pl.pallas_call(
        final_kernel,
        out_shape=jax.ShapeDtypeStruct((requests, heads, p, n), F32),
        in_specs=[vmem] * 4,
        out_specs=pl.BlockSpec(memory_space=pltpu.HBM),
        scratch_shapes=[
            pltpu.VMEM((requests, heads, p, n), F32),
            pltpu.SemaphoreType.DMA((requests,)),
        ],
        compiler_params=pltpu.CompilerParams(vmem_limit_bytes=16 * MIB),
        cost_estimate=pl.CostEstimate(
            flops=2 * requests * width * n * 32, bytes_accessed=6 * MIB, transcendentals=0
        ),
        name="finals",
    )(*in_vmem(held, grow, small, f1))


def norm_kernel(channels, g_ref, s0_ref, s1_ref, s2_ref, s3_ref, gain_ref, out_ref, made_ref, sem):
    tokens, width = g_ref.shape
    seq = s0_ref.shape[1]
    step = 128
    gain = gain_ref[...].astype(F32)
    square = s0_ref[...] + s1_ref[...] + s2_ref[...] + s3_ref[...]
    scale = lax.rsqrt(square / channels + EPSILON)

    def copy(i):
        rows = slice(i * step, i * step + step)
        return pltpu.make_async_copy(made_ref.at[rows], out_ref.at[rows], sem.at[i])

    for i in range(tokens // step):
        rows = slice(i * step, i * step + step)
        r, at = i * step // seq, i * step % seq
        wide = jnp.broadcast_to(scale[r : r + 1, at : at + step], (128, step)).T
        for q in range(width // 128):
            cols = slice(q * 128, q * 128 + 128)
            made_ref[rows, cols] = (g_ref[rows, cols].astype(F32) * wide * gain[:, cols]).astype(BF16)
        copy(i).start()
    for i in range(tokens // step):
        copy(i).wait()


def normalise(g, parts, gain, channels):
    tokens, width = g.shape
    vmem = pl.BlockSpec(memory_space=pltpu.VMEM)
    return pl.pallas_call(
        functools.partial(norm_kernel, channels),
        out_shape=jax.ShapeDtypeStruct((tokens, width), BF16),
        in_specs=[vmem] * 6,
        out_specs=pl.BlockSpec(memory_space=pltpu.HBM),
        scratch_shapes=[pltpu.VMEM((tokens, width), BF16), pltpu.SemaphoreType.DMA((tokens // 128,))],
        compiler_params=pltpu.CompilerParams(vmem_limit_bytes=8 * MIB),
        cost_estimate=pl.CostEstimate(flops=2 * tokens * width, bytes_accessed=4 * MIB, transcendentals=0),
        name="normalise",
    )(g, *parts, gain)


def local(
    activations,
    gate_weight,
    inner_weight,
    state_proj,
    step_weight,
    inner_kernel,
    state_kernel,
    step_bias,
    decay_rate,
    skip_scale,
    norm_gain,
    scan_cache,
    window_cache,
    state_history,
    hit_owner,
    hit_slot,
):
    owners = lax.axis_size("dp")
    groups = lax.axis_size("mp")
    requests, heads = hit_owner.shape
    slots, _, p, n = scan_cache.shape
    width = inner_weight.shape[1]
    blocks = slots * heads

    cache = scan_cache.reshape(blocks, p, n)
    wanted, pos, cache, wa, wb = prep(hit_owner, hit_slot, cache, window_cache.reshape(blocks, -1), owners)
    codes = lax.all_to_all(wanted, "dp", split_axis=0, concat_axis=0, tiled=True)
    sent = pick(codes, cache, wa, wb)
    back = lax.all_to_all(sent, "dp", split_axis=0, concat_axis=0, tiled=True)

    inner, gate, state, step = project(activations, inner_weight, gate_weight, state_proj, step_weight)
    az, ez, c, f1, small, first = ssd(
        inner,
        gate,
        state,
        step,
        state_history,
        inner_kernel,
        state_kernel,
        step_bias[None],
        decay_rate[None],
        jnp.repeat(skip_scale, p)[None],
    )
    g, square, grow, held, f1 = tail(pos, back, ez, f1, az, c, small, first)
    final = finals(held, grow, small, f1)
    pair = [(i, i ^ 1) for i in range(groups)]
    square = square + lax.ppermute(square, "mp", pair)
    parts = [square] + [
        lax.ppermute(square, "mp", [(i, (i + 2 * s) % groups) for i in range(groups)])
        for s in range(1, groups // 2)
    ]
    normed = normalise(g, parts, norm_gain[None], width * groups)
    return normed, final


def solution(mesh):
    placed = (
        P("dp", None),
        P(None, "mp"),
        P(None, "mp"),
        P(),
        P(None, "mp"),
        P(None, "mp"),
        P(),
        P("mp"),
        P("mp"),
        P("mp"),
        P("mp"),
        P("dp", "mp", None, None),
        P("dp", "mp", None),
        P("dp", None, None),
        P("dp", "mp"),
        P("dp", "mp"),
    )
    return jax.shard_map(
        local,
        mesh=mesh,
        in_specs=placed,
        out_specs=(P("dp", "mp"), P("dp", "mp", None, None)),
        check_vma=False,
    )
```

```python
import functools

import jax
import jax.numpy as jnp
from jax import lax
from jax.experimental import pallas as pl
from jax.experimental.pallas import tpu as pltpu
from jax.sharding import PartitionSpec as P

EPSILON = 1e-05
CAP = 8
F32 = jnp.float32
BF16 = jnp.bfloat16
MIB = 1024 * 1024


def silu(v):
    half = 0.5 * v
    return half + half * jnp.tanh(half)


def full(shape, **kw):
    return pl.BlockSpec(shape, lambda *_: (0,) * len(shape), **kw)


def in_hbm(*arrays):
    return [pltpu.with_memory_space_constraint(v, pltpu.HBM) for v in arrays]


def in_vmem(*arrays):
    return [pltpu.with_memory_space_constraint(v, pltpu.VMEM) for v in arrays]


def prep_kernel(
    owner_ref,
    slot_ref,
    cache_hbm,
    window_hbm,
    wanted_hbm,
    pos_hbm,
    cache_ref,
    wa_ref,
    wb_ref,
    wanted_ref,
    pos_ref,
    count_ref,
    window_ref,
    sem,
):
    owners = wanted_ref.shape[0]
    requests, heads = owner_ref.shape
    window_copy = pltpu.make_async_copy(window_hbm, window_ref, sem.at[0])
    window_copy.start()
    cache_copy = pltpu.make_async_copy(cache_hbm, cache_ref, sem.at[1])
    cache_copy.start()
    for o in range(owners):
        count_ref[o] = 0
        for k in range(CAP):
            wanted_ref[o, 0, k] = 0
    for r in range(requests):
        for h in range(heads):
            o = owner_ref[r, h]
            k = count_ref[o]
            count_ref[o] = k + 1
            wanted_ref[o, 0, k] = slot_ref[r, h] * heads + h
            pos_ref[r * heads + h] = o * CAP + k
    wanted_copy = pltpu.make_async_copy(wanted_ref, wanted_hbm, sem.at[2])
    wanted_copy.start()
    pos_copy = pltpu.make_async_copy(pos_ref, pos_hbm, sem.at[3])
    pos_copy.start()
    window_copy.wait()
    half = window_ref.shape[1] // 3
    w = window_ref[...].astype(F32)
    first = w[:, : 2 * half]
    second = jnp.concatenate([w[:, 2 * half :], jnp.zeros((w.shape[0], half), F32)], axis=1)
    odd = lax.broadcasted_iota(jnp.int32, first.shape, 0) % 2 == 1
    wa_ref[...] = jnp.where(odd, pltpu.roll(first, half, 1), first)
    wb_ref[...] = jnp.where(odd, pltpu.roll(second, half, 1), second)
    wanted_copy.wait()
    pos_copy.wait()
    cache_copy.wait()


def prep(hit_owner, hit_slot, cache, window, owners):
    entries = hit_owner.size
    smem = pl.BlockSpec(memory_space=pltpu.SMEM)
    vmem = pl.BlockSpec(memory_space=pltpu.VMEM)
    hbm = pl.BlockSpec(memory_space=pltpu.HBM)
    blocks, p, n = cache.shape
    return pl.pallas_call(
        prep_kernel,
        out_shape=(
            pltpu.HBM((owners, 1, 128), jnp.int32),
            pltpu.HBM((entries,), jnp.int32),
            pltpu.VMEM((blocks, p, n), F32),
            pltpu.VMEM((blocks, n), F32),
            pltpu.VMEM((blocks, n), F32),
        ),
        in_specs=[smem, smem, hbm, hbm],
        out_specs=(hbm, hbm, vmem, vmem, vmem),
        scratch_shapes=[
            pltpu.SMEM((owners, 1, 128), jnp.int32),
            pltpu.SMEM((entries,), jnp.int32),
            pltpu.SMEM((owners,), jnp.int32),
            pltpu.VMEM(window.shape, window.dtype),
            pltpu.SemaphoreType.DMA((4,)),
        ],
        compiler_params=pltpu.CompilerParams(vmem_limit_bytes=8 * MIB),
        name="prep",
    )(*in_hbm(hit_owner, hit_slot, cache, window))


def pick_kernel(codes_ref, cache_ref, wa_ref, wb_ref, out_ref, rows_ref, sem):
    owners = out_ref.shape[0]
    p = cache_ref.shape[1]
    cached = CAP * p

    @pl.loop(0, owners)
    def _(d):
        for k in range(CAP):
            pltpu.make_async_copy(
                cache_ref.at[codes_ref[d, 0, k]], out_ref.at[d, k * p : k * p + p], sem
            ).start()

    @pl.loop(0, owners)
    def _(d):
        for k in range(CAP):
            at = pl.ds(codes_ref[d, 0, k], 1)
            rows_ref[d, 2 * k : 2 * k + 1] = wa_ref[at]
            rows_ref[d, 2 * k + 1 : 2 * k + 2] = wb_ref[at]

    pltpu.make_async_copy(rows_ref, out_ref.at[:, cached:], sem).start()
    pltpu.make_async_copy(out_ref, out_ref, sem).wait()


def pick(codes, cache, wa, wb):
    owners = codes.shape[0]
    blocks, p, n = cache.shape
    vmem = pl.BlockSpec(memory_space=pltpu.VMEM)
    hbm = pl.BlockSpec(memory_space=pltpu.HBM)
    return pl.pallas_call(
        pick_kernel,
        out_shape=pltpu.HBM((owners, CAP * p + 2 * CAP, n), F32),
        in_specs=[pl.BlockSpec(memory_space=pltpu.SMEM), vmem, vmem, vmem],
        out_specs=hbm,
        scratch_shapes=[pltpu.VMEM((owners, 2 * CAP, n), F32), pltpu.SemaphoreType.DMA],
        compiler_params=pltpu.CompilerParams(vmem_limit_bytes=8 * MIB),
        cost_estimate=pl.CostEstimate(flops=0, bytes_accessed=8 * MIB, transcendentals=0),
        name="pick",
    )(codes, *in_vmem(cache, wa, wb))


TILE = 256


def project_kernel(steps, act_ref, wi_ref, wg_ref, ws_ref, wd_ref, inner_ref, gate_ref, state_ref, step_ref):
    j = pl.program_id(0)
    rows = act_ref.shape[0]
    chunk = 1024

    def run(w_ref, out_ref):
        @pl.loop(0, rows // chunk)
        def _(m):
            at = pl.ds(pl.multiple_of(m * chunk, chunk), chunk)
            out_ref[at, :] = jnp.dot(act_ref[at, :], w_ref[...], preferred_element_type=F32).astype(out_ref.dtype)

    @pl.when(j == 0)
    def _():
        run(ws_ref, state_ref)
        run(wd_ref, step_ref)

    @pl.when((j > 0) & (j <= steps))
    def _():
        run(wi_ref, inner_ref)

    @pl.when(j > steps)
    def _():
        run(wg_ref, gate_ref)


def project(act, wi, wg, ws, wd):
    rows, depth = act.shape
    width = wi.shape[1]
    steps = width // TILE

    def at_inner(j):
        return (0, jnp.clip(j - 1, 0, steps - 1))

    def at_gate(j):
        return (0, jnp.clip(j - 1 - steps, 0, steps - 1))

    flops = 2 * rows * depth * (2 * width + ws.shape[1] + wd.shape[1])
    return pl.pallas_call(
        functools.partial(project_kernel, steps),
        out_shape=(
            jax.ShapeDtypeStruct((rows, width), BF16),
            jax.ShapeDtypeStruct((rows, width), BF16),
            jax.ShapeDtypeStruct((rows, ws.shape[1]), BF16),
            jax.ShapeDtypeStruct((rows, wd.shape[1]), F32),
        ),
        grid=(1 + 2 * steps,),
        in_specs=[
            full((rows, depth), pipeline_mode=pl.Buffered(1)),
            pl.BlockSpec((depth, TILE), at_inner),
            pl.BlockSpec((depth, TILE), at_gate),
            full(ws.shape, pipeline_mode=pl.Buffered(1)),
            full(wd.shape, pipeline_mode=pl.Buffered(1)),
        ],
        out_specs=(
            pl.BlockSpec((rows, TILE), at_inner),
            pl.BlockSpec((rows, TILE), at_gate),
            full((rows, ws.shape[1])),
            full((rows, wd.shape[1])),
        ),
        compiler_params=pltpu.CompilerParams(vmem_limit_bytes=60 * MIB),
        cost_estimate=pl.CostEstimate(flops=flops, bytes_accessed=32 * MIB, transcendentals=0),
        name="project",
    )(act, wi, wg, ws, wd)


def ssd_kernel(
    inner_ref,
    gate_ref,
    state_ref,
    step_ref,
    hist_ref,
    ik_ref,
    sk_ref,
    bias_ref,
    decay_ref,
    skip_ref,
    az_ref,
    ez_ref,
    c_ref,
    f1_ref,
    small_ref,
    first_ref,
    u_ref,
    v_ref,
):
    seq, width = inner_ref.shape
    heads = step_ref.shape[1]
    p = width // heads
    taps = ik_ref.shape[0]
    lag = taps - 1
    n = state_ref.shape[1] // 2
    lead = 8 - lag
    half = seq // 2

    v_ref[lead:8, :] = hist_ref[0].astype(F32)
    v_ref[8:, :] = state_ref[...].astype(F32)
    sk = sk_ref[...].astype(F32)
    run = jnp.zeros((seq, 2 * n), F32)
    for k in range(taps):
        run = run + sk[k : k + 1] * v_ref[lead + k : lead + k + seq, :]
    conv = silu(run).astype(BF16)
    b = conv[:, :n]
    c = conv[:, n:]
    c_ref[:, :n] = c
    small_ref[0, 2 * heads :] = b[:16].astype(F32)[:8]

    raw = step_ref[...] + bias_ref[...]
    dt = jnp.maximum(raw, 0.0) + jnp.log1p(jnp.exp(-jnp.abs(raw)))
    dt = jnp.concatenate([dt, jnp.zeros((seq, 128 - heads), F32)], axis=1)
    decay = jnp.concatenate([decay_ref[...], jnp.zeros((1, 128 - heads), F32)], axis=1)
    t_at = lax.broadcasted_iota(jnp.int32, (seq, seq), 0)
    s_at = lax.broadcasted_iota(jnp.int32, (seq, seq), 1)
    causal = s_at <= t_at
    cum = jnp.dot(
        causal.astype(F32), -decay * dt, preferred_element_type=F32, precision=lax.Precision.HIGHEST
    )
    cum_t = cum.T
    dt_t = dt.T
    begin = cum[lag - 1 : lag]
    last = cum[seq - 1 : seq]
    spread = (
        lax.broadcasted_iota(jnp.int32, (128, width), 1) // p
        == lax.broadcasted_iota(jnp.int32, (128, width), 0)
    )
    spread = spread.astype(F32).astype(BF16)
    early = lax.broadcasted_iota(jnp.int32, (seq, 128), 0) < lag
    grown = jnp.exp(jnp.where(early, cum, jnp.minimum(cum - begin, 0.0))).astype(BF16)
    tail = jnp.exp(jnp.minimum(last - cum, 0.0)) * dt
    begin_t = cum_t[:heads, lag - 1 : lag]
    last_t = cum_t[:heads, seq - 1 : seq]
    small_ref[0, :heads] = jnp.broadcast_to(jnp.exp(jnp.minimum(last_t - begin_t, 0.0)), (heads, n))
    small_ref[0, heads : 2 * heads] = jnp.broadcast_to(jnp.exp(begin_t), (heads, n))

    scores = lax.dot_general(c, b, (((1,), (1,)), ((), ())), preferred_element_type=F32)
    scores = jnp.where(causal, scores, 0.0)
    own = scores[:, :n]
    seen = (lax.broadcasted_iota(jnp.int32, own.shape, 1) < lag) & (
        lax.broadcasted_iota(jnp.int32, own.shape, 0) >= lag
    )
    c_ref[:, n:] = pltpu.roll(jnp.where(seen, own, 0.0), 8 * pl.program_id(0), 1).astype(BF16)
    top = scores[:half, :half]
    bottom = scores[half:]

    row8 = lax.broadcasted_iota(jnp.int32, (8, 128), 0)
    cum8 = cum[:8]
    dt8 = dt[:8]
    small = [jnp.where(row8 < lag, jnp.exp(jnp.minimum(begin - cum8, 0.0)) * dt8, 0.0).astype(BF16)]
    for j in range(lag):
        rows = []
        for t in range(8):
            if j <= t < lag:
                s = t - j
                gap = jnp.exp(jnp.minimum(cum[t : t + 1] - cum[s : s + 1], 0.0))
                rows.append(gap * scores[t : t + 1, s : s + 1] * dt[s : s + 1])
            else:
                rows.append(jnp.zeros((1, 128), F32))
        small.append(jnp.concatenate(rows, axis=0).astype(BF16))
    small = jnp.concatenate([m.astype(F32) for m in small], axis=0).astype(BF16)

    u_ref[:8, :] = jnp.zeros((8, width), F32)
    u_ref[8:, :] = inner_ref[...].astype(F32)
    lane = lax.broadcasted_iota(jnp.int32, (1, 128), 1)
    for q in range(width // 128):
        cols = slice(q * 128, q * 128 + 128)
        ik = ik_ref[:, cols].astype(F32)
        run = jnp.zeros((seq, 128), F32)
        for k in range(taps):
            run = run + ik[k : k + 1] * u_ref[lead + k : lead + k + seq, cols]
        x = jnp.where(early, 0.0, silu(run)).astype(BF16)
        xf = x.astype(F32)
        y_top = jnp.zeros((half, 128), F32)
        y_bottom = jnp.zeros((seq - half, 128), F32)
        for s in range(128 // p):
            h = q * (128 // p) + s
            own = (lane >= s * p) & (lane < (s + 1) * p)
            xs = jnp.where(own, xf, 0.0).astype(BF16)
            col = cum[:, h : h + 1]
            row = cum_t[h : h + 1]
            dr = dt_t[h : h + 1]
            w_top = jnp.exp(jnp.minimum(col[:half] - row[:, :half], 0.0)) * (top * dr[:, :half])
            w_bottom = jnp.exp(jnp.minimum(col[half:] - row, 0.0)) * (bottom * dr)
            y_top = y_top + jnp.dot(w_top.astype(BF16), xs[:half], preferred_element_type=F32)
            y_bottom = y_bottom + jnp.dot(w_bottom.astype(BF16), xs, preferred_element_type=F32)
        skip = skip_ref[:, cols]
        y = jnp.concatenate([y_top, y_bottom], axis=0) + skip * xf
        z = silu(gate_ref[:, cols].astype(F32))
        az_ref[:, cols] = (y * z).astype(BF16)
        ez = jnp.dot(grown, spread[:, cols], preferred_element_type=F32) * z
        ez_ref[:, cols] = ez.astype(BF16)
        tw = jnp.dot(tail.astype(BF16), spread[:, cols], preferred_element_type=F32)
        xt = (xf * tw).astype(BF16)
        f1_ref[0, cols, :] = lax.dot_general(
            xt, b, (((0,), (0,)), ((), ())), preferred_element_type=F32
        )
        wide = jnp.dot(small, spread[:, cols], preferred_element_type=F32)
        first_ref[0, 0:8, cols] = run[:8]
        first_ref[0, 16 + 8 * lag : 16 + 8 * lag + taps, cols] = ik
        first_ref[0, 8:16, cols] = wide[:8]
        z8 = z[:8]
        first_ref[0, 16:24, cols] = jnp.where(row8 < lag, (wide[8:16] + skip) * z8, 0.0)
        for j in range(1, lag):
            first_ref[0, 16 + 8 * j : 24 + 8 * j, cols] = wide[8 + 8 * j : 16 + 8 * j] * z8


def ssd(inner, gate, state, step, history, ik, sk, bias, decay, skip):
    tokens, width = inner.shape
    requests = history.shape[0]
    seq = tokens // requests
    heads = step.shape[1]
    n2 = state.shape[1]
    n = n2 // 2
    lag = ik.shape[0] - 1
    rows = lambda w: pl.BlockSpec((seq, w), lambda r: (r, 0))
    per = lambda *s: pl.BlockSpec((1,) + s, lambda r: (r,) + (0,) * len(s))
    return pl.pallas_call(
        ssd_kernel,
        out_shape=(
            pltpu.VMEM((tokens, width), BF16),
            pltpu.HBM((tokens, width), BF16),
            pltpu.VMEM((tokens, 2 * n), BF16),
            pltpu.HBM((requests, width, n), F32),
            pltpu.VMEM((requests, 2 * heads + 8, n), F32),
            pltpu.VMEM((requests, 24 + 8 * lag, width), F32),
        ),
        grid=(requests,),
        in_specs=[
            rows(width),
            rows(width),
            rows(n2),
            rows(heads),
            per(*history.shape[1:]),
            full(ik.shape),
            full(sk.shape),
            full(bias.shape),
            full(decay.shape),
            full(skip.shape),
        ],
        out_specs=(
            rows(width),
            rows(width),
            rows(2 * n),
            per(width, n),
            per(2 * heads + 8, n),
            per(24 + 8 * lag, width),
        ),
        scratch_shapes=[pltpu.VMEM((seq + 8, width), F32), pltpu.VMEM((seq + 8, n2), F32)],
        compiler_params=pltpu.CompilerParams(vmem_limit_bytes=40 * MIB),
        cost_estimate=pl.CostEstimate(
            flops=2 * tokens * width * seq * 2, bytes_accessed=14 * MIB, transcendentals=tokens * seq * heads
        ),
        name="ssd",
    )(*in_hbm(inner, gate, state, step), history, ik, sk, bias, decay, skip)


def first_sources(grow_ref, small_ref, r):
    requests = small_ref.shape[0]
    b = small_ref[r, small_ref.shape[1] - 8 :]
    zero = jnp.zeros_like(b)
    b = jnp.concatenate([b if i == r else zero for i in range(requests)], axis=0).astype(BF16)
    return jnp.dot(grow_ref[...], b, preferred_element_type=F32)


def tail_kernel(
    pos_ref,
    back_ref,
    ez_hbm,
    f1_hbm,
    az_ref,
    c_ref,
    small_ref,
    first_ref,
    g_ref,
    sq_ref,
    grow_ref,
    held_ref,
    f1_ref,
    ez_ref,
    rows_ref,
    s_ref,
    raw_ref,
    win_ref,
    mix_ref,
    x_ref,
    extra_ref,
    sem,
    ez_sem,
    once_sem,
):
    requests = first_ref.shape[0]
    heads = (small_ref.shape[1] - 8) // 2
    p = held_ref.shape[1]
    tokens, width = g_ref.shape
    seq = tokens // requests
    lag = (first_ref.shape[1] - 24) // 8
    pairs = heads // 2

    def rows_of(r):
        return slice(r * seq, r * seq + seq)

    batch = requests // 2

    def ez_copy(i):
        rows = slice(i * batch * seq, (i + 1) * batch * seq)
        return pltpu.make_async_copy(ez_hbm.at[rows], ez_ref.at[rows], ez_sem.at[i])

    def fetch(i):
        ez_copy(i).start()
        for e in range(i * batch * heads, (i + 1) * batch * heads):
            at = pos_ref[e]
            pltpu.make_async_copy(
                back_ref.at[at // CAP, pl.ds(pl.multiple_of((at % CAP) * p, p), p)],
                held_ref.at[e],
                sem.at[i],
            ).start()

    row_copy = pltpu.make_async_copy(back_ref.at[:, CAP * p :], rows_ref, once_sem.at[0])
    f1_copy = pltpu.make_async_copy(f1_hbm, f1_ref, once_sem.at[1])
    row_copy.start()
    fetch(0)
    fetch(1)
    f1_copy.start()
    win_ref[...] = jnp.zeros_like(win_ref)
    x_ref[...] = jnp.zeros_like(x_ref)
    row_copy.wait()

    low = lax.broadcasted_iota(jnp.int32, (1, 128), 1) < p
    flat = rows_ref.reshape(rows_ref.shape[0] * rows_ref.shape[1], 128)
    for i in range(requests):
        for q in range(pairs):
            cols = slice(q * 128, q * 128 + 128)
            even = 2 * pos_ref[i * heads + 2 * q]
            odd = 2 * pos_ref[i * heads + 2 * q + 1]
            a0, a1 = flat[pl.ds(even, 1)], flat[pl.ds(odd, 1)]
            b0, b1 = flat[pl.ds(even + 1, 1)], flat[pl.ds(odd + 1, 1)]
            win_ref[i, 0:1, cols] = jnp.where(low, a0, a1)
            win_ref[i, 2:3, cols] = jnp.where(low, b0, b1)
            mix_ref[i * pairs + q : i * pairs + q + 1] = jnp.where(low, a1, a0)
    mix = pltpu.roll(mix_ref[...], p, 1)
    for i in range(requests):
        for q in range(pairs):
            win_ref[i, 1:2, q * 128 : q * 128 + 128] = mix[i * pairs + q : i * pairs + q + 1]

    run = first_ref[:, 0:8]
    for k in range(lag):
        at = 16 + 8 * lag + k
        run = run + first_ref[:, at : at + 1] * win_ref[:, k : k + 8]
    row8 = lax.broadcasted_iota(jnp.int32, run.shape, 1)
    x = jnp.where(row8 < lag, silu(run), 0.0).astype(BF16).astype(F32)
    x_ref[:, 8:16] = x
    extra = first_ref[:, 16:24] * x
    for j in range(1, lag):
        extra = extra + first_ref[:, 16 + 8 * j : 24 + 8 * j] * x_ref[:, 8 - j : 16 - j]
    extra_ref[...] = extra
    grow = (x * first_ref[:, 8:16]).reshape(requests * 8, width).T
    grow_ref[...] = grow.astype(BF16)
    n = c_ref.shape[1] // 2
    grow = jnp.concatenate([grow, jnp.zeros((width, n - requests * 8), F32)], axis=1).astype(BF16)
    s_ref[0, :, n:] = grow
    s_ref[1, :, n:] = grow

    row16 = lax.broadcasted_iota(jnp.int32, (16, 256), 0)
    nt = (((1,), (1,)), ((), ()))
    squares = []
    for r in range(requests):
        rows = rows_of(r)
        if r % batch == 0:
            part = held_ref.at[r * heads : (r + batch) * heads]
            pltpu.make_async_copy(part, part, sem.at[r // batch]).wait()
            ez_copy(r // batch).wait()
        for h in range(heads):
            at = slice(h * p, h * p + p)
            block = held_ref[r * heads + h]
            raw_ref[r % 2, at] = block.astype(BF16)
            s_ref[r % 2, at, :n] = (small_ref[r, heads + h : heads + h + 1] * block).astype(BF16)
        c = c_ref[rows]
        total = jnp.zeros((seq - 16, 128), F32)
        total16 = jnp.zeros((16, 128), F32)
        for q in range(width // 256):
            cols = slice(q * 256, q * 256 + 256)
            seen = lax.dot_general(c, s_ref[r % 2, cols], nt, preferred_element_type=F32)
            seen16 = lax.dot_general(c[:16, :n], raw_ref[r % 2, cols], nt, preferred_element_type=F32)
            seen16 = jnp.where(row16 < lag, seen16, seen[:16])
            az = az_ref[rows, cols].astype(F32)
            ez = ez_ref[rows, cols].astype(F32)
            g = az[16:] + ez[16:] * seen[16:]
            g16 = az[:16] + ez[:16] * seen16
            g16 = g16 + jnp.concatenate([extra_ref[r, :, cols], jnp.zeros((8, 256), F32)], axis=0)
            g_ref[r * seq : r * seq + 16, cols] = g16.astype(BF16)
            g_ref[r * seq + 16 : r * seq + seq, cols] = g.astype(BF16)
            g = g * g
            g16 = g16 * g16
            total = total + g[:, :128] + g[:, 128:]
            total16 = total16 + g16[:, :128] + g16[:, 128:]
        total = jnp.concatenate([total16, total], axis=0)
        squares.append(jnp.sum(total.T, axis=0, keepdims=True))
    squares.append(jnp.zeros((8 - requests, seq), F32))
    sq_ref[...] = jnp.concatenate(squares, axis=0)
    f1_copy.wait()


def tail(pos, back, ez, f1, az, c, small, first):
    requests, packed, n = small.shape
    heads = (packed - 8) // 2
    assert requests * 8 <= n
    tokens, width = az.shape
    p = width // heads
    seq = tokens // requests
    owners = back.shape[0]
    vmem = pl.BlockSpec(memory_space=pltpu.VMEM)
    hbm = pl.BlockSpec(memory_space=pltpu.HBM)
    return pl.pallas_call(
        tail_kernel,
        out_shape=(
            pltpu.VMEM((tokens, width), BF16),
            pltpu.VMEM((8, seq), F32),
            pltpu.VMEM((width, requests * 8), BF16),
            pltpu.VMEM((requests * heads, p, n), F32),
            pltpu.VMEM(f1.shape, F32),
        ),
        in_specs=[pl.BlockSpec(memory_space=pltpu.SMEM)] + [hbm] * 3 + [vmem] * 4,
        out_specs=(vmem,) * 5,
        scratch_shapes=[
            pltpu.VMEM((tokens, width), BF16),
            pltpu.VMEM((owners, 2 * CAP, n), F32),
            pltpu.VMEM((2, width, 2 * n), BF16),
            pltpu.VMEM((2, width, n), BF16),
            pltpu.VMEM((requests, 16, width), F32),
            pltpu.VMEM((requests * heads // 2, 128), F32),
            pltpu.VMEM((requests, 16, width), F32),
            pltpu.VMEM((requests, 8, width), F32),
            pltpu.SemaphoreType.DMA((2,)),
            pltpu.SemaphoreType.DMA((2,)),
            pltpu.SemaphoreType.DMA((2,)),
        ],
        compiler_params=pltpu.CompilerParams(vmem_limit_bytes=24 * MIB),
        cost_estimate=pl.CostEstimate(
            flops=2 * tokens * width * n, bytes_accessed=10 * MIB, transcendentals=0
        ),
        name="tail",
    )(pos, *in_hbm(back, ez, f1), *in_vmem(az, c, small, first))


def final_kernel(held_ref, grow_ref, small_ref, f1_ref, out_ref, made_ref, sem):
    requests, heads, p = out_ref.shape[:3]

    def copy(r):
        return pltpu.make_async_copy(made_ref.at[r], out_ref.at[r], sem.at[r])

    for r in range(requests):
        add = first_sources(grow_ref, small_ref, r)
        for h in range(heads):
            at = slice(h * p, h * p + p)
            block = small_ref[r, heads + h : heads + h + 1] * held_ref[r * heads + h] + add[at]
            made_ref[r, h] = small_ref[r, h : h + 1] * block + f1_ref[r, at]
        copy(r).start()
    for r in range(requests):
        copy(r).wait()


def finals(held, grow, small, f1):
    requests, width, n = f1.shape
    heads = (small.shape[1] - 8) // 2
    p = width // heads
    vmem = pl.BlockSpec(memory_space=pltpu.VMEM)
    return pl.pallas_call(
        final_kernel,
        out_shape=jax.ShapeDtypeStruct((requests, heads, p, n), F32),
        in_specs=[vmem] * 4,
        out_specs=pl.BlockSpec(memory_space=pltpu.HBM),
        scratch_shapes=[
            pltpu.VMEM((requests, heads, p, n), F32),
            pltpu.SemaphoreType.DMA((requests,)),
        ],
        compiler_params=pltpu.CompilerParams(vmem_limit_bytes=16 * MIB),
        cost_estimate=pl.CostEstimate(
            flops=2 * requests * width * n * 32, bytes_accessed=6 * MIB, transcendentals=0
        ),
        name="finals",
    )(*in_vmem(held, grow, small, f1))


def norm_kernel(channels, g_ref, s0_ref, s1_ref, s2_ref, s3_ref, gain_ref, out_ref, made_ref, sem):
    tokens, width = g_ref.shape
    seq = s0_ref.shape[1]
    step = 128
    gain = gain_ref[...].astype(F32)
    square = s0_ref[...] + s1_ref[...] + s2_ref[...] + s3_ref[...]
    scale = lax.rsqrt(square / channels + EPSILON)

    def copy(i):
        rows = slice(i * step, i * step + step)
        return pltpu.make_async_copy(made_ref.at[rows], out_ref.at[rows], sem.at[i])

    for i in range(tokens // step):
        rows = slice(i * step, i * step + step)
        r, at = i * step // seq, i * step % seq
        wide = jnp.broadcast_to(scale[r : r + 1, at : at + step], (128, step)).T
        for q in range(width // 128):
            cols = slice(q * 128, q * 128 + 128)
            made_ref[rows, cols] = (g_ref[rows, cols].astype(F32) * wide * gain[:, cols]).astype(BF16)
        copy(i).start()
    for i in range(tokens // step):
        copy(i).wait()


def normalise(g, parts, gain, channels):
    tokens, width = g.shape
    vmem = pl.BlockSpec(memory_space=pltpu.VMEM)
    return pl.pallas_call(
        functools.partial(norm_kernel, channels),
        out_shape=jax.ShapeDtypeStruct((tokens, width), BF16),
        in_specs=[vmem] * 6,
        out_specs=pl.BlockSpec(memory_space=pltpu.HBM),
        scratch_shapes=[pltpu.VMEM((tokens, width), BF16), pltpu.SemaphoreType.DMA((tokens // 128,))],
        compiler_params=pltpu.CompilerParams(vmem_limit_bytes=8 * MIB),
        cost_estimate=pl.CostEstimate(flops=2 * tokens * width, bytes_accessed=4 * MIB, transcendentals=0),
        name="normalise",
    )(g, *parts, gain)


def local(
    activations,
    gate_weight,
    inner_weight,
    state_proj,
    step_weight,
    inner_kernel,
    state_kernel,
    step_bias,
    decay_rate,
    skip_scale,
    norm_gain,
    scan_cache,
    window_cache,
    state_history,
    hit_owner,
    hit_slot,
):
    owners = lax.axis_size("dp")
    groups = lax.axis_size("mp")
    requests, heads = hit_owner.shape
    slots, _, p, n = scan_cache.shape
    width = inner_weight.shape[1]
    blocks = slots * heads

    cache = scan_cache.reshape(blocks, p, n)
    wanted, pos, cache, wa, wb = prep(hit_owner, hit_slot, cache, window_cache.reshape(blocks, -1), owners)
    codes = lax.all_to_all(wanted, "dp", split_axis=0, concat_axis=0, tiled=True)
    sent = pick(codes, cache, wa, wb)
    back = lax.all_to_all(sent, "dp", split_axis=0, concat_axis=0, tiled=True)

    inner, gate, state, step = project(activations, inner_weight, gate_weight, state_proj, step_weight)
    az, ez, c, f1, small, first = ssd(
        inner,
        gate,
        state,
        step,
        state_history,
        inner_kernel,
        state_kernel,
        step_bias[None],
        decay_rate[None],
        jnp.repeat(skip_scale, p)[None],
    )
    g, square, grow, held, f1 = tail(pos, back, ez, f1, az, c, small, first)
    final = finals(held, grow, small, f1)
    pair = [(i, i ^ 1) for i in range(groups)]
    square = square + lax.ppermute(square, "mp", pair)
    parts = [square] + [
        lax.ppermute(square, "mp", [(i, (i + 2 * s) % groups) for i in range(groups)])
        for s in range(1, groups // 2)
    ]
    normed = normalise(g, parts, norm_gain[None], width * groups)
    return normed, final


def solution(mesh):
    placed = (
        P("dp", None),
        P(None, "mp"),
        P(None, "mp"),
        P(),
        P(None, "mp"),
        P(None, "mp"),
        P(),
        P("mp"),
        P("mp"),
        P("mp"),
        P("mp"),
        P("dp", "mp", None, None),
        P("dp", "mp", None),
        P("dp", None, None),
        P("dp", "mp"),
        P("dp", "mp"),
    )
    return jax.shard_map(
        local,
        mesh=mesh,
        in_specs=placed,
        out_specs=(P("dp", "mp"), P("dp", "mp", None, None)),
        check_vma=False,
    )
```

```python
import functools

import jax
import jax.numpy as jnp
from jax import lax
from jax.experimental import pallas as pl
from jax.experimental.pallas import tpu as pltpu
from jax.sharding import PartitionSpec as P

EPSILON = 1e-05
CAP = 8
F32 = jnp.float32
BF16 = jnp.bfloat16
MIB = 1024 * 1024


def silu(v):
    half = 0.5 * v
    return half + half * jnp.tanh(half)


def full(shape, **kw):
    return pl.BlockSpec(shape, lambda *_: (0,) * len(shape), **kw)


def in_hbm(*arrays):
    return [pltpu.with_memory_space_constraint(v, pltpu.HBM) for v in arrays]


def in_vmem(*arrays):
    return [pltpu.with_memory_space_constraint(v, pltpu.VMEM) for v in arrays]


def prep_kernel(
    owner_hbm,
    slot_hbm,
    cache_hbm,
    window_hbm,
    wanted_hbm,
    pos_hbm,
    cache_ref,
    wa_ref,
    wb_ref,
    owner_ref,
    slot_ref,
    wanted_ref,
    pos_ref,
    count_ref,
    window_ref,
    sem,
):
    owners = wanted_ref.shape[0]
    requests, heads = owner_ref.shape
    tables = [
        pltpu.make_async_copy(owner_hbm, owner_ref, sem.at[4]),
        pltpu.make_async_copy(slot_hbm, slot_ref, sem.at[5]),
    ]
    for copy in tables:
        copy.start()
    cache_copy = pltpu.make_async_copy(cache_hbm, cache_ref, sem.at[1])
    cache_copy.start()
    window_copy = pltpu.make_async_copy(window_hbm, window_ref, sem.at[0])
    window_copy.start()
    for o in range(owners):
        count_ref[o] = 0
        for k in range(CAP):
            wanted_ref[o, 0, k] = 0
    for copy in tables:
        copy.wait()
    for r in range(requests):
        for h in range(heads):
            o = owner_ref[r, h]
            k = count_ref[o]
            count_ref[o] = k + 1
            wanted_ref[o, 0, k] = slot_ref[r, h] * heads + h
            pos_ref[r * heads + h] = o * CAP + k
    for o in range(owners):
        wanted_ref[o, 0, CAP] = count_ref[o]
    wanted_copy = pltpu.make_async_copy(wanted_ref, wanted_hbm, sem.at[2])
    wanted_copy.start()
    pos_copy = pltpu.make_async_copy(pos_ref, pos_hbm, sem.at[3])
    pos_copy.start()
    window_copy.wait()
    half = window_ref.shape[1] // 3
    w = window_ref[...].astype(F32)
    first = w[:, : 2 * half]
    second = jnp.concatenate([w[:, 2 * half :], jnp.zeros((w.shape[0], half), F32)], axis=1)
    odd = lax.broadcasted_iota(jnp.int32, first.shape, 0) % 2 == 1
    wa_ref[...] = jnp.where(odd, pltpu.roll(first, half, 1), first)
    wb_ref[...] = jnp.where(odd, pltpu.roll(second, half, 1), second)
    wanted_copy.wait()
    pos_copy.wait()
    cache_copy.wait()


def prep(hit_owner, hit_slot, cache, window, owners):
    entries = hit_owner.size
    vmem = pl.BlockSpec(memory_space=pltpu.VMEM)
    hbm = pl.BlockSpec(memory_space=pltpu.HBM)
    blocks, p, n = cache.shape
    return pl.pallas_call(
        prep_kernel,
        out_shape=(
            pltpu.HBM((owners, 1, 128), jnp.int32),
            pltpu.HBM((entries,), jnp.int32),
            pltpu.VMEM((blocks, p, n), F32),
            pltpu.VMEM((blocks, n), F32),
            pltpu.VMEM((blocks, n), F32),
        ),
        in_specs=[hbm] * 4,
        out_specs=(hbm, hbm, vmem, vmem, vmem),
        scratch_shapes=[
            pltpu.SMEM(hit_owner.shape, jnp.int32),
            pltpu.SMEM(hit_slot.shape, jnp.int32),
            pltpu.SMEM((owners, 1, 128), jnp.int32),
            pltpu.SMEM((entries,), jnp.int32),
            pltpu.SMEM((owners,), jnp.int32),
            pltpu.VMEM(window.shape, window.dtype),
            pltpu.SemaphoreType.DMA((6,)),
        ],
        compiler_params=pltpu.CompilerParams(vmem_limit_bytes=8 * MIB),
        name="prep",
    )(*in_hbm(hit_owner, hit_slot, cache, window))


def pick_kernel(codes_ref, cache_ref, wa_ref, wb_ref, out_ref, rows_ref, extra_ref, sem, extra_sem):
    owners = out_ref.shape[0]
    p = cache_ref.shape[1]
    cached = CAP * p
    always = CAP // 2
    extra_ref[0] = 0

    @pl.loop(0, owners)
    def _(d):
        for k in range(always):
            pltpu.make_async_copy(
                cache_ref.at[codes_ref[d, 0, k]], out_ref.at[d, k * p : k * p + p], sem
            ).start()
        count = codes_ref[d, 0, CAP]

        @pl.when(count > always)
        def _():
            extra_ref[0] += count - always

            @pl.loop(always, count)
            def _(k):
                pltpu.make_async_copy(
                    cache_ref.at[codes_ref[d, 0, k]],
                    out_ref.at[d, pl.ds(pl.multiple_of(k * p, p), p)],
                    extra_sem,
                ).start()

    @pl.loop(0, owners)
    def _(d):
        for k in range(CAP):
            at = pl.ds(codes_ref[d, 0, k], 1)
            rows_ref[d, 2 * k : 2 * k + 1] = wa_ref[at]
            rows_ref[d, 2 * k + 1 : 2 * k + 2] = wb_ref[at]

    pltpu.make_async_copy(rows_ref, out_ref.at[:, cached:], sem).start()

    @pl.loop(0, extra_ref[0])
    def _(_):
        pltpu.make_async_copy(cache_ref.at[0], out_ref.at[0, :p], extra_sem).wait()

    done = out_ref.at[:, : always * p + 2 * CAP]
    pltpu.make_async_copy(done, done, sem).wait()


def pick(codes, cache, wa, wb):
    owners = codes.shape[0]
    blocks, p, n = cache.shape
    vmem = pl.BlockSpec(memory_space=pltpu.VMEM)
    hbm = pl.BlockSpec(memory_space=pltpu.HBM)
    return pl.pallas_call(
        pick_kernel,
        out_shape=pltpu.HBM((owners, CAP * p + 2 * CAP, n), F32),
        in_specs=[pl.BlockSpec(memory_space=pltpu.SMEM), vmem, vmem, vmem],
        out_specs=hbm,
        scratch_shapes=[
            pltpu.VMEM((owners, 2 * CAP, n), F32),
            pltpu.SMEM((1,), jnp.int32),
            pltpu.SemaphoreType.DMA,
            pltpu.SemaphoreType.DMA,
        ],
        compiler_params=pltpu.CompilerParams(vmem_limit_bytes=8 * MIB),
        cost_estimate=pl.CostEstimate(flops=0, bytes_accessed=8 * MIB, transcendentals=0),
        name="pick",
    )(codes, *in_vmem(cache, wa, wb))


TILE = 256


def project_kernel(steps, act_ref, wi_ref, wg_ref, ws_ref, wd_ref, inner_ref, gate_ref, state_ref, step_ref):
    j = pl.program_id(0)
    rows = act_ref.shape[0]
    chunk = 1024

    def run(w_ref, out_ref):
        @pl.loop(0, rows // chunk)
        def _(m):
            at = pl.ds(pl.multiple_of(m * chunk, chunk), chunk)
            out_ref[at, :] = jnp.dot(act_ref[at, :], w_ref[...], preferred_element_type=F32).astype(out_ref.dtype)

    @pl.when(j == 0)
    def _():
        run(ws_ref, state_ref)
        run(wd_ref, step_ref)

    @pl.when((j > 0) & (j <= steps))
    def _():
        run(wi_ref, inner_ref)

    @pl.when(j > steps)
    def _():
        run(wg_ref, gate_ref)


def project(act, wi, wg, ws, wd):
    rows, depth = act.shape
    width = wi.shape[1]
    steps = width // TILE

    def at_inner(j):
        return (0, jnp.clip(j - 1, 0, steps - 1))

    def at_gate(j):
        return (0, jnp.clip(j - 1 - steps, 0, steps - 1))

    flops = 2 * rows * depth * (2 * width + ws.shape[1] + wd.shape[1])
    return pl.pallas_call(
        functools.partial(project_kernel, steps),
        out_shape=(
            jax.ShapeDtypeStruct((rows, width), BF16),
            jax.ShapeDtypeStruct((rows, width), BF16),
            jax.ShapeDtypeStruct((rows, ws.shape[1]), BF16),
            jax.ShapeDtypeStruct((rows, wd.shape[1]), F32),
        ),
        grid=(1 + 2 * steps,),
        in_specs=[
            full((rows, depth), pipeline_mode=pl.Buffered(1)),
            pl.BlockSpec((depth, TILE), at_inner),
            pl.BlockSpec((depth, TILE), at_gate),
            full(ws.shape, pipeline_mode=pl.Buffered(1)),
            full(wd.shape, pipeline_mode=pl.Buffered(1)),
        ],
        out_specs=(
            pl.BlockSpec((rows, TILE), at_inner),
            pl.BlockSpec((rows, TILE), at_gate),
            full((rows, ws.shape[1])),
            full((rows, wd.shape[1])),
        ),
        compiler_params=pltpu.CompilerParams(vmem_limit_bytes=60 * MIB),
        cost_estimate=pl.CostEstimate(flops=flops, bytes_accessed=32 * MIB, transcendentals=0),
        name="project",
    )(act, wi, wg, ws, wd)


def ssd_kernel(
    inner_ref,
    gate_ref,
    state_ref,
    step_ref,
    hist_ref,
    ik_ref,
    sk_ref,
    bias_ref,
    decay_ref,
    skip_ref,
    az_ref,
    ez_ref,
    c_ref,
    f1_ref,
    small_ref,
    first_ref,
    u_ref,
    v_ref,
):
    seq, width = inner_ref.shape
    heads = step_ref.shape[1]
    p = width // heads
    taps = ik_ref.shape[0]
    lag = taps - 1
    n = state_ref.shape[1] // 2
    lead = 8 - lag
    half = seq // 2

    v_ref[lead:8, :] = hist_ref[0].astype(F32)
    v_ref[8:, :] = state_ref[...].astype(F32)
    sk = sk_ref[...].astype(F32)
    run = jnp.zeros((seq, 2 * n), F32)
    for k in range(taps):
        run = run + sk[k : k + 1] * v_ref[lead + k : lead + k + seq, :]
    conv = silu(run).astype(BF16)
    b = conv[:, :n]
    c = conv[:, n:]
    c_ref[:, :n] = c
    small_ref[0, 2 * heads :] = b[:16].astype(F32)[:8]

    raw = step_ref[...] + bias_ref[...]
    dt = jnp.maximum(raw, 0.0) + jnp.log1p(jnp.exp(-jnp.abs(raw)))
    dt = jnp.concatenate([dt, jnp.zeros((seq, 128 - heads), F32)], axis=1)
    decay = jnp.concatenate([decay_ref[...], jnp.zeros((1, 128 - heads), F32)], axis=1)
    t_at = lax.broadcasted_iota(jnp.int32, (seq, seq), 0)
    s_at = lax.broadcasted_iota(jnp.int32, (seq, seq), 1)
    causal = s_at <= t_at
    cum = jnp.dot(
        causal.astype(F32), -decay * dt, preferred_element_type=F32, precision=lax.Precision.HIGHEST
    )
    cum_t = cum.T
    dt_t = dt.T
    begin = cum[lag - 1 : lag]
    last = cum[seq - 1 : seq]
    spread = (
        lax.broadcasted_iota(jnp.int32, (128, width), 1) // p
        == lax.broadcasted_iota(jnp.int32, (128, width), 0)
    )
    spread = spread.astype(F32).astype(BF16)
    early = lax.broadcasted_iota(jnp.int32, (seq, 128), 0) < lag
    grown = jnp.exp(jnp.where(early, cum, jnp.minimum(cum - begin, 0.0))).astype(BF16)
    tail = jnp.exp(jnp.minimum(last - cum, 0.0)) * dt
    begin_t = cum_t[:heads, lag - 1 : lag]
    last_t = cum_t[:heads, seq - 1 : seq]
    small_ref[0, :heads] = jnp.broadcast_to(jnp.exp(jnp.minimum(last_t - begin_t, 0.0)), (heads, n))
    small_ref[0, heads : 2 * heads] = jnp.broadcast_to(jnp.exp(begin_t), (heads, n))

    scores = lax.dot_general(c, b, (((1,), (1,)), ((), ())), preferred_element_type=F32)
    scores = jnp.where(causal, scores, 0.0)
    own = scores[:, :n]
    seen = (lax.broadcasted_iota(jnp.int32, own.shape, 1) < lag) & (
        lax.broadcasted_iota(jnp.int32, own.shape, 0) >= lag
    )
    c_ref[:, n:] = pltpu.roll(jnp.where(seen, own, 0.0), 8 * pl.program_id(0), 1).astype(BF16)
    top = scores[:half, :half]
    bottom = scores[half:]

    row8 = lax.broadcasted_iota(jnp.int32, (8, 128), 0)
    cum8 = cum[:8]
    dt8 = dt[:8]
    small = [jnp.where(row8 < lag, jnp.exp(jnp.minimum(begin - cum8, 0.0)) * dt8, 0.0).astype(BF16)]
    for j in range(lag):
        rows = []
        for t in range(8):
            if j <= t < lag:
                s = t - j
                gap = jnp.exp(jnp.minimum(cum[t : t + 1] - cum[s : s + 1], 0.0))
                rows.append(gap * scores[t : t + 1, s : s + 1] * dt[s : s + 1])
            else:
                rows.append(jnp.zeros((1, 128), F32))
        small.append(jnp.concatenate(rows, axis=0).astype(BF16))
    small = jnp.concatenate([m.astype(F32) for m in small], axis=0).astype(BF16)

    u_ref[:8, :] = jnp.zeros((8, width), F32)
    u_ref[8:, :] = inner_ref[...].astype(F32)
    lane = lax.broadcasted_iota(jnp.int32, (1, 128), 1)
    for q in range(width // 128):
        cols = slice(q * 128, q * 128 + 128)
        ik = ik_ref[:, cols].astype(F32)
        run = jnp.zeros((seq, 128), F32)
        for k in range(taps):
            run = run + ik[k : k + 1] * u_ref[lead + k : lead + k + seq, cols]
        x = jnp.where(early, 0.0, silu(run)).astype(BF16)
        xf = x.astype(F32)
        y_top = jnp.zeros((half, 128), F32)
        y_bottom = jnp.zeros((seq - half, 128), F32)
        for s in range(128 // p):
            h = q * (128 // p) + s
            own = (lane >= s * p) & (lane < (s + 1) * p)
            xs = jnp.where(own, xf, 0.0).astype(BF16)
            col = cum[:, h : h + 1]
            row = cum_t[h : h + 1]
            dr = dt_t[h : h + 1]
            w_top = jnp.exp(jnp.minimum(col[:half] - row[:, :half], 0.0)) * (top * dr[:, :half])
            w_bottom = jnp.exp(jnp.minimum(col[half:] - row, 0.0)) * (bottom * dr)
            y_top = y_top + jnp.dot(w_top.astype(BF16), xs[:half], preferred_element_type=F32)
            y_bottom = y_bottom + jnp.dot(w_bottom.astype(BF16), xs, preferred_element_type=F32)
        skip = skip_ref[:, cols]
        y = jnp.concatenate([y_top, y_bottom], axis=0) + skip * xf
        z = silu(gate_ref[:, cols].astype(F32))
        az_ref[:, cols] = (y * z).astype(BF16)
        ez = jnp.dot(grown, spread[:, cols], preferred_element_type=F32) * z
        ez_ref[:, cols] = ez.astype(BF16)
        tw = jnp.dot(tail.astype(BF16), spread[:, cols], preferred_element_type=F32)
        xt = (xf * tw).astype(BF16)
        f1_ref[0, cols, :] = lax.dot_general(
            xt, b, (((0,), (0,)), ((), ())), preferred_element_type=F32
        )
        wide = jnp.dot(small, spread[:, cols], preferred_element_type=F32)
        first_ref[0, 0:8, cols] = run[:8]
        first_ref[0, 16 + 8 * lag : 16 + 8 * lag + taps, cols] = ik
        first_ref[0, 8:16, cols] = wide[:8]
        z8 = z[:8]
        first_ref[0, 16:24, cols] = jnp.where(row8 < lag, (wide[8:16] + skip) * z8, 0.0)
        for j in range(1, lag):
            first_ref[0, 16 + 8 * j : 24 + 8 * j, cols] = wide[8 + 8 * j : 16 + 8 * j] * z8


def ssd(inner, gate, state, step, history, ik, sk, bias, decay, skip):
    tokens, width = inner.shape
    requests = history.shape[0]
    seq = tokens // requests
    heads = step.shape[1]
    n2 = state.shape[1]
    n = n2 // 2
    lag = ik.shape[0] - 1
    rows = lambda w: pl.BlockSpec((seq, w), lambda r: (r, 0))
    per = lambda *s: pl.BlockSpec((1,) + s, lambda r: (r,) + (0,) * len(s))
    return pl.pallas_call(
        ssd_kernel,
        out_shape=(
            pltpu.VMEM((tokens, width), BF16),
            pltpu.HBM((tokens, width), BF16),
            pltpu.VMEM((tokens, 2 * n), BF16),
            pltpu.HBM((requests, width, n), F32),
            pltpu.VMEM((requests, 2 * heads + 8, n), F32),
            pltpu.VMEM((requests, 24 + 8 * lag, width), F32),
        ),
        grid=(requests,),
        in_specs=[
            rows(width),
            rows(width),
            rows(n2),
            rows(heads),
            per(*history.shape[1:]),
            full(ik.shape),
            full(sk.shape),
            full(bias.shape),
            full(decay.shape),
            full(skip.shape),
        ],
        out_specs=(
            rows(width),
            rows(width),
            rows(2 * n),
            per(width, n),
            per(2 * heads + 8, n),
            per(24 + 8 * lag, width),
        ),
        scratch_shapes=[pltpu.VMEM((seq + 8, width), F32), pltpu.VMEM((seq + 8, n2), F32)],
        compiler_params=pltpu.CompilerParams(vmem_limit_bytes=40 * MIB),
        cost_estimate=pl.CostEstimate(
            flops=2 * tokens * width * seq * 2, bytes_accessed=14 * MIB, transcendentals=tokens * seq * heads
        ),
        name="ssd",
    )(*in_hbm(inner, gate, state, step), history, ik, sk, bias, decay, skip)


def first_sources(grow_ref, small_ref, r):
    requests = small_ref.shape[0]
    b = small_ref[r, small_ref.shape[1] - 8 :]
    zero = jnp.zeros_like(b)
    b = jnp.concatenate([b if i == r else zero for i in range(requests)], axis=0).astype(BF16)
    return jnp.dot(grow_ref[...], b, preferred_element_type=F32)


def tail_kernel(
    pos_ref,
    back_ref,
    ez_hbm,
    f1_hbm,
    az_ref,
    c_ref,
    small_ref,
    first_ref,
    g_ref,
    sq_ref,
    grow_ref,
    held_ref,
    f1_ref,
    ez_ref,
    rows_ref,
    s_ref,
    raw_ref,
    win_ref,
    mix_ref,
    x_ref,
    extra_ref,
    sem,
    ez_sem,
    once_sem,
):
    requests = first_ref.shape[0]
    heads = (small_ref.shape[1] - 8) // 2
    p = held_ref.shape[1]
    tokens, width = g_ref.shape
    seq = tokens // requests
    lag = (first_ref.shape[1] - 24) // 8
    pairs = heads // 2

    def rows_of(r):
        return slice(r * seq, r * seq + seq)

    batch = requests // 2

    def ez_copy(i):
        rows = slice(i * batch * seq, (i + 1) * batch * seq)
        return pltpu.make_async_copy(ez_hbm.at[rows], ez_ref.at[rows], ez_sem.at[i])

    def fetch(i):
        ez_copy(i).start()
        for e in range(i * batch * heads, (i + 1) * batch * heads):
            at = pos_ref[e]
            pltpu.make_async_copy(
                back_ref.at[at // CAP, pl.ds(pl.multiple_of((at % CAP) * p, p), p)],
                held_ref.at[e],
                sem.at[i],
            ).start()

    row_copy = pltpu.make_async_copy(back_ref.at[:, CAP * p :], rows_ref, once_sem.at[0])
    f1_copy = pltpu.make_async_copy(f1_hbm, f1_ref, once_sem.at[1])
    row_copy.start()
    fetch(0)
    fetch(1)
    f1_copy.start()
    win_ref[...] = jnp.zeros_like(win_ref)
    x_ref[...] = jnp.zeros_like(x_ref)
    row_copy.wait()

    low = lax.broadcasted_iota(jnp.int32, (1, 128), 1) < p
    flat = rows_ref.reshape(rows_ref.shape[0] * rows_ref.shape[1], 128)
    for i in range(requests):
        for q in range(pairs):
            cols = slice(q * 128, q * 128 + 128)
            even = 2 * pos_ref[i * heads + 2 * q]
            odd = 2 * pos_ref[i * heads + 2 * q + 1]
            a0, a1 = flat[pl.ds(even, 1)], flat[pl.ds(odd, 1)]
            b0, b1 = flat[pl.ds(even + 1, 1)], flat[pl.ds(odd + 1, 1)]
            win_ref[i, 0:1, cols] = jnp.where(low, a0, a1)
            win_ref[i, 2:3, cols] = jnp.where(low, b0, b1)
            mix_ref[i * pairs + q : i * pairs + q + 1] = jnp.where(low, a1, a0)
    mix = pltpu.roll(mix_ref[...], p, 1)
    for i in range(requests):
        for q in range(pairs):
            win_ref[i, 1:2, q * 128 : q * 128 + 128] = mix[i * pairs + q : i * pairs + q + 1]

    run = first_ref[:, 0:8]
    for k in range(lag):
        at = 16 + 8 * lag + k
        run = run + first_ref[:, at : at + 1] * win_ref[:, k : k + 8]
    row8 = lax.broadcasted_iota(jnp.int32, run.shape, 1)
    x = jnp.where(row8 < lag, silu(run), 0.0).astype(BF16).astype(F32)
    x_ref[:, 8:16] = x
    extra = first_ref[:, 16:24] * x
    for j in range(1, lag):
        extra = extra + first_ref[:, 16 + 8 * j : 24 + 8 * j] * x_ref[:, 8 - j : 16 - j]
    extra_ref[...] = extra
    grow = (x * first_ref[:, 8:16]).reshape(requests * 8, width).T
    grow_ref[...] = grow.astype(BF16)
    n = c_ref.shape[1] // 2
    grow = jnp.concatenate([grow, jnp.zeros((width, n - requests * 8), F32)], axis=1).astype(BF16)
    s_ref[0, :, n:] = grow
    s_ref[1, :, n:] = grow

    row16 = lax.broadcasted_iota(jnp.int32, (16, 256), 0)
    nt = (((1,), (1,)), ((), ()))
    squares = []
    for r in range(requests):
        rows = rows_of(r)
        if r % batch == 0:
            part = held_ref.at[r * heads : (r + batch) * heads]
            pltpu.make_async_copy(part, part, sem.at[r // batch]).wait()
            ez_copy(r // batch).wait()
        for h in range(heads):
            at = slice(h * p, h * p + p)
            block = held_ref[r * heads + h]
            raw_ref[r % 2, at] = block.astype(BF16)
            s_ref[r % 2, at, :n] = (small_ref[r, heads + h : heads + h + 1] * block).astype(BF16)
        c = c_ref[rows]
        total = jnp.zeros((seq - 16, 128), F32)
        total16 = jnp.zeros((16, 128), F32)
        for q in range(width // 256):
            cols = slice(q * 256, q * 256 + 256)
            seen = lax.dot_general(c, s_ref[r % 2, cols], nt, preferred_element_type=F32)
            seen16 = lax.dot_general(c[:16, :n], raw_ref[r % 2, cols], nt, preferred_element_type=F32)
            seen16 = jnp.where(row16 < lag, seen16, seen[:16])
            az = az_ref[rows, cols].astype(F32)
            ez = ez_ref[rows, cols].astype(F32)
            g = az[16:] + ez[16:] * seen[16:]
            g16 = az[:16] + ez[:16] * seen16
            g16 = g16 + jnp.concatenate([extra_ref[r, :, cols], jnp.zeros((8, 256), F32)], axis=0)
            g_ref[r * seq : r * seq + 16, cols] = g16.astype(BF16)
            g_ref[r * seq + 16 : r * seq + seq, cols] = g.astype(BF16)
            g = g * g
            g16 = g16 * g16
            total = total + g[:, :128] + g[:, 128:]
            total16 = total16 + g16[:, :128] + g16[:, 128:]
        total = jnp.concatenate([total16, total], axis=0)
        squares.append(jnp.sum(total.T, axis=0, keepdims=True))
    squares.append(jnp.zeros((8 - requests, seq), F32))
    sq_ref[...] = jnp.concatenate(squares, axis=0)
    f1_copy.wait()


def tail(pos, back, ez, f1, az, c, small, first):
    requests, packed, n = small.shape
    heads = (packed - 8) // 2
    assert requests * 8 <= n
    tokens, width = az.shape
    p = width // heads
    seq = tokens // requests
    owners = back.shape[0]
    vmem = pl.BlockSpec(memory_space=pltpu.VMEM)
    hbm = pl.BlockSpec(memory_space=pltpu.HBM)
    return pl.pallas_call(
        tail_kernel,
        out_shape=(
            pltpu.VMEM((tokens, width), BF16),
            pltpu.VMEM((8, seq), F32),
            pltpu.VMEM((width, requests * 8), BF16),
            pltpu.VMEM((requests * heads, p, n), F32),
            pltpu.VMEM(f1.shape, F32),
        ),
        in_specs=[pl.BlockSpec(memory_space=pltpu.SMEM)] + [hbm] * 3 + [vmem] * 4,
        out_specs=(vmem,) * 5,
        scratch_shapes=[
            pltpu.VMEM((tokens, width), BF16),
            pltpu.VMEM((owners, 2 * CAP, n), F32),
            pltpu.VMEM((2, width, 2 * n), BF16),
            pltpu.VMEM((2, width, n), BF16),
            pltpu.VMEM((requests, 16, width), F32),
            pltpu.VMEM((requests * heads // 2, 128), F32),
            pltpu.VMEM((requests, 16, width), F32),
            pltpu.VMEM((requests, 8, width), F32),
            pltpu.SemaphoreType.DMA((2,)),
            pltpu.SemaphoreType.DMA((2,)),
            pltpu.SemaphoreType.DMA((2,)),
        ],
        compiler_params=pltpu.CompilerParams(vmem_limit_bytes=24 * MIB),
        cost_estimate=pl.CostEstimate(
            flops=2 * tokens * width * n, bytes_accessed=10 * MIB, transcendentals=0
        ),
        name="tail",
    )(pos, *in_hbm(back, ez, f1), *in_vmem(az, c, small, first))


def final_kernel(held_ref, grow_ref, small_ref, f1_ref, out_ref, made_ref, sem):
    requests, heads, p = out_ref.shape[:3]

    def copy(r):
        return pltpu.make_async_copy(made_ref.at[r], out_ref.at[r], sem.at[r])

    for r in range(requests):
        add = first_sources(grow_ref, small_ref, r)
        for h in range(heads):
            at = slice(h * p, h * p + p)
            block = small_ref[r, heads + h : heads + h + 1] * held_ref[r * heads + h] + add[at]
            made_ref[r, h] = small_ref[r, h : h + 1] * block + f1_ref[r, at]
        copy(r).start()
    for r in range(requests):
        copy(r).wait()


def finals(held, grow, small, f1):
    requests, width, n = f1.shape
    heads = (small.shape[1] - 8) // 2
    p = width // heads
    vmem = pl.BlockSpec(memory_space=pltpu.VMEM)
    return pl.pallas_call(
        final_kernel,
        out_shape=jax.ShapeDtypeStruct((requests, heads, p, n), F32),
        in_specs=[vmem] * 4,
        out_specs=pl.BlockSpec(memory_space=pltpu.HBM),
        scratch_shapes=[
            pltpu.VMEM((requests, heads, p, n), F32),
            pltpu.SemaphoreType.DMA((requests,)),
        ],
        compiler_params=pltpu.CompilerParams(vmem_limit_bytes=16 * MIB),
        cost_estimate=pl.CostEstimate(
            flops=2 * requests * width * n * 32, bytes_accessed=6 * MIB, transcendentals=0
        ),
        name="finals",
    )(*in_vmem(held, grow, small, f1))


def norm_kernel(channels, g_ref, s0_ref, s1_ref, s2_ref, s3_ref, gain_ref, out_ref, made_ref, sem):
    tokens, width = g_ref.shape
    seq = s0_ref.shape[1]
    step = 128
    gain = gain_ref[...].astype(F32)
    square = s0_ref[...] + s1_ref[...] + s2_ref[...] + s3_ref[...]
    scale = lax.rsqrt(square / channels + EPSILON)

    def copy(i):
        rows = slice(i * step, i * step + step)
        return pltpu.make_async_copy(made_ref.at[rows], out_ref.at[rows], sem.at[i])

    for i in range(tokens // step):
        rows = slice(i * step, i * step + step)
        r, at = i * step // seq, i * step % seq
        wide = jnp.broadcast_to(scale[r : r + 1, at : at + step], (128, step)).T
        for q in range(width // 128):
            cols = slice(q * 128, q * 128 + 128)
            made_ref[rows, cols] = (g_ref[rows, cols].astype(F32) * wide * gain[:, cols]).astype(BF16)
        copy(i).start()
    for i in range(tokens // step):
        copy(i).wait()


def normalise(g, parts, gain, channels):
    tokens, width = g.shape
    vmem = pl.BlockSpec(memory_space=pltpu.VMEM)
    return pl.pallas_call(
        functools.partial(norm_kernel, channels),
        out_shape=jax.ShapeDtypeStruct((tokens, width), BF16),
        in_specs=[vmem] * 6,
        out_specs=pl.BlockSpec(memory_space=pltpu.HBM),
        scratch_shapes=[pltpu.VMEM((tokens, width), BF16), pltpu.SemaphoreType.DMA((tokens // 128,))],
        compiler_params=pltpu.CompilerParams(vmem_limit_bytes=8 * MIB),
        cost_estimate=pl.CostEstimate(flops=2 * tokens * width, bytes_accessed=4 * MIB, transcendentals=0),
        name="normalise",
    )(g, *parts, gain)


def local(
    activations,
    gate_weight,
    inner_weight,
    state_proj,
    step_weight,
    inner_kernel,
    state_kernel,
    step_bias,
    decay_rate,
    skip_scale,
    norm_gain,
    scan_cache,
    window_cache,
    state_history,
    hit_owner,
    hit_slot,
):
    owners = lax.axis_size("dp")
    groups = lax.axis_size("mp")
    requests, heads = hit_owner.shape
    slots, _, p, n = scan_cache.shape
    width = inner_weight.shape[1]
    blocks = slots * heads

    cache = scan_cache.reshape(blocks, p, n)
    wanted, pos, cache, wa, wb = prep(hit_owner, hit_slot, cache, window_cache.reshape(blocks, -1), owners)
    codes = lax.all_to_all(wanted, "dp", split_axis=0, concat_axis=0, tiled=True)
    sent = pick(codes, cache, wa, wb)
    back = lax.all_to_all(sent, "dp", split_axis=0, concat_axis=0, tiled=True)

    inner, gate, state, step = project(activations, inner_weight, gate_weight, state_proj, step_weight)
    az, ez, c, f1, small, first = ssd(
        inner,
        gate,
        state,
        step,
        state_history,
        inner_kernel,
        state_kernel,
        step_bias[None],
        decay_rate[None],
        jnp.repeat(skip_scale, p)[None],
    )
    g, square, grow, held, f1 = tail(pos, back, ez, f1, az, c, small, first)
    final = finals(held, grow, small, f1)
    pair = [(i, i ^ 1) for i in range(groups)]
    square = square + lax.ppermute(square, "mp", pair)
    parts = [square] + [
        lax.ppermute(square, "mp", [(i, (i + 2 * s) % groups) for i in range(groups)])
        for s in range(1, groups // 2)
    ]
    normed = normalise(g, parts, norm_gain[None], width * groups)
    return normed, final


def solution(mesh):
    placed = (
        P("dp", None),
        P(None, "mp"),
        P(None, "mp"),
        P(),
        P(None, "mp"),
        P(None, "mp"),
        P(),
        P("mp"),
        P("mp"),
        P("mp"),
        P("mp"),
        P("dp", "mp", None, None),
        P("dp", "mp", None),
        P("dp", None, None),
        P("dp", "mp"),
        P("dp", "mp"),
    )
    return jax.shard_map(
        local,
        mesh=mesh,
        in_specs=placed,
        out_specs=(P("dp", "mp"), P("dp", "mp", None, None)),
        check_vma=False,
    )
```

```python
import functools

import jax
import jax.numpy as jnp
from jax import lax
from jax.experimental import pallas as pl
from jax.experimental.pallas import tpu as pltpu
from jax.sharding import PartitionSpec as P

EPSILON = 1e-05
CAP = 8
F32 = jnp.float32
BF16 = jnp.bfloat16
MIB = 1024 * 1024


def silu(v):
    half = 0.5 * v
    return half + half * jnp.tanh(half)


def full(shape, **kw):
    return pl.BlockSpec(shape, lambda *_: (0,) * len(shape), **kw)


def in_hbm(*arrays):
    return [pltpu.with_memory_space_constraint(v, pltpu.HBM) for v in arrays]


def in_vmem(*arrays):
    return [pltpu.with_memory_space_constraint(v, pltpu.VMEM) for v in arrays]


def prep_kernel(
    owner_hbm,
    slot_hbm,
    cache_hbm,
    window_hbm,
    wanted_hbm,
    pos_hbm,
    cache_ref,
    wa_ref,
    wb_ref,
    owner_ref,
    slot_ref,
    wanted_ref,
    pos_ref,
    count_ref,
    window_ref,
    sem,
):
    owners = wanted_ref.shape[0]
    requests, heads = owner_ref.shape
    tables = [
        pltpu.make_async_copy(owner_hbm, owner_ref, sem.at[4]),
        pltpu.make_async_copy(slot_hbm, slot_ref, sem.at[5]),
    ]
    for copy in tables:
        copy.start()
    cache_copy = pltpu.make_async_copy(cache_hbm, cache_ref, sem.at[1])
    cache_copy.start()
    window_copy = pltpu.make_async_copy(window_hbm, window_ref, sem.at[0])
    window_copy.start()
    for o in range(owners):
        count_ref[o] = 0
        for k in range(CAP):
            wanted_ref[o, 0, k] = 0
    for copy in tables:
        copy.wait()
    for r in range(requests):
        for h in range(heads):
            o = owner_ref[r, h]
            k = count_ref[o]
            count_ref[o] = k + 1
            wanted_ref[o, 0, k] = slot_ref[r, h] * heads + h
            pos_ref[r * heads + h] = o * CAP + k
    for o in range(owners):
        wanted_ref[o, 0, CAP] = count_ref[o]
    wanted_copy = pltpu.make_async_copy(wanted_ref, wanted_hbm, sem.at[2])
    wanted_copy.start()
    pos_copy = pltpu.make_async_copy(pos_ref, pos_hbm, sem.at[3])
    pos_copy.start()
    window_copy.wait()
    half = window_ref.shape[1] // 3
    w = window_ref[...].astype(F32)
    first = w[:, : 2 * half]
    second = jnp.concatenate([w[:, 2 * half :], jnp.zeros((w.shape[0], half), F32)], axis=1)
    odd = lax.broadcasted_iota(jnp.int32, first.shape, 0) % 2 == 1
    wa_ref[...] = jnp.where(odd, pltpu.roll(first, half, 1), first)
    wb_ref[...] = jnp.where(odd, pltpu.roll(second, half, 1), second)
    wanted_copy.wait()
    pos_copy.wait()
    cache_copy.wait()


def prep(hit_owner, hit_slot, cache, window, owners):
    entries = hit_owner.size
    vmem = pl.BlockSpec(memory_space=pltpu.VMEM)
    hbm = pl.BlockSpec(memory_space=pltpu.HBM)
    blocks, p, n = cache.shape
    return pl.pallas_call(
        prep_kernel,
        out_shape=(
            pltpu.HBM((owners, 1, 128), jnp.int32),
            pltpu.HBM((entries,), jnp.int32),
            pltpu.VMEM((blocks, p, n), F32),
            pltpu.VMEM((blocks, n), F32),
            pltpu.VMEM((blocks, n), F32),
        ),
        in_specs=[hbm] * 4,
        out_specs=(hbm, hbm, vmem, vmem, vmem),
        scratch_shapes=[
            pltpu.SMEM(hit_owner.shape, jnp.int32),
            pltpu.SMEM(hit_slot.shape, jnp.int32),
            pltpu.SMEM((owners, 1, 128), jnp.int32),
            pltpu.SMEM((entries,), jnp.int32),
            pltpu.SMEM((owners,), jnp.int32),
            pltpu.VMEM(window.shape, window.dtype),
            pltpu.SemaphoreType.DMA((6,)),
        ],
        compiler_params=pltpu.CompilerParams(vmem_limit_bytes=8 * MIB),
        name="prep",
    )(*in_hbm(hit_owner, hit_slot, cache, window))


def pick_kernel(codes_ref, cache_ref, wa_ref, wb_ref, out_ref, rows_ref, extra_ref, sem, extra_sem):
    owners = out_ref.shape[0]
    p = cache_ref.shape[1]
    cached = CAP * p
    always = CAP // 2
    extra_ref[0] = 0

    @pl.loop(0, owners)
    def _(d):
        for k in range(always):
            pltpu.make_async_copy(
                cache_ref.at[codes_ref[d, 0, k]], out_ref.at[d, k * p : k * p + p], sem
            ).start()
        count = codes_ref[d, 0, CAP]

        @pl.when(count > always)
        def _():
            extra_ref[0] += count - always

            @pl.loop(always, count)
            def _(k):
                pltpu.make_async_copy(
                    cache_ref.at[codes_ref[d, 0, k]],
                    out_ref.at[d, pl.ds(pl.multiple_of(k * p, p), p)],
                    extra_sem,
                ).start()

    @pl.loop(0, owners)
    def _(d):
        for k in range(CAP):
            at = pl.ds(codes_ref[d, 0, k], 1)
            rows_ref[d, 2 * k : 2 * k + 1] = wa_ref[at]
            rows_ref[d, 2 * k + 1 : 2 * k + 2] = wb_ref[at]

    pltpu.make_async_copy(rows_ref, out_ref.at[:, cached:], sem).start()

    @pl.loop(0, extra_ref[0])
    def _(_):
        pltpu.make_async_copy(cache_ref.at[0], out_ref.at[0, :p], extra_sem).wait()

    done = out_ref.at[:, : always * p + 2 * CAP]
    pltpu.make_async_copy(done, done, sem).wait()


def pick(codes, cache, wa, wb):
    owners = codes.shape[0]
    blocks, p, n = cache.shape
    vmem = pl.BlockSpec(memory_space=pltpu.VMEM)
    hbm = pl.BlockSpec(memory_space=pltpu.HBM)
    return pl.pallas_call(
        pick_kernel,
        out_shape=pltpu.HBM((owners, CAP * p + 2 * CAP, n), F32),
        in_specs=[pl.BlockSpec(memory_space=pltpu.SMEM), vmem, vmem, vmem],
        out_specs=hbm,
        scratch_shapes=[
            pltpu.VMEM((owners, 2 * CAP, n), F32),
            pltpu.SMEM((1,), jnp.int32),
            pltpu.SemaphoreType.DMA,
            pltpu.SemaphoreType.DMA,
        ],
        compiler_params=pltpu.CompilerParams(vmem_limit_bytes=8 * MIB),
        cost_estimate=pl.CostEstimate(flops=0, bytes_accessed=8 * MIB, transcendentals=0),
        name="pick",
    )(codes, *in_vmem(cache, wa, wb))


TILE = 256


def project_kernel(steps, act_ref, wi_ref, wg_ref, ws_ref, wd_ref, inner_ref, gate_ref, state_ref, step_ref):
    j = pl.program_id(0)
    rows = act_ref.shape[0]
    chunk = 1024

    def run(w_ref, out_ref):
        @pl.loop(0, rows // chunk)
        def _(m):
            at = pl.ds(pl.multiple_of(m * chunk, chunk), chunk)
            out_ref[at, :] = jnp.dot(act_ref[at, :], w_ref[...], preferred_element_type=F32).astype(out_ref.dtype)

    @pl.when(j == 0)
    def _():
        run(ws_ref, state_ref)
        run(wd_ref, step_ref)

    @pl.when((j > 0) & (j <= steps))
    def _():
        run(wi_ref, inner_ref)

    @pl.when(j > steps)
    def _():
        run(wg_ref, gate_ref)


def project(act, wi, wg, ws, wd):
    rows, depth = act.shape
    width = wi.shape[1]
    steps = width // TILE

    def at_inner(j):
        return (0, jnp.clip(j - 1, 0, steps - 1))

    def at_gate(j):
        return (0, jnp.clip(j - 1 - steps, 0, steps - 1))

    flops = 2 * rows * depth * (2 * width + ws.shape[1] + wd.shape[1])
    return pl.pallas_call(
        functools.partial(project_kernel, steps),
        out_shape=(
            jax.ShapeDtypeStruct((rows, width), BF16),
            jax.ShapeDtypeStruct((rows, width), BF16),
            jax.ShapeDtypeStruct((rows, ws.shape[1]), BF16),
            jax.ShapeDtypeStruct((rows, wd.shape[1]), F32),
        ),
        grid=(1 + 2 * steps,),
        in_specs=[
            full((rows, depth), pipeline_mode=pl.Buffered(1)),
            pl.BlockSpec((depth, TILE), at_inner),
            pl.BlockSpec((depth, TILE), at_gate),
            full(ws.shape, pipeline_mode=pl.Buffered(1)),
            full(wd.shape, pipeline_mode=pl.Buffered(1)),
        ],
        out_specs=(
            pl.BlockSpec((rows, TILE), at_inner),
            pl.BlockSpec((rows, TILE), at_gate),
            full((rows, ws.shape[1])),
            full((rows, wd.shape[1])),
        ),
        compiler_params=pltpu.CompilerParams(vmem_limit_bytes=60 * MIB),
        cost_estimate=pl.CostEstimate(flops=flops, bytes_accessed=32 * MIB, transcendentals=0),
        name="project",
    )(act, wi, wg, ws, wd)


def ssd_kernel(
    inner_ref,
    gate_ref,
    state_ref,
    step_ref,
    hist_ref,
    ik_ref,
    sk_ref,
    bias_ref,
    decay_ref,
    skip_ref,
    az_ref,
    ez_ref,
    c_ref,
    f1_ref,
    small_ref,
    first_ref,
    u_ref,
    v_ref,
):
    seq, width = inner_ref.shape
    heads = step_ref.shape[1]
    p = width // heads
    taps = ik_ref.shape[0]
    lag = taps - 1
    n = state_ref.shape[1] // 2
    lead = 8 - lag
    half = seq // 2

    v_ref[lead:8, :] = hist_ref[0].astype(F32)
    v_ref[8:, :] = state_ref[...].astype(F32)
    sk = sk_ref[...].astype(F32)
    run = jnp.zeros((seq, 2 * n), F32)
    for k in range(taps):
        run = run + sk[k : k + 1] * v_ref[lead + k : lead + k + seq, :]
    conv = silu(run).astype(BF16)
    b = conv[:, :n]
    c = conv[:, n:]
    c_ref[:, :n] = c
    small_ref[0, 2 * heads :] = b[:16].astype(F32)[:8]

    raw = step_ref[...] + bias_ref[...]
    dt = jnp.maximum(raw, 0.0) + jnp.log1p(jnp.exp(-jnp.abs(raw)))
    dt = jnp.concatenate([dt, jnp.zeros((seq, 128 - heads), F32)], axis=1)
    decay = jnp.concatenate([decay_ref[...], jnp.zeros((1, 128 - heads), F32)], axis=1)
    t_at = lax.broadcasted_iota(jnp.int32, (seq, seq), 0)
    s_at = lax.broadcasted_iota(jnp.int32, (seq, seq), 1)
    causal = s_at <= t_at
    cum = jnp.dot(
        causal.astype(F32), -decay * dt, preferred_element_type=F32, precision=lax.Precision.HIGHEST
    )
    cum_t = cum.T
    dt_t = dt.T
    begin = cum[lag - 1 : lag]
    last = cum[seq - 1 : seq]
    spread = (
        lax.broadcasted_iota(jnp.int32, (128, width), 1) // p
        == lax.broadcasted_iota(jnp.int32, (128, width), 0)
    )
    spread = spread.astype(F32).astype(BF16)
    early = lax.broadcasted_iota(jnp.int32, (seq, 128), 0) < lag
    grown = jnp.exp(jnp.where(early, cum, jnp.minimum(cum - begin, 0.0))).astype(BF16)
    tail = jnp.exp(jnp.minimum(last - cum, 0.0)) * dt
    begin_t = cum_t[:heads, lag - 1 : lag]
    last_t = cum_t[:heads, seq - 1 : seq]
    small_ref[0, :heads] = jnp.broadcast_to(jnp.exp(jnp.minimum(last_t - begin_t, 0.0)), (heads, n))
    small_ref[0, heads : 2 * heads] = jnp.broadcast_to(jnp.exp(begin_t), (heads, n))

    scores = lax.dot_general(c, b, (((1,), (1,)), ((), ())), preferred_element_type=F32)
    scores = jnp.where(causal, scores, 0.0)
    own = scores[:, :n]
    seen = (lax.broadcasted_iota(jnp.int32, own.shape, 1) < lag) & (
        lax.broadcasted_iota(jnp.int32, own.shape, 0) >= lag
    )
    c_ref[:, n:] = pltpu.roll(jnp.where(seen, own, 0.0), 8 * pl.program_id(0), 1).astype(BF16)
    top = scores[:half, :half]
    bottom = scores[half:]

    row8 = lax.broadcasted_iota(jnp.int32, (8, 128), 0)
    cum8 = cum[:8]
    dt8 = dt[:8]
    small = [jnp.where(row8 < lag, jnp.exp(jnp.minimum(begin - cum8, 0.0)) * dt8, 0.0).astype(BF16)]
    for j in range(lag):
        rows = []
        for t in range(8):
            if j <= t < lag:
                s = t - j
                gap = jnp.exp(jnp.minimum(cum[t : t + 1] - cum[s : s + 1], 0.0))
                rows.append(gap * scores[t : t + 1, s : s + 1] * dt[s : s + 1])
            else:
                rows.append(jnp.zeros((1, 128), F32))
        small.append(jnp.concatenate(rows, axis=0).astype(BF16))
    small = jnp.concatenate([m.astype(F32) for m in small], axis=0).astype(BF16)

    u_ref[:8, :] = jnp.zeros((8, width), F32)
    u_ref[8:, :] = inner_ref[...].astype(F32)
    lane = lax.broadcasted_iota(jnp.int32, (1, 128), 1)
    for q in range(width // 128):
        cols = slice(q * 128, q * 128 + 128)
        ik = ik_ref[:, cols].astype(F32)
        run = jnp.zeros((seq, 128), F32)
        for k in range(taps):
            run = run + ik[k : k + 1] * u_ref[lead + k : lead + k + seq, cols]
        x = jnp.where(early, 0.0, silu(run)).astype(BF16)
        xf = x.astype(F32)
        y_top = jnp.zeros((half, 128), F32)
        y_bottom = jnp.zeros((seq - half, 128), F32)
        for s in range(128 // p):
            h = q * (128 // p) + s
            own = (lane >= s * p) & (lane < (s + 1) * p)
            xs = jnp.where(own, xf, 0.0).astype(BF16)
            col = cum[:, h : h + 1]
            row = cum_t[h : h + 1]
            dr = dt_t[h : h + 1]
            w_top = jnp.exp(jnp.minimum(col[:half] - row[:, :half], 0.0)) * (top * dr[:, :half])
            w_bottom = jnp.exp(jnp.minimum(col[half:] - row, 0.0)) * (bottom * dr)
            y_top = y_top + jnp.dot(w_top.astype(BF16), xs[:half], preferred_element_type=F32)
            y_bottom = y_bottom + jnp.dot(w_bottom.astype(BF16), xs, preferred_element_type=F32)
        skip = skip_ref[:, cols]
        y = jnp.concatenate([y_top, y_bottom], axis=0) + skip * xf
        z = silu(gate_ref[:, cols].astype(F32))
        az_ref[:, cols] = (y * z).astype(BF16)
        ez = jnp.dot(grown, spread[:, cols], preferred_element_type=F32) * z
        ez_ref[:, cols] = ez.astype(BF16)
        tw = jnp.dot(tail.astype(BF16), spread[:, cols], preferred_element_type=F32)
        xt = (xf * tw).astype(BF16)
        f1_ref[0, cols, :] = lax.dot_general(
            xt, b, (((0,), (0,)), ((), ())), preferred_element_type=F32
        )
        wide = jnp.dot(small, spread[:, cols], preferred_element_type=F32)
        first_ref[0, 0:8, cols] = run[:8]
        first_ref[0, 16 + 8 * lag : 16 + 8 * lag + taps, cols] = ik
        first_ref[0, 8:16, cols] = wide[:8]
        z8 = z[:8]
        first_ref[0, 16:24, cols] = jnp.where(row8 < lag, (wide[8:16] + skip) * z8, 0.0)
        for j in range(1, lag):
            first_ref[0, 16 + 8 * j : 24 + 8 * j, cols] = wide[8 + 8 * j : 16 + 8 * j] * z8


def ssd(inner, gate, state, step, history, ik, sk, bias, decay, skip):
    tokens, width = inner.shape
    requests = history.shape[0]
    seq = tokens // requests
    heads = step.shape[1]
    n2 = state.shape[1]
    n = n2 // 2
    lag = ik.shape[0] - 1
    rows = lambda w: pl.BlockSpec((seq, w), lambda r: (r, 0))
    per = lambda *s: pl.BlockSpec((1,) + s, lambda r: (r,) + (0,) * len(s))
    return pl.pallas_call(
        ssd_kernel,
        out_shape=(
            pltpu.VMEM((tokens, width), BF16),
            pltpu.HBM((tokens, width), BF16),
            pltpu.VMEM((tokens, 2 * n), BF16),
            pltpu.HBM((requests, width, n), F32),
            pltpu.VMEM((requests, 2 * heads + 8, n), F32),
            pltpu.VMEM((requests, 24 + 8 * lag, width), F32),
        ),
        grid=(requests,),
        in_specs=[
            rows(width),
            rows(width),
            rows(n2),
            rows(heads),
            per(*history.shape[1:]),
            full(ik.shape),
            full(sk.shape),
            full(bias.shape),
            full(decay.shape),
            full(skip.shape),
        ],
        out_specs=(
            rows(width),
            rows(width),
            rows(2 * n),
            per(width, n),
            per(2 * heads + 8, n),
            per(24 + 8 * lag, width),
        ),
        scratch_shapes=[pltpu.VMEM((seq + 8, width), F32), pltpu.VMEM((seq + 8, n2), F32)],
        compiler_params=pltpu.CompilerParams(vmem_limit_bytes=40 * MIB),
        cost_estimate=pl.CostEstimate(
            flops=2 * tokens * width * seq * 2, bytes_accessed=14 * MIB, transcendentals=tokens * seq * heads
        ),
        name="ssd",
    )(*in_hbm(inner, gate, state, step), history, ik, sk, bias, decay, skip)


def first_sources(grow_ref, small_ref, r):
    requests = small_ref.shape[0]
    b = small_ref[r, small_ref.shape[1] - 8 :]
    zero = jnp.zeros_like(b)
    b = jnp.concatenate([b if i == r else zero for i in range(requests)], axis=0).astype(BF16)
    return jnp.dot(grow_ref[...], b, preferred_element_type=F32)


def tail_kernel(
    pos_hbm,
    back_ref,
    ez_hbm,
    f1_hbm,
    az_ref,
    c_ref,
    small_ref,
    first_ref,
    g_ref,
    sq_ref,
    grow_ref,
    held_ref,
    f1_ref,
    pos_ref,
    ez_ref,
    rows_ref,
    s_ref,
    raw_ref,
    win_ref,
    mix_ref,
    x_ref,
    extra_ref,
    sem,
    ez_sem,
    once_sem,
):
    requests = first_ref.shape[0]
    heads = (small_ref.shape[1] - 8) // 2
    p = held_ref.shape[1]
    tokens, width = g_ref.shape
    seq = tokens // requests
    lag = (first_ref.shape[1] - 24) // 8
    pairs = heads // 2

    def rows_of(r):
        return slice(r * seq, r * seq + seq)

    batch = requests // 2

    def ez_copy(i):
        rows = slice(i * batch * seq, (i + 1) * batch * seq)
        return pltpu.make_async_copy(ez_hbm.at[rows], ez_ref.at[rows], ez_sem.at[i])

    def fetch(i):
        for e in range(i * batch * heads, (i + 1) * batch * heads):
            at = pos_ref[e]
            pltpu.make_async_copy(
                back_ref.at[at // CAP, pl.ds(pl.multiple_of((at % CAP) * p, p), p)],
                held_ref.at[e],
                sem.at[i],
            ).start()

    row_copy = pltpu.make_async_copy(back_ref.at[:, CAP * p :], rows_ref, once_sem.at[0])
    f1_copy = pltpu.make_async_copy(f1_hbm, f1_ref, once_sem.at[1])
    pos_copy = pltpu.make_async_copy(pos_hbm, pos_ref, once_sem.at[2])
    pos_copy.start()
    row_copy.start()
    ez_copy(0).start()
    win_ref[...] = jnp.zeros_like(win_ref)
    x_ref[...] = jnp.zeros_like(x_ref)
    pos_copy.wait()
    fetch(0)
    ez_copy(1).start()
    fetch(1)
    f1_copy.start()
    row_copy.wait()

    low = lax.broadcasted_iota(jnp.int32, (1, 128), 1) < p
    flat = rows_ref.reshape(rows_ref.shape[0] * rows_ref.shape[1], 128)
    for i in range(requests):
        for q in range(pairs):
            cols = slice(q * 128, q * 128 + 128)
            even = 2 * pos_ref[i * heads + 2 * q]
            odd = 2 * pos_ref[i * heads + 2 * q + 1]
            a0, a1 = flat[pl.ds(even, 1)], flat[pl.ds(odd, 1)]
            b0, b1 = flat[pl.ds(even + 1, 1)], flat[pl.ds(odd + 1, 1)]
            win_ref[i, 0:1, cols] = jnp.where(low, a0, a1)
            win_ref[i, 2:3, cols] = jnp.where(low, b0, b1)
            mix_ref[i * pairs + q : i * pairs + q + 1] = jnp.where(low, a1, a0)
    mix = pltpu.roll(mix_ref[...], p, 1)
    for i in range(requests):
        for q in range(pairs):
            win_ref[i, 1:2, q * 128 : q * 128 + 128] = mix[i * pairs + q : i * pairs + q + 1]

    run = first_ref[:, 0:8]
    for k in range(lag):
        at = 16 + 8 * lag + k
        run = run + first_ref[:, at : at + 1] * win_ref[:, k : k + 8]
    row8 = lax.broadcasted_iota(jnp.int32, run.shape, 1)
    x = jnp.where(row8 < lag, silu(run), 0.0).astype(BF16).astype(F32)
    x_ref[:, 8:16] = x
    extra = first_ref[:, 16:24] * x
    for j in range(1, lag):
        extra = extra + first_ref[:, 16 + 8 * j : 24 + 8 * j] * x_ref[:, 8 - j : 16 - j]
    extra_ref[...] = extra
    grow = (x * first_ref[:, 8:16]).reshape(requests * 8, width).T
    grow_ref[...] = grow.astype(BF16)
    n = c_ref.shape[1] // 2
    grow = jnp.concatenate([grow, jnp.zeros((width, n - requests * 8), F32)], axis=1).astype(BF16)
    s_ref[0, :, n:] = grow
    s_ref[1, :, n:] = grow

    row16 = lax.broadcasted_iota(jnp.int32, (16, 256), 0)
    nt = (((1,), (1,)), ((), ()))
    squares = []
    for r in range(requests):
        rows = rows_of(r)
        if r % batch == 0:
            part = held_ref.at[r * heads : (r + batch) * heads]
            pltpu.make_async_copy(part, part, sem.at[r // batch]).wait()
            ez_copy(r // batch).wait()
        for h in range(heads):
            at = slice(h * p, h * p + p)
            block = held_ref[r * heads + h]
            raw_ref[r % 2, at] = block.astype(BF16)
            s_ref[r % 2, at, :n] = (small_ref[r, heads + h : heads + h + 1] * block).astype(BF16)
        c = c_ref[rows]
        total = jnp.zeros((seq - 16, 128), F32)
        total16 = jnp.zeros((16, 128), F32)
        for q in range(width // 256):
            cols = slice(q * 256, q * 256 + 256)
            seen = lax.dot_general(c, s_ref[r % 2, cols], nt, preferred_element_type=F32)
            seen16 = lax.dot_general(c[:16, :n], raw_ref[r % 2, cols], nt, preferred_element_type=F32)
            seen16 = jnp.where(row16 < lag, seen16, seen[:16])
            az = az_ref[rows, cols].astype(F32)
            ez = ez_ref[rows, cols].astype(F32)
            g = az[16:] + ez[16:] * seen[16:]
            g16 = az[:16] + ez[:16] * seen16
            g16 = g16 + jnp.concatenate([extra_ref[r, :, cols], jnp.zeros((8, 256), F32)], axis=0)
            g_ref[r * seq : r * seq + 16, cols] = g16.astype(BF16)
            g_ref[r * seq + 16 : r * seq + seq, cols] = g.astype(BF16)
            g = g * g
            g16 = g16 * g16
            total = total + g[:, :128] + g[:, 128:]
            total16 = total16 + g16[:, :128] + g16[:, 128:]
        total = jnp.concatenate([total16, total], axis=0)
        squares.append(jnp.sum(total.T, axis=0, keepdims=True))
    squares.append(jnp.zeros((8 - requests, seq), F32))
    sq_ref[...] = jnp.concatenate(squares, axis=0)
    f1_copy.wait()


def tail(pos, back, ez, f1, az, c, small, first):
    requests, packed, n = small.shape
    heads = (packed - 8) // 2
    assert requests * 8 <= n
    tokens, width = az.shape
    p = width // heads
    seq = tokens // requests
    owners = back.shape[0]
    vmem = pl.BlockSpec(memory_space=pltpu.VMEM)
    hbm = pl.BlockSpec(memory_space=pltpu.HBM)
    return pl.pallas_call(
        tail_kernel,
        out_shape=(
            pltpu.VMEM((tokens, width), BF16),
            pltpu.VMEM((8, seq), F32),
            pltpu.VMEM((width, requests * 8), BF16),
            pltpu.VMEM((requests * heads, p, n), F32),
            pltpu.VMEM(f1.shape, F32),
        ),
        in_specs=[hbm] * 4 + [vmem] * 4,
        out_specs=(vmem,) * 5,
        scratch_shapes=[
            pltpu.SMEM(pos.shape, jnp.int32),
            pltpu.VMEM((tokens, width), BF16),
            pltpu.VMEM((owners, 2 * CAP, n), F32),
            pltpu.VMEM((2, width, 2 * n), BF16),
            pltpu.VMEM((2, width, n), BF16),
            pltpu.VMEM((requests, 16, width), F32),
            pltpu.VMEM((requests * heads // 2, 128), F32),
            pltpu.VMEM((requests, 16, width), F32),
            pltpu.VMEM((requests, 8, width), F32),
            pltpu.SemaphoreType.DMA((2,)),
            pltpu.SemaphoreType.DMA((2,)),
            pltpu.SemaphoreType.DMA((3,)),
        ],
        compiler_params=pltpu.CompilerParams(vmem_limit_bytes=24 * MIB),
        cost_estimate=pl.CostEstimate(
            flops=2 * tokens * width * n, bytes_accessed=10 * MIB, transcendentals=0
        ),
        name="tail",
    )(*in_hbm(pos, back, ez, f1), *in_vmem(az, c, small, first))


def final_kernel(held_ref, grow_ref, small_ref, f1_ref, out_ref, made_ref, sem):
    requests, heads, p = out_ref.shape[:3]

    def copy(r):
        return pltpu.make_async_copy(made_ref.at[r], out_ref.at[r], sem.at[r])

    for r in range(requests):
        add = first_sources(grow_ref, small_ref, r)
        for h in range(heads):
            at = slice(h * p, h * p + p)
            block = small_ref[r, heads + h : heads + h + 1] * held_ref[r * heads + h] + add[at]
            made_ref[r, h] = small_ref[r, h : h + 1] * block + f1_ref[r, at]
        copy(r).start()
    for r in range(requests):
        copy(r).wait()


def finals(held, grow, small, f1):
    requests, width, n = f1.shape
    heads = (small.shape[1] - 8) // 2
    p = width // heads
    vmem = pl.BlockSpec(memory_space=pltpu.VMEM)
    return pl.pallas_call(
        final_kernel,
        out_shape=jax.ShapeDtypeStruct((requests, heads, p, n), F32),
        in_specs=[vmem] * 4,
        out_specs=pl.BlockSpec(memory_space=pltpu.HBM),
        scratch_shapes=[
            pltpu.VMEM((requests, heads, p, n), F32),
            pltpu.SemaphoreType.DMA((requests,)),
        ],
        compiler_params=pltpu.CompilerParams(vmem_limit_bytes=16 * MIB),
        cost_estimate=pl.CostEstimate(
            flops=2 * requests * width * n * 32, bytes_accessed=6 * MIB, transcendentals=0
        ),
        name="finals",
    )(*in_vmem(held, grow, small, f1))


def norm_kernel(channels, g_ref, s0_ref, s1_ref, s2_ref, s3_ref, gain_ref, out_ref, made_ref, sem):
    tokens, width = g_ref.shape
    seq = s0_ref.shape[1]
    step = 128
    gain = gain_ref[...].astype(F32)
    square = s0_ref[...] + s1_ref[...] + s2_ref[...] + s3_ref[...]
    scale = lax.rsqrt(square / channels + EPSILON)

    def copy(i):
        rows = slice(i * step, i * step + step)
        return pltpu.make_async_copy(made_ref.at[rows], out_ref.at[rows], sem.at[i])

    for i in range(tokens // step):
        rows = slice(i * step, i * step + step)
        r, at = i * step // seq, i * step % seq
        wide = jnp.broadcast_to(scale[r : r + 1, at : at + step], (128, step)).T
        for q in range(width // 128):
            cols = slice(q * 128, q * 128 + 128)
            made_ref[rows, cols] = (g_ref[rows, cols].astype(F32) * wide * gain[:, cols]).astype(BF16)
        copy(i).start()
    for i in range(tokens // step):
        copy(i).wait()


def normalise(g, parts, gain, channels):
    tokens, width = g.shape
    vmem = pl.BlockSpec(memory_space=pltpu.VMEM)
    return pl.pallas_call(
        functools.partial(norm_kernel, channels),
        out_shape=jax.ShapeDtypeStruct((tokens, width), BF16),
        in_specs=[vmem] * 6,
        out_specs=pl.BlockSpec(memory_space=pltpu.HBM),
        scratch_shapes=[pltpu.VMEM((tokens, width), BF16), pltpu.SemaphoreType.DMA((tokens // 128,))],
        compiler_params=pltpu.CompilerParams(vmem_limit_bytes=8 * MIB),
        cost_estimate=pl.CostEstimate(flops=2 * tokens * width, bytes_accessed=4 * MIB, transcendentals=0),
        name="normalise",
    )(g, *parts, gain)


def local(
    activations,
    gate_weight,
    inner_weight,
    state_proj,
    step_weight,
    inner_kernel,
    state_kernel,
    step_bias,
    decay_rate,
    skip_scale,
    norm_gain,
    scan_cache,
    window_cache,
    state_history,
    hit_owner,
    hit_slot,
):
    owners = lax.axis_size("dp")
    groups = lax.axis_size("mp")
    requests, heads = hit_owner.shape
    slots, _, p, n = scan_cache.shape
    width = inner_weight.shape[1]
    blocks = slots * heads

    cache = scan_cache.reshape(blocks, p, n)
    wanted, pos, cache, wa, wb = prep(hit_owner, hit_slot, cache, window_cache.reshape(blocks, -1), owners)
    codes = lax.all_to_all(wanted, "dp", split_axis=0, concat_axis=0, tiled=True)
    sent = pick(codes, cache, wa, wb)
    back = lax.all_to_all(sent, "dp", split_axis=0, concat_axis=0, tiled=True)

    inner, gate, state, step = project(activations, inner_weight, gate_weight, state_proj, step_weight)
    az, ez, c, f1, small, first = ssd(
        inner,
        gate,
        state,
        step,
        state_history,
        inner_kernel,
        state_kernel,
        step_bias[None],
        decay_rate[None],
        jnp.repeat(skip_scale, p)[None],
    )
    g, square, grow, held, f1 = tail(pos, back, ez, f1, az, c, small, first)
    final = finals(held, grow, small, f1)
    pair = [(i, i ^ 1) for i in range(groups)]
    square = square + lax.ppermute(square, "mp", pair)
    parts = [square] + [
        lax.ppermute(square, "mp", [(i, (i + 2 * s) % groups) for i in range(groups)])
        for s in range(1, groups // 2)
    ]
    normed = normalise(g, parts, norm_gain[None], width * groups)
    return normed, final


def solution(mesh):
    placed = (
        P("dp", None),
        P(None, "mp"),
        P(None, "mp"),
        P(),
        P(None, "mp"),
        P(None, "mp"),
        P(),
        P("mp"),
        P("mp"),
        P("mp"),
        P("mp"),
        P("dp", "mp", None, None),
        P("dp", "mp", None),
        P("dp", None, None),
        P("dp", "mp"),
        P("dp", "mp"),
    )
    return jax.shard_map(
        local,
        mesh=mesh,
        in_specs=placed,
        out_specs=(P("dp", "mp"), P("dp", "mp", None, None)),
        check_vma=False,
    )
```

```python
import functools

import jax
import jax.numpy as jnp
from jax import lax
from jax.experimental import pallas as pl
from jax.experimental.pallas import tpu as pltpu
from jax.sharding import PartitionSpec as P

EPSILON = 1e-05
CAP = 8
F32 = jnp.float32
BF16 = jnp.bfloat16
MIB = 1024 * 1024


def silu(v):
    half = 0.5 * v
    return half + half * jnp.tanh(half)


def full(shape, **kw):
    return pl.BlockSpec(shape, lambda *_: (0,) * len(shape), **kw)


def in_hbm(*arrays):
    return [pltpu.with_memory_space_constraint(v, pltpu.HBM) for v in arrays]


def in_vmem(*arrays):
    return [pltpu.with_memory_space_constraint(v, pltpu.VMEM) for v in arrays]


def prep_kernel(
    owner_hbm,
    slot_hbm,
    cache_hbm,
    window_hbm,
    wanted_hbm,
    pos_hbm,
    cache_ref,
    wa_ref,
    wb_ref,
    owner_ref,
    slot_ref,
    wanted_ref,
    pos_ref,
    count_ref,
    window_ref,
    sem,
):
    owners = wanted_ref.shape[0]
    requests, heads = owner_ref.shape
    tables = [
        pltpu.make_async_copy(owner_hbm, owner_ref, sem.at[4]),
        pltpu.make_async_copy(slot_hbm, slot_ref, sem.at[5]),
    ]
    for copy in tables:
        copy.start()
    cache_copy = pltpu.make_async_copy(cache_hbm, cache_ref, sem.at[1])
    cache_copy.start()
    window_copy = pltpu.make_async_copy(window_hbm, window_ref, sem.at[0])
    window_copy.start()
    for o in range(owners):
        count_ref[o] = 0
        for k in range(CAP):
            wanted_ref[o, 0, k] = 0
    for copy in tables:
        copy.wait()
    for r in range(requests):
        for h in range(heads):
            o = owner_ref[r, h]
            k = count_ref[o]
            count_ref[o] = k + 1
            wanted_ref[o, 0, k] = slot_ref[r, h] * heads + h
            pos_ref[r * heads + h] = o * CAP + k
    for o in range(owners):
        wanted_ref[o, 0, CAP] = count_ref[o]
    wanted_copy = pltpu.make_async_copy(wanted_ref, wanted_hbm, sem.at[2])
    wanted_copy.start()
    pos_copy = pltpu.make_async_copy(pos_ref, pos_hbm, sem.at[3])
    pos_copy.start()
    window_copy.wait()
    half = window_ref.shape[1] // 3
    w = window_ref[...].astype(F32)
    first = w[:, : 2 * half]
    second = jnp.concatenate([w[:, 2 * half :], jnp.zeros((w.shape[0], half), F32)], axis=1)
    odd = lax.broadcasted_iota(jnp.int32, first.shape, 0) % 2 == 1
    wa_ref[...] = jnp.where(odd, pltpu.roll(first, half, 1), first)
    wb_ref[...] = jnp.where(odd, pltpu.roll(second, half, 1), second)
    wanted_copy.wait()
    pos_copy.wait()
    cache_copy.wait()


def prep(hit_owner, hit_slot, cache, window, owners):
    entries = hit_owner.size
    vmem = pl.BlockSpec(memory_space=pltpu.VMEM)
    hbm = pl.BlockSpec(memory_space=pltpu.HBM)
    blocks, p, n = cache.shape
    return pl.pallas_call(
        prep_kernel,
        out_shape=(
            pltpu.HBM((owners, 1, 128), jnp.int32),
            pltpu.HBM((entries,), jnp.int32),
            pltpu.VMEM((blocks, p, n), F32),
            pltpu.VMEM((blocks, n), F32),
            pltpu.VMEM((blocks, n), F32),
        ),
        in_specs=[hbm] * 4,
        out_specs=(hbm, hbm, vmem, vmem, vmem),
        scratch_shapes=[
            pltpu.SMEM(hit_owner.shape, jnp.int32),
            pltpu.SMEM(hit_slot.shape, jnp.int32),
            pltpu.SMEM((owners, 1, 128), jnp.int32),
            pltpu.SMEM((entries,), jnp.int32),
            pltpu.SMEM((owners,), jnp.int32),
            pltpu.VMEM(window.shape, window.dtype),
            pltpu.SemaphoreType.DMA((6,)),
        ],
        compiler_params=pltpu.CompilerParams(vmem_limit_bytes=8 * MIB),
        name="prep",
    )(*in_hbm(hit_owner, hit_slot, cache, window))


def pick_kernel(codes_ref, cache_ref, wa_ref, wb_ref, out_ref, rows_ref, extra_ref, sem, extra_sem):
    owners = out_ref.shape[0]
    p = cache_ref.shape[1]
    cached = CAP * p
    always = CAP // 2
    extra_ref[0] = 0

    @pl.loop(0, owners, unroll=4)
    def _(d):
        for k in range(always):
            pltpu.make_async_copy(
                cache_ref.at[codes_ref[d, 0, k]], out_ref.at[d, k * p : k * p + p], sem
            ).start()
        count = codes_ref[d, 0, CAP]

        @pl.when(count > always)
        def _():
            extra_ref[0] += count - always

            @pl.loop(always, count)
            def _(k):
                pltpu.make_async_copy(
                    cache_ref.at[codes_ref[d, 0, k]],
                    out_ref.at[d, pl.ds(pl.multiple_of(k * p, p), p)],
                    extra_sem,
                ).start()

    @pl.loop(0, owners, unroll=4)
    def _(d):
        for k in range(CAP):
            at = pl.ds(codes_ref[d, 0, k], 1)
            rows_ref[d, 2 * k : 2 * k + 1] = wa_ref[at]
            rows_ref[d, 2 * k + 1 : 2 * k + 2] = wb_ref[at]

    pltpu.make_async_copy(rows_ref, out_ref.at[:, cached:], sem).start()

    @pl.loop(0, extra_ref[0])
    def _(_):
        pltpu.make_async_copy(cache_ref.at[0], out_ref.at[0, :p], extra_sem).wait()

    done = out_ref.at[:, : always * p + 2 * CAP]
    pltpu.make_async_copy(done, done, sem).wait()


def pick(codes, cache, wa, wb):
    owners = codes.shape[0]
    blocks, p, n = cache.shape
    vmem = pl.BlockSpec(memory_space=pltpu.VMEM)
    hbm = pl.BlockSpec(memory_space=pltpu.HBM)
    return pl.pallas_call(
        pick_kernel,
        out_shape=pltpu.HBM((owners, CAP * p + 2 * CAP, n), F32),
        in_specs=[pl.BlockSpec(memory_space=pltpu.SMEM), vmem, vmem, vmem],
        out_specs=hbm,
        scratch_shapes=[
            pltpu.VMEM((owners, 2 * CAP, n), F32),
            pltpu.SMEM((1,), jnp.int32),
            pltpu.SemaphoreType.DMA,
            pltpu.SemaphoreType.DMA,
        ],
        compiler_params=pltpu.CompilerParams(vmem_limit_bytes=8 * MIB),
        cost_estimate=pl.CostEstimate(flops=0, bytes_accessed=8 * MIB, transcendentals=0),
        name="pick",
    )(codes, *in_vmem(cache, wa, wb))


TILE = 256


def project_kernel(steps, act_ref, wi_ref, wg_ref, ws_ref, wd_ref, inner_ref, gate_ref, state_ref, step_ref):
    j = pl.program_id(0)
    rows = act_ref.shape[0]
    chunk = 1024

    def run(w_ref, out_ref):
        @pl.loop(0, rows // chunk)
        def _(m):
            at = pl.ds(pl.multiple_of(m * chunk, chunk), chunk)
            out_ref[at, :] = jnp.dot(act_ref[at, :], w_ref[...], preferred_element_type=F32).astype(out_ref.dtype)

    @pl.when(j == 0)
    def _():
        run(ws_ref, state_ref)
        run(wd_ref, step_ref)

    @pl.when((j > 0) & (j <= steps))
    def _():
        run(wi_ref, inner_ref)

    @pl.when(j > steps)
    def _():
        run(wg_ref, gate_ref)


def project(act, wi, wg, ws, wd):
    rows, depth = act.shape
    width = wi.shape[1]
    steps = width // TILE

    def at_inner(j):
        return (0, jnp.clip(j - 1, 0, steps - 1))

    def at_gate(j):
        return (0, jnp.clip(j - 1 - steps, 0, steps - 1))

    flops = 2 * rows * depth * (2 * width + ws.shape[1] + wd.shape[1])
    return pl.pallas_call(
        functools.partial(project_kernel, steps),
        out_shape=(
            jax.ShapeDtypeStruct((rows, width), BF16),
            jax.ShapeDtypeStruct((rows, width), BF16),
            jax.ShapeDtypeStruct((rows, ws.shape[1]), BF16),
            jax.ShapeDtypeStruct((rows, wd.shape[1]), F32),
        ),
        grid=(1 + 2 * steps,),
        in_specs=[
            full((rows, depth), pipeline_mode=pl.Buffered(1)),
            pl.BlockSpec((depth, TILE), at_inner),
            pl.BlockSpec((depth, TILE), at_gate),
            full(ws.shape, pipeline_mode=pl.Buffered(1)),
            full(wd.shape, pipeline_mode=pl.Buffered(1)),
        ],
        out_specs=(
            pl.BlockSpec((rows, TILE), at_inner),
            pl.BlockSpec((rows, TILE), at_gate),
            full((rows, ws.shape[1])),
            full((rows, wd.shape[1])),
        ),
        compiler_params=pltpu.CompilerParams(vmem_limit_bytes=60 * MIB),
        cost_estimate=pl.CostEstimate(flops=flops, bytes_accessed=32 * MIB, transcendentals=0),
        name="project",
    )(act, wi, wg, ws, wd)


def ssd_kernel(
    inner_ref,
    gate_ref,
    state_ref,
    step_ref,
    hist_ref,
    ik_ref,
    sk_ref,
    bias_ref,
    decay_ref,
    skip_ref,
    az_ref,
    ez_ref,
    c_ref,
    f1_ref,
    small_ref,
    first_ref,
    u_ref,
    v_ref,
):
    seq, width = inner_ref.shape
    heads = step_ref.shape[1]
    p = width // heads
    taps = ik_ref.shape[0]
    lag = taps - 1
    n = state_ref.shape[1] // 2
    lead = 8 - lag
    half = seq // 2

    v_ref[lead:8, :] = hist_ref[0].astype(F32)
    v_ref[8:, :] = state_ref[...].astype(F32)
    sk = sk_ref[...].astype(F32)
    run = jnp.zeros((seq, 2 * n), F32)
    for k in range(taps):
        run = run + sk[k : k + 1] * v_ref[lead + k : lead + k + seq, :]
    conv = silu(run).astype(BF16)
    b = conv[:, :n]
    c = conv[:, n:]
    c_ref[:, :n] = c
    small_ref[0, 2 * heads :] = b[:16].astype(F32)[:8]

    raw = step_ref[...] + bias_ref[...]
    dt = jnp.maximum(raw, 0.0) + jnp.log1p(jnp.exp(-jnp.abs(raw)))
    dt = jnp.concatenate([dt, jnp.zeros((seq, 128 - heads), F32)], axis=1)
    decay = jnp.concatenate([decay_ref[...], jnp.zeros((1, 128 - heads), F32)], axis=1)
    t_at = lax.broadcasted_iota(jnp.int32, (seq, seq), 0)
    s_at = lax.broadcasted_iota(jnp.int32, (seq, seq), 1)
    causal = s_at <= t_at
    cum = jnp.dot(
        causal.astype(F32), -decay * dt, preferred_element_type=F32, precision=lax.Precision.HIGHEST
    )
    cum_t = cum.T
    dt_t = dt.T
    begin = cum[lag - 1 : lag]
    last = cum[seq - 1 : seq]
    spread = (
        lax.broadcasted_iota(jnp.int32, (128, width), 1) // p
        == lax.broadcasted_iota(jnp.int32, (128, width), 0)
    )
    spread = spread.astype(F32).astype(BF16)
    early = lax.broadcasted_iota(jnp.int32, (seq, 128), 0) < lag
    grown = jnp.exp(jnp.where(early, cum, jnp.minimum(cum - begin, 0.0))).astype(BF16)
    tail = jnp.exp(jnp.minimum(last - cum, 0.0)) * dt
    begin_t = cum_t[:heads, lag - 1 : lag]
    last_t = cum_t[:heads, seq - 1 : seq]
    small_ref[0, :heads] = jnp.broadcast_to(jnp.exp(jnp.minimum(last_t - begin_t, 0.0)), (heads, n))
    small_ref[0, heads : 2 * heads] = jnp.broadcast_to(jnp.exp(begin_t), (heads, n))

    scores = lax.dot_general(c, b, (((1,), (1,)), ((), ())), preferred_element_type=F32)
    scores = jnp.where(causal, scores, 0.0)
    own = scores[:, :n]
    seen = (lax.broadcasted_iota(jnp.int32, own.shape, 1) < lag) & (
        lax.broadcasted_iota(jnp.int32, own.shape, 0) >= lag
    )
    c_ref[:, n:] = pltpu.roll(jnp.where(seen, own, 0.0), 8 * pl.program_id(0), 1).astype(BF16)
    top = scores[:half, :half]
    bottom = scores[half:]

    row8 = lax.broadcasted_iota(jnp.int32, (8, 128), 0)
    cum8 = cum[:8]
    dt8 = dt[:8]
    small = [jnp.where(row8 < lag, jnp.exp(jnp.minimum(begin - cum8, 0.0)) * dt8, 0.0).astype(BF16)]
    for j in range(lag):
        rows = []
        for t in range(8):
            if j <= t < lag:
                s = t - j
                gap = jnp.exp(jnp.minimum(cum[t : t + 1] - cum[s : s + 1], 0.0))
                rows.append(gap * scores[t : t + 1, s : s + 1] * dt[s : s + 1])
            else:
                rows.append(jnp.zeros((1, 128), F32))
        small.append(jnp.concatenate(rows, axis=0).astype(BF16))
    small = jnp.concatenate([m.astype(F32) for m in small], axis=0).astype(BF16)

    u_ref[:8, :] = jnp.zeros((8, width), F32)
    u_ref[8:, :] = inner_ref[...].astype(F32)
    lane = lax.broadcasted_iota(jnp.int32, (1, 128), 1)
    for q in range(width // 128):
        cols = slice(q * 128, q * 128 + 128)
        ik = ik_ref[:, cols].astype(F32)
        run = jnp.zeros((seq, 128), F32)
        for k in range(taps):
            run = run + ik[k : k + 1] * u_ref[lead + k : lead + k + seq, cols]
        x = jnp.where(early, 0.0, silu(run)).astype(BF16)
        xf = x.astype(F32)
        y_top = jnp.zeros((half, 128), F32)
        y_bottom = jnp.zeros((seq - half, 128), F32)
        for s in range(128 // p):
            h = q * (128 // p) + s
            own = (lane >= s * p) & (lane < (s + 1) * p)
            xs = jnp.where(own, xf, 0.0).astype(BF16)
            col = cum[:, h : h + 1]
            row = cum_t[h : h + 1]
            dr = dt_t[h : h + 1]
            w_top = jnp.exp(jnp.minimum(col[:half] - row[:, :half], 0.0)) * (top * dr[:, :half])
            w_bottom = jnp.exp(jnp.minimum(col[half:] - row, 0.0)) * (bottom * dr)
            y_top = y_top + jnp.dot(w_top.astype(BF16), xs[:half], preferred_element_type=F32)
            y_bottom = y_bottom + jnp.dot(w_bottom.astype(BF16), xs, preferred_element_type=F32)
        skip = skip_ref[:, cols]
        y = jnp.concatenate([y_top, y_bottom], axis=0) + skip * xf
        z = silu(gate_ref[:, cols].astype(F32))
        az_ref[:, cols] = (y * z).astype(BF16)
        ez = jnp.dot(grown, spread[:, cols], preferred_element_type=F32) * z
        ez_ref[:, cols] = ez.astype(BF16)
        tw = jnp.dot(tail.astype(BF16), spread[:, cols], preferred_element_type=F32)
        xt = (xf * tw).astype(BF16)
        f1_ref[0, cols, :] = lax.dot_general(
            xt, b, (((0,), (0,)), ((), ())), preferred_element_type=F32
        )
        wide = jnp.dot(small, spread[:, cols], preferred_element_type=F32)
        first_ref[0, 0:8, cols] = run[:8]
        first_ref[0, 16 + 8 * lag : 16 + 8 * lag + taps, cols] = ik
        first_ref[0, 8:16, cols] = wide[:8]
        z8 = z[:8]
        first_ref[0, 16:24, cols] = jnp.where(row8 < lag, (wide[8:16] + skip) * z8, 0.0)
        for j in range(1, lag):
            first_ref[0, 16 + 8 * j : 24 + 8 * j, cols] = wide[8 + 8 * j : 16 + 8 * j] * z8


def ssd(inner, gate, state, step, history, ik, sk, bias, decay, skip):
    tokens, width = inner.shape
    requests = history.shape[0]
    seq = tokens // requests
    heads = step.shape[1]
    n2 = state.shape[1]
    n = n2 // 2
    lag = ik.shape[0] - 1
    rows = lambda w: pl.BlockSpec((seq, w), lambda r: (r, 0))
    per = lambda *s: pl.BlockSpec((1,) + s, lambda r: (r,) + (0,) * len(s))
    return pl.pallas_call(
        ssd_kernel,
        out_shape=(
            pltpu.VMEM((tokens, width), BF16),
            pltpu.HBM((tokens, width), BF16),
            pltpu.VMEM((tokens, 2 * n), BF16),
            pltpu.HBM((requests, width, n), F32),
            pltpu.VMEM((requests, 2 * heads + 8, n), F32),
            pltpu.VMEM((requests, 24 + 8 * lag, width), F32),
        ),
        grid=(requests,),
        in_specs=[
            rows(width),
            rows(width),
            rows(n2),
            rows(heads),
            per(*history.shape[1:]),
            full(ik.shape),
            full(sk.shape),
            full(bias.shape),
            full(decay.shape),
            full(skip.shape),
        ],
        out_specs=(
            rows(width),
            rows(width),
            rows(2 * n),
            per(width, n),
            per(2 * heads + 8, n),
            per(24 + 8 * lag, width),
        ),
        scratch_shapes=[pltpu.VMEM((seq + 8, width), F32), pltpu.VMEM((seq + 8, n2), F32)],
        compiler_params=pltpu.CompilerParams(vmem_limit_bytes=40 * MIB),
        cost_estimate=pl.CostEstimate(
            flops=2 * tokens * width * seq * 2, bytes_accessed=14 * MIB, transcendentals=tokens * seq * heads
        ),
        name="ssd",
    )(*in_hbm(inner, gate, state, step), history, ik, sk, bias, decay, skip)


def first_sources(grow_ref, small_ref, r):
    requests = small_ref.shape[0]
    b = small_ref[r, small_ref.shape[1] - 8 :]
    zero = jnp.zeros_like(b)
    b = jnp.concatenate([b if i == r else zero for i in range(requests)], axis=0).astype(BF16)
    return jnp.dot(grow_ref[...], b, preferred_element_type=F32)


def tail_kernel(
    pos_hbm,
    back_ref,
    ez_hbm,
    f1_hbm,
    az_ref,
    c_ref,
    small_ref,
    first_ref,
    g_ref,
    sq_ref,
    grow_ref,
    held_ref,
    f1_ref,
    pos_ref,
    ez_ref,
    rows_ref,
    s_ref,
    raw_ref,
    win_ref,
    mix_ref,
    x_ref,
    extra_ref,
    sem,
    ez_sem,
    once_sem,
):
    requests = first_ref.shape[0]
    heads = (small_ref.shape[1] - 8) // 2
    p = held_ref.shape[1]
    tokens, width = g_ref.shape
    seq = tokens // requests
    lag = (first_ref.shape[1] - 24) // 8
    pairs = heads // 2

    def rows_of(r):
        return slice(r * seq, r * seq + seq)

    batch = requests // 2

    def ez_copy(i):
        rows = slice(i * batch * seq, (i + 1) * batch * seq)
        return pltpu.make_async_copy(ez_hbm.at[rows], ez_ref.at[rows], ez_sem.at[i])

    def fetch(i):
        for e in range(i * batch * heads, (i + 1) * batch * heads):
            at = pos_ref[e]
            pltpu.make_async_copy(
                back_ref.at[at // CAP, pl.ds(pl.multiple_of((at % CAP) * p, p), p)],
                held_ref.at[e],
                sem.at[i],
            ).start()

    row_copy = pltpu.make_async_copy(back_ref.at[:, CAP * p :], rows_ref, once_sem.at[0])
    f1_copy = pltpu.make_async_copy(f1_hbm, f1_ref, once_sem.at[1])
    pos_copy = pltpu.make_async_copy(pos_hbm, pos_ref, once_sem.at[2])
    pos_copy.start()
    row_copy.start()
    ez_copy(0).start()
    win_ref[...] = jnp.zeros_like(win_ref)
    x_ref[...] = jnp.zeros_like(x_ref)
    pos_copy.wait()
    fetch(0)
    ez_copy(1).start()
    fetch(1)
    f1_copy.start()
    row_copy.wait()

    low = lax.broadcasted_iota(jnp.int32, (1, 128), 1) < p
    flat = rows_ref.reshape(rows_ref.shape[0] * rows_ref.shape[1], 128)
    for i in range(requests):
        for q in range(pairs):
            cols = slice(q * 128, q * 128 + 128)
            even = 2 * pos_ref[i * heads + 2 * q]
            odd = 2 * pos_ref[i * heads + 2 * q + 1]
            a0, a1 = flat[pl.ds(even, 1)], flat[pl.ds(odd, 1)]
            b0, b1 = flat[pl.ds(even + 1, 1)], flat[pl.ds(odd + 1, 1)]
            win_ref[i, 0:1, cols] = jnp.where(low, a0, a1)
            win_ref[i, 2:3, cols] = jnp.where(low, b0, b1)
            mix_ref[i * pairs + q : i * pairs + q + 1] = jnp.where(low, a1, a0)
    mix = pltpu.roll(mix_ref[...], p, 1)
    for i in range(requests):
        for q in range(pairs):
            win_ref[i, 1:2, q * 128 : q * 128 + 128] = mix[i * pairs + q : i * pairs + q + 1]

    run = first_ref[:, 0:8]
    for k in range(lag):
        at = 16 + 8 * lag + k
        run = run + first_ref[:, at : at + 1] * win_ref[:, k : k + 8]
    row8 = lax.broadcasted_iota(jnp.int32, run.shape, 1)
    x = jnp.where(row8 < lag, silu(run), 0.0).astype(BF16).astype(F32)
    x_ref[:, 8:16] = x
    extra = first_ref[:, 16:24] * x
    for j in range(1, lag):
        extra = extra + first_ref[:, 16 + 8 * j : 24 + 8 * j] * x_ref[:, 8 - j : 16 - j]
    extra_ref[...] = extra
    grow = (x * first_ref[:, 8:16]).reshape(requests * 8, width).T
    grow_ref[...] = grow.astype(BF16)
    n = c_ref.shape[1] // 2
    grow = jnp.concatenate([grow, jnp.zeros((width, n - requests * 8), F32)], axis=1).astype(BF16)
    s_ref[0, :, n:] = grow
    s_ref[1, :, n:] = grow

    row16 = lax.broadcasted_iota(jnp.int32, (16, 256), 0)
    nt = (((1,), (1,)), ((), ()))
    squares = []
    for r in range(requests):
        rows = rows_of(r)
        if r % batch == 0:
            part = held_ref.at[r * heads : (r + batch) * heads]
            pltpu.make_async_copy(part, part, sem.at[r // batch]).wait()
            ez_copy(r // batch).wait()
        for h in range(heads):
            at = slice(h * p, h * p + p)
            block = held_ref[r * heads + h]
            raw_ref[r % 2, at] = block.astype(BF16)
            s_ref[r % 2, at, :n] = (small_ref[r, heads + h : heads + h + 1] * block).astype(BF16)
        c = c_ref[rows]
        total = jnp.zeros((seq - 16, 128), F32)
        total16 = jnp.zeros((16, 128), F32)
        for q in range(width // 256):
            cols = slice(q * 256, q * 256 + 256)
            seen = lax.dot_general(c, s_ref[r % 2, cols], nt, preferred_element_type=F32)
            seen16 = lax.dot_general(c[:16, :n], raw_ref[r % 2, cols], nt, preferred_element_type=F32)
            seen16 = jnp.where(row16 < lag, seen16, seen[:16])
            az = az_ref[rows, cols].astype(F32)
            ez = ez_ref[rows, cols].astype(F32)
            g = az[16:] + ez[16:] * seen[16:]
            g16 = az[:16] + ez[:16] * seen16
            g16 = g16 + jnp.concatenate([extra_ref[r, :, cols], jnp.zeros((8, 256), F32)], axis=0)
            g_ref[r * seq : r * seq + 16, cols] = g16.astype(BF16)
            g_ref[r * seq + 16 : r * seq + seq, cols] = g.astype(BF16)
            g = g * g
            g16 = g16 * g16
            total = total + g[:, :128] + g[:, 128:]
            total16 = total16 + g16[:, :128] + g16[:, 128:]
        total = jnp.concatenate([total16, total], axis=0)
        squares.append(jnp.sum(total.T, axis=0, keepdims=True))
    squares.append(jnp.zeros((8 - requests, seq), F32))
    sq_ref[...] = jnp.concatenate(squares, axis=0)
    f1_copy.wait()


def tail(pos, back, ez, f1, az, c, small, first):
    requests, packed, n = small.shape
    heads = (packed - 8) // 2
    assert requests * 8 <= n
    tokens, width = az.shape
    p = width // heads
    seq = tokens // requests
    owners = back.shape[0]
    vmem = pl.BlockSpec(memory_space=pltpu.VMEM)
    hbm = pl.BlockSpec(memory_space=pltpu.HBM)
    return pl.pallas_call(
        tail_kernel,
        out_shape=(
            pltpu.VMEM((tokens, width), BF16),
            pltpu.VMEM((8, seq), F32),
            pltpu.VMEM((width, requests * 8), BF16),
            pltpu.VMEM((requests * heads, p, n), F32),
            pltpu.VMEM(f1.shape, F32),
        ),
        in_specs=[hbm] * 4 + [vmem] * 4,
        out_specs=(vmem,) * 5,
        scratch_shapes=[
            pltpu.SMEM(pos.shape, jnp.int32),
            pltpu.VMEM((tokens, width), BF16),
            pltpu.VMEM((owners, 2 * CAP, n), F32),
            pltpu.VMEM((2, width, 2 * n), BF16),
            pltpu.VMEM((2, width, n), BF16),
            pltpu.VMEM((requests, 16, width), F32),
            pltpu.VMEM((requests * heads // 2, 128), F32),
            pltpu.VMEM((requests, 16, width), F32),
            pltpu.VMEM((requests, 8, width), F32),
            pltpu.SemaphoreType.DMA((2,)),
            pltpu.SemaphoreType.DMA((2,)),
            pltpu.SemaphoreType.DMA((3,)),
        ],
        compiler_params=pltpu.CompilerParams(vmem_limit_bytes=24 * MIB),
        cost_estimate=pl.CostEstimate(
            flops=2 * tokens * width * n, bytes_accessed=10 * MIB, transcendentals=0
        ),
        name="tail",
    )(*in_hbm(pos, back, ez, f1), *in_vmem(az, c, small, first))


def final_kernel(held_ref, grow_ref, small_ref, f1_ref, out_ref, made_ref, sem):
    requests, heads, p = out_ref.shape[:3]

    def copy(r):
        return pltpu.make_async_copy(made_ref.at[r], out_ref.at[r], sem.at[r])

    for r in range(requests):
        add = first_sources(grow_ref, small_ref, r)
        for h in range(heads):
            at = slice(h * p, h * p + p)
            block = small_ref[r, heads + h : heads + h + 1] * held_ref[r * heads + h] + add[at]
            made_ref[r, h] = small_ref[r, h : h + 1] * block + f1_ref[r, at]
        copy(r).start()
    for r in range(requests):
        copy(r).wait()


def finals(held, grow, small, f1):
    requests, width, n = f1.shape
    heads = (small.shape[1] - 8) // 2
    p = width // heads
    vmem = pl.BlockSpec(memory_space=pltpu.VMEM)
    return pl.pallas_call(
        final_kernel,
        out_shape=jax.ShapeDtypeStruct((requests, heads, p, n), F32),
        in_specs=[vmem] * 4,
        out_specs=pl.BlockSpec(memory_space=pltpu.HBM),
        scratch_shapes=[
            pltpu.VMEM((requests, heads, p, n), F32),
            pltpu.SemaphoreType.DMA((requests,)),
        ],
        compiler_params=pltpu.CompilerParams(vmem_limit_bytes=16 * MIB),
        cost_estimate=pl.CostEstimate(
            flops=2 * requests * width * n * 32, bytes_accessed=6 * MIB, transcendentals=0
        ),
        name="finals",
    )(*in_vmem(held, grow, small, f1))


def norm_kernel(channels, g_ref, s0_ref, s1_ref, s2_ref, s3_ref, gain_ref, out_ref, made_ref, sem):
    tokens, width = g_ref.shape
    seq = s0_ref.shape[1]
    step = 128
    gain = gain_ref[...].astype(F32)
    square = s0_ref[...] + s1_ref[...] + s2_ref[...] + s3_ref[...]
    scale = lax.rsqrt(square / channels + EPSILON)

    def copy(i):
        rows = slice(i * step, i * step + step)
        return pltpu.make_async_copy(made_ref.at[rows], out_ref.at[rows], sem.at[i])

    for i in range(tokens // step):
        rows = slice(i * step, i * step + step)
        r, at = i * step // seq, i * step % seq
        wide = jnp.broadcast_to(scale[r : r + 1, at : at + step], (128, step)).T
        for q in range(width // 128):
            cols = slice(q * 128, q * 128 + 128)
            made_ref[rows, cols] = (g_ref[rows, cols].astype(F32) * wide * gain[:, cols]).astype(BF16)
        copy(i).start()
    for i in range(tokens // step):
        copy(i).wait()


def normalise(g, parts, gain, channels):
    tokens, width = g.shape
    vmem = pl.BlockSpec(memory_space=pltpu.VMEM)
    return pl.pallas_call(
        functools.partial(norm_kernel, channels),
        out_shape=jax.ShapeDtypeStruct((tokens, width), BF16),
        in_specs=[vmem] * 6,
        out_specs=pl.BlockSpec(memory_space=pltpu.HBM),
        scratch_shapes=[pltpu.VMEM((tokens, width), BF16), pltpu.SemaphoreType.DMA((tokens // 128,))],
        compiler_params=pltpu.CompilerParams(vmem_limit_bytes=8 * MIB),
        cost_estimate=pl.CostEstimate(flops=2 * tokens * width, bytes_accessed=4 * MIB, transcendentals=0),
        name="normalise",
    )(g, *parts, gain)


def local(
    activations,
    gate_weight,
    inner_weight,
    state_proj,
    step_weight,
    inner_kernel,
    state_kernel,
    step_bias,
    decay_rate,
    skip_scale,
    norm_gain,
    scan_cache,
    window_cache,
    state_history,
    hit_owner,
    hit_slot,
):
    owners = lax.axis_size("dp")
    groups = lax.axis_size("mp")
    requests, heads = hit_owner.shape
    slots, _, p, n = scan_cache.shape
    width = inner_weight.shape[1]
    blocks = slots * heads

    cache = scan_cache.reshape(blocks, p, n)
    wanted, pos, cache, wa, wb = prep(hit_owner, hit_slot, cache, window_cache.reshape(blocks, -1), owners)
    codes = lax.all_to_all(wanted, "dp", split_axis=0, concat_axis=0, tiled=True)
    sent = pick(codes, cache, wa, wb)
    back = lax.all_to_all(sent, "dp", split_axis=0, concat_axis=0, tiled=True)

    inner, gate, state, step = project(activations, inner_weight, gate_weight, state_proj, step_weight)
    az, ez, c, f1, small, first = ssd(
        inner,
        gate,
        state,
        step,
        state_history,
        inner_kernel,
        state_kernel,
        step_bias[None],
        decay_rate[None],
        jnp.repeat(skip_scale, p)[None],
    )
    g, square, grow, held, f1 = tail(pos, back, ez, f1, az, c, small, first)
    final = finals(held, grow, small, f1)
    pair = [(i, i ^ 1) for i in range(groups)]
    square = square + lax.ppermute(square, "mp", pair)
    parts = [square] + [
        lax.ppermute(square, "mp", [(i, (i + 2 * s) % groups) for i in range(groups)])
        for s in range(1, groups // 2)
    ]
    normed = normalise(g, parts, norm_gain[None], width * groups)
    return normed, final


def solution(mesh):
    placed = (
        P("dp", None),
        P(None, "mp"),
        P(None, "mp"),
        P(),
        P(None, "mp"),
        P(None, "mp"),
        P(),
        P("mp"),
        P("mp"),
        P("mp"),
        P("mp"),
        P("dp", "mp", None, None),
        P("dp", "mp", None),
        P("dp", None, None),
        P("dp", "mp"),
        P("dp", "mp"),
    )
    return jax.shard_map(
        local,
        mesh=mesh,
        in_specs=placed,
        out_specs=(P("dp", "mp"), P("dp", "mp", None, None)),
        check_vma=False,
    )
```
